128 devices in a mesh: row: 16 (over z_hi, x, core), col: 8 (over y, z_lo).
Axes of the slice: x: 4, y: 4, z: 4 (z_hi: 2, z_lo: 2; z = z_hi * 2 + z_lo), core: 2. Of those that a mesh axis runs over, the one named last changes fastest.
Arguments:
- tokens: bfloat16 [2, 4096, 2048], P(None, 'row', 'col'), may hold values from -6 to 6
- out_grad: bfloat16 [2, 4096, 2048], P(None, 'row', 'col'), may hold values from -6 to 6
- parents: int32 [2, 13], replicated, may hold values from 0 to 11, as said below
- routes: int32 [2, 4096, 6], P(None, 'row'), may hold values from 0 to 7, all different within a row; in each aligned block of 256 rows (0 to 255, 256 to 511, ..., all dimensions but the last counted through in order) at most 256 rows name the same one
- gates: float32 [2, 4096, 6], P(None, 'row'), may hold values from 0.2 to 1
- norm_in: bfloat16 [2048], replicated, may hold values from 0.5 to 1.5
- w_query: bfloat16 [2048, 3072], P('row', 'col'), may hold values from -0.125 to 0.125
- w_latent: bfloat16 [2048, 576], P('row', 'col'), may hold values from -0.125 to 0.125
- norm_latent: bfloat16 [512], replicated, may hold values from 0.5 to 1.5
- w_expand: bfloat16 [512, 4096], P('row', 'col'), may hold values from -0.25 to 0.25
- w_output: bfloat16 [2048, 2048], P('col', 'row'), may hold values from -4 to 4
- norm_mid: bfloat16 [2048], replicated, may hold values from 0.5 to 1.5
- w_shared_gate: bfloat16 [2048, 2816], P('row', 'col'), may hold values from -0.125 to 0.125
- w_shared_up: bfloat16 [2048, 2816], P('row', 'col'), may hold values from -0.125 to 0.125
- w_shared_down: bfloat16 [2816, 2048], P('col', 'row'), may hold values from -0.109375 to 0.109375
- w_expert_gate: bfloat16 [8, 2048, 1408], P(None, 'row', 'col'), may hold values from -0.125 to 0.125
- w_expert_up: bfloat16 [8, 2048, 1408], P(None, 'row', 'col'), may hold values from -0.125 to 0.125
- w_expert_down: bfloat16 [8, 1408, 2048], P(None, 'col', 'row'), may hold values from -0.15625 to 0.15625
Outputs:
- layer_out: bfloat16 [2, 4096, 2048], P(None, 'row', 'col')
- input_grad: bfloat16 [2, 4096, 2048], P(None, 'row', 'col')
- grad_norm_in: float32 [2048], replicated
- grad_query: float32 [2048, 3072], P('row', 'col')
- grad_latent: float32 [2048, 576], P('row', 'col')
- grad_norm_latent: float32 [512], replicated
- grad_expand: float32 [512, 4096], P('row', 'col')
- grad_output: float32 [2048, 2048], P('col', 'row')
- grad_norm_mid: float32 [2048], replicated
- grad_shared_gate: float32 [2048, 2816], P('row', 'col')
- grad_shared_up: float32 [2048, 2816], P('row', 'col')
- grad_shared_down: float32 [2816, 2048], P('col', 'row')
- grad_expert_gate: float32 [8, 2048, 1408], P(None, 'row', 'col')
- grad_expert_up: float32 [8, 2048, 1408], P(None, 'row', 'col')
- grad_expert_down: float32 [8, 1408, 2048], P(None, 'col', 'row')
The draws below stay inside these ranges and needn't reach their ends.
Inputs may be any that keep to these rules, and one draw needn't show every extreme that they name: parents[m, 0] is 0 for the trunk, segment 0, which holds tokens 0 to 1023; segment s >= 1 holds the 256 tokens from 1024 + (s - 1) * 256 on, and parents[m, s] is a segment below s; the last segment's parent is segment 13 - 2. `routes`: each row names 6 different experts; of the 256 tokens of a tree held by one index of row (aligned blocks of 256 rows), no expert is named by more than 256.
All inputs are finite; a program needn't handle non-finite values.
Results may differ from the reference program's by a relative error of at most 0.028.
Values may be sent and summed in bfloat16 or wider, within the bound.
No kernel may reach another device: no remote copies, remote signals or barrier semaphores. Data moves between devices by JAX's collectives and lax.ppermute only.
A program may use at most 320 MiB of HBM per device.

```python
import math
from functools import partial
import jax
import jax.numpy as jnp
import numpy as np
from jax import lax

D = 2048
H = 16
NOPE = 128
ROPE = 64
VDIM = 128
KVL = 512
FF = 1408
SFF = 2816
TOPK = 6
EXPERTS = 8
MICRO = 2
TRUNK = 1024
BRANCH = 256
SEGS = 13
TREE = 4096
TD = 256
CAP = 256
N_ROW = 16


def draw_parents(key, part):
    seg_range = jnp.arange(SEGS, dtype=jnp.int32)
    upper_bound = jnp.maximum(seg_range, 1)
    picked = jax.random.randint(key, (MICRO, SEGS), 0, upper_bound[None, :], dtype=jnp.int32)
    picked = jnp.where(seg_range[None, :] == SEGS - 1, SEGS - 2, picked)
    return jnp.where(seg_range[None, :] == 0, 0, picked).astype(jnp.int32)


def level_of(key, dims, shards, smallest, largest):
    level = 1.0
    for axis_at, parts in shards:
        steps = jax.random.uniform(jax.random.fold_in(jax.random.fold_in(key, 6), axis_at), (parts,), jnp.float32, smallest / len(shards), largest / len(shards))
        level = level * jnp.repeat(jnp.exp(steps), dims[axis_at] // parts).reshape((-1,) + (1,) * (len(dims) - 1 - axis_at))
    return level


def deal_out(stream_key, own, number, rows, amount, top, bound, skew):
    sequence = jax.random.permutation(stream_key, amount)
    heavy_load, common = portions_of(amount, rows * top, bound, skew, True), portions_of(amount, rows * top, bound, skew, False)
    places = jnp.arange(amount)

    def named(lengths, rotation):
        used = int((lengths > 0).sum())
        fixed = max(1, used // 4)
        moved = fixed + (places - fixed + rotation * (used - fixed)) % max(1, amount - fixed)
        return jnp.zeros((amount,), jnp.int32).at[sequence[jnp.where(places < fixed, places, moved)]].set(jnp.asarray(lengths, jnp.int32))

    lengths = jnp.where(number % 4 == 0, named(heavy_load, number // 4), named(common, number - number // 4 - 1))
    mixed = jax.random.permutation(jax.random.fold_in(own, 3), amount)
    source_of, taker = mixed[0:amount // 2 * 2:2], mixed[1:amount // 2 * 2:2]
    margin = jnp.minimum(lengths[source_of] - 1, bound - lengths[taker]) // 2
    margin = jnp.where((source_of == sequence[0]) | (taker == sequence[0]) | (lengths[taker] == 0), 0, jnp.maximum(margin, 0))
    moved = jax.random.randint(jax.random.fold_in(own, 4), (amount // 2,), 0, 1 << 20) % (margin + 1)
    lengths = lengths.at[source_of].add(-moved).at[taker].add(moved)
    members = jnp.searchsorted(jnp.cumsum(lengths), jnp.arange(rows * top), side="right").astype(jnp.int32)
    table = members.reshape(top, rows).T
    table = table[jax.random.permutation(jax.random.fold_in(own, 1), rows)]
    rotation = jax.random.randint(jax.random.fold_in(own, 2), (rows, 1), 0, top)
    return jnp.take_along_axis(table, (jnp.arange(top)[None, :] + rotation) % top, axis=1)


def portions_of(amount, total, limit, skew, full):
    portions = [(1 << 20) // math.isqrt(grade ** skew) + 1 for grade in range(1, amount + 1)]
    largest = limit if full else min(limit, max(-(-total // amount), total * portions[0] // sum(portions)))
    least = 1 if total - largest >= amount - 1 else 0
    holding, surplus = [largest] + [least] * (amount - 1), total - largest - least * (amount - 1)
    while surplus > 0:
        free = [i for i in range(1, amount) if holding[i] < largest] or [i for i in range(1, amount) if holding[i] < limit]
        pool, remaining = sum([portions[i] for i in free]), surplus
        for i in free:
            more = min(limit - holding[i], max(1, remaining * portions[i] // pool), surplus)
            holding[i] = holding[i] + more
            surplus = surplus - more
    return np.array(holding)


def gaussian(stream_key, extent, scale, reach, shards=(), kind=jnp.bfloat16):
    loudness = level_of(stream_key, extent, shards, -0.22, 0.18) if shards else 1.0
    values = jax.random.normal(stream_key, extent, jnp.float32) * scale * loudness
    return jnp.minimum(jnp.maximum(values, -reach), reach).astype(kind)


def setup_inputs(seed: int = 0) -> dict:
    splits = jax.random.split(jax.random.key(seed), 19)
    tokens = gaussian(splits[0], (MICRO, TREE, D), 1.0, 6.0, ((1, 16), (2, 8)))
    out_grad = gaussian(splits[1], (MICRO, TREE, D), 1.0, 6.0, ((1, 16), (2, 8)))
    parents = draw_parents(jax.random.fold_in(splits[18], 71), 0)
    routes_keys = jax.random.split(jax.random.fold_in(splits[3], 1), MICRO * TREE // TD)
    routes_turns = jax.random.permutation(jax.random.fold_in(splits[3], 3), MICRO * TREE // TD)
    routes = jax.vmap(lambda own, number: deal_out(jax.random.fold_in(splits[3], 2), own, number, TD, EXPERTS, TOPK, CAP, 0))(routes_keys, routes_turns).reshape((MICRO, TREE, TOPK))
    gates = jnp.clip(0.2 + 0.8 * jax.random.uniform(splits[4], (MICRO, TREE, TOPK), jnp.float32) ** level_of(splits[4], (MICRO, TREE, TOPK), ((1, 16),), -0.2, 0.2), 0.2, 1.0)
    norm_in = jnp.clip(1.0 + 0.1 * jax.random.normal(splits[5], (D,), jnp.float32), 0.5, 1.5).astype(jnp.bfloat16)
    w_query = gaussian(splits[6], (D, H * (NOPE + ROPE)), D ** -0.5, 0.125, ((0, 16), (1, 8)))
    w_latent = gaussian(splits[7], (D, KVL + ROPE), D ** -0.5, 0.125, ((0, 16), (1, 8)))
    norm_latent = jnp.clip(1.0 + 0.1 * jax.random.normal(splits[8], (KVL,), jnp.float32), 0.5, 1.5).astype(jnp.bfloat16)
    w_expand = gaussian(splits[9], (KVL, H * (NOPE + VDIM)), KVL ** -0.5, 0.25, ((0, 16), (1, 8)))
    w_output = gaussian(splits[10], (H * VDIM, D), (max(1, H * VDIM // 1024)) ** -0.5, 4.0, ((0, 8), (1, 16)))
    norm_mid = jnp.clip(1.0 + 0.1 * jax.random.normal(splits[11], (D,), jnp.float32), 0.5, 1.5).astype(jnp.bfloat16)
    w_shared_gate = gaussian(splits[12], (D, SFF), D ** -0.5, 0.125, ((0, 16), (1, 8)))
    w_shared_up = gaussian(splits[13], (D, SFF), D ** -0.5, 0.125, ((0, 16), (1, 8)))
    w_shared_down = gaussian(splits[14], (SFF, D), SFF ** -0.5, 0.109375, ((0, 8), (1, 16)))
    w_expert_gate = gaussian(splits[15], (EXPERTS, D, FF), D ** -0.5, 0.125, ((1, 16), (2, 8)))
    w_expert_up = gaussian(splits[16], (EXPERTS, D, FF), D ** -0.5, 0.125, ((1, 16), (2, 8)))
    w_expert_down = gaussian(splits[17], (EXPERTS, FF, D), FF ** -0.5, 0.15625, ((1, 8), (2, 16)))
    return {"tokens": tokens, "out_grad": out_grad, "parents": parents, "routes": routes, "gates": gates, "norm_in": norm_in, "w_query": w_query, "w_latent": w_latent, "norm_latent": norm_latent, "w_expand": w_expand, "w_output": w_output, "norm_mid": norm_mid, "w_shared_gate": w_shared_gate, "w_shared_up": w_shared_up, "w_shared_down": w_shared_down, "w_expert_gate": w_expert_gate, "w_expert_up": w_expert_up, "w_expert_down": w_expert_down}


EPS = 1e-06
THETA = 10000.0
HIGHEST = lax.Precision.HIGHEST
NEG_LARGE = -1e+30

@jax.custom_vjp
def low(v):
    return lax.optimization_barrier(v.astype(jnp.bfloat16)).astype(jnp.float32)

@jax.custom_vjp
def low_back(v):
    return v

def low_keep(v):
    return (low(v), None)

def low_pass(kept, grad):
    return (grad,)

def back_keep(v):
    return (v, None)

def back_low(kept, grad):
    return (low(grad),)
low.defvjp(low_keep, low_pass)
low_back.defvjp(back_keep, back_low)

def inverse_rms(values):
    return lax.rsqrt(lax.optimization_barrier(jnp.mean(values * values, axis=-1, keepdims=True)) + EPS)

def rope_tables(positions, width):
    half_width = width // 2
    frequency = THETA ** (-jnp.arange(half_width, dtype=jnp.float32) / half_width)
    angles = positions.astype(jnp.float32)[:, None] * frequency[None, :]
    return (jnp.cos(angles), jnp.sin(angles))

def rotate(values, cos_table, sin_table):
    half_width = values.shape[-1] // 2
    first_half = values[..., :half_width]
    second_half = values[..., half_width:]
    return jnp.concatenate([first_half * cos_table - second_half * sin_table, first_half * sin_table + second_half * cos_table], axis=-1)

def tree_layout(parent_ids, trunk_len, branch_len, total_len):
    seg_count = parent_ids.shape[0]
    tokens_at = jnp.arange(total_len, dtype=jnp.int32)
    in_trunk = tokens_at < trunk_len
    segment_of = jnp.where(in_trunk, 0, 1 + (tokens_at - trunk_len) // branch_len).astype(jnp.int32)
    offset_in = jnp.where(in_trunk, tokens_at, (tokens_at - trunk_len) % branch_len).astype(jnp.int32)
    identity = jnp.eye(seg_count, dtype=jnp.float32)
    seg_range = jnp.arange(seg_count, dtype=jnp.int32)
    parent_onehot = (parent_ids[:, None] == seg_range[None, :]).astype(jnp.float32)
    ancestry = identity
    for repeat in range(seg_count - 1):
        ancestry = jnp.maximum(identity, jnp.dot(parent_onehot, ancestry, precision=HIGHEST))
    seg_lengths = jnp.where(seg_range == 0, trunk_len, branch_len).astype(jnp.float32)
    starts = jnp.dot(ancestry - identity, seg_lengths, precision=HIGHEST)
    member = (segment_of[:, None] == seg_range[None, :]).astype(jnp.float32)
    positions = jnp.dot(member, starts, precision=HIGHEST) + offset_in.astype(jnp.float32)
    return (member, positions, ancestry)

def visibility(member, ancestry, query_start, query_count):
    total_len = member.shape[0]
    query_member = lax.dynamic_slice_in_dim(member, query_start, query_count, 0)
    reach_seg = jnp.dot(query_member, ancestry, precision=HIGHEST)
    reachable = jnp.einsum('qs,ks->qk', reach_seg, member, precision=HIGHEST)
    same_seg = jnp.einsum('qs,ks->qk', query_member, member, precision=HIGHEST)
    query_ids = query_start + jnp.arange(query_count, dtype=jnp.int32)
    key_ids = jnp.arange(total_len, dtype=jnp.int32)
    causal = key_ids[None, :] <= query_ids[:, None]
    return (reachable > 0.5) & ((same_seg < 0.5) | causal)

def dispatch_tables(route_ids, gate_values, expert_count, capacity):
    token_count, top_count = route_ids.shape
    flat_routes = route_ids.reshape(-1).astype(jnp.int32)
    onehot = (flat_routes[:, None] == jnp.arange(expert_count, dtype=jnp.int32)[None, :]).astype(jnp.int32)
    before = jnp.cumsum(onehot, axis=0) - onehot
    slot_of = lax.optimization_barrier(jnp.sum(before * onehot, axis=1)).astype(jnp.int32)
    owner_row = (jnp.arange(token_count * top_count, dtype=jnp.int32) // top_count).astype(jnp.int32)
    slot_token = jnp.full((expert_count, capacity), token_count, jnp.int32).at[flat_routes, slot_of].set(owner_row)
    slot_gate = jnp.zeros((expert_count, capacity), jnp.float32).at[flat_routes, slot_of].set(gate_values.reshape(-1).astype(jnp.float32))
    return (slot_token, slot_gate)

def layer_forward(params, tokens_in, tree_parents, tree_routes, tree_gates):
    norm_in, w_query, w_latent, norm_latent, w_expand, w_output, norm_mid, w_shared_gate, w_shared_up, w_shared_down, w_expert_gate, w_expert_up, w_expert_down = params
    total_len = tokens_in.shape[0]
    member, positions, ancestry = tree_layout(tree_parents, TRUNK, BRANCH, total_len)
    slot_token, slot_gate = jax.vmap(partial(dispatch_tables, expert_count=EXPERTS, capacity=CAP))(tree_routes.reshape(N_ROW, total_len // N_ROW, TOPK), tree_gates.reshape(N_ROW, total_len // N_ROW, TOPK))
    normed_in = low(tokens_in * inverse_rms(tokens_in) * norm_in)
    query_all = low_back(jnp.dot(normed_in, w_query, precision=HIGHEST, preferred_element_type=jnp.float32)).reshape(total_len, H, NOPE + ROPE)
    cos_table, sin_table = rope_tables(positions, ROPE)
    query_rot = low(jnp.concatenate([query_all[..., :NOPE], rotate(query_all[..., NOPE:], cos_table[:, None, :], sin_table[:, None, :])], axis=-1))
    latent = low(low_back(jnp.dot(normed_in, w_latent, precision=HIGHEST, preferred_element_type=jnp.float32)))
    compressed = latent[:, :KVL]
    latent_normed = low(compressed * inverse_rms(compressed) * norm_latent)
    expanded = low(low_back(jnp.dot(latent_normed, w_expand, precision=HIGHEST, preferred_element_type=jnp.float32))).reshape(total_len, H, NOPE + VDIM)
    rope_keys = low(rotate(latent[:, KVL:], cos_table, sin_table))
    keys_full = jnp.concatenate([expanded[..., :NOPE], jnp.broadcast_to(rope_keys[:, None, :], (total_len, H, ROPE))], axis=-1)
    values_full = expanded[..., NOPE:]
    block_rows = total_len // 8
    score_scale = (NOPE + ROPE) ** (-0.5)

    def attend_block(block_start):
        query_block = lax.dynamic_slice_in_dim(query_rot, block_start, block_rows, 0)
        visible = visibility(member, ancestry, block_start, block_rows)
        raw = low_back(jnp.einsum('qhd,khd->hqk', query_block, keys_full, precision=HIGHEST))
        scores = jnp.where(visible[None], raw * score_scale, NEG_LARGE)
        probs = low(jnp.exp(scores - jax.nn.logsumexp(scores, axis=-1, keepdims=True)))
        return jnp.einsum('hqk,khd->qhd', probs, values_full, precision=HIGHEST)
    block_starts = jnp.arange(8, dtype=jnp.int32) * block_rows
    attended = lax.map(jax.checkpoint(attend_block), block_starts).reshape(total_len, H * VDIM)
    attended = low(low_back(attended))
    attn_out = low_back(jnp.dot(attended, w_output, precision=HIGHEST, preferred_element_type=jnp.float32))
    residual = tokens_in + attn_out
    normed_mid = low(residual * inverse_rms(residual) * norm_mid)
    shared_gate_pre = low_back(jnp.dot(normed_mid, w_shared_gate, precision=HIGHEST, preferred_element_type=jnp.float32))
    shared_up_pre = low_back(jnp.dot(normed_mid, w_shared_up, precision=HIGHEST, preferred_element_type=jnp.float32))
    shared_act = low(low_back(jax.nn.silu(shared_gate_pre) * shared_up_pre))
    shared_out = jnp.dot(shared_act, w_shared_down, precision=HIGHEST, preferred_element_type=jnp.float32)
    block_len = total_len // N_ROW
    mid_blocks = normed_mid.reshape(N_ROW, block_len, D)

    def expert_block(inputs):
        block_in, table, gate_table = inputs
        padded = jnp.concatenate([block_in, jnp.zeros((1, D), jnp.float32)], axis=0)
        buffers = padded[table]
        gate_pre = low_back(jnp.einsum('ecd,edf->ecf', buffers, w_expert_gate, precision=HIGHEST))
        up_pre = low_back(jnp.einsum('ecd,edf->ecf', buffers, w_expert_up, precision=HIGHEST))
        expert_act = low(low_back(jax.nn.silu(gate_pre) * up_pre))
        expert_out = low_back(jnp.einsum('ecf,efd->ecd', expert_act, w_expert_down, precision=HIGHEST))
        combined = jnp.zeros((block_len + 1, D), jnp.float32).at[table].add(expert_out * gate_table[..., None])
        return combined[:block_len]
    routed = lax.map(jax.checkpoint(expert_block), (mid_blocks, slot_token, slot_gate)).reshape(total_len, D)
    return residual + (routed + shared_out)

def reference(tokens, out_grad, parents, routes, gates, norm_in, w_query, w_latent, norm_latent, w_expand, w_output, norm_mid, w_shared_gate, w_shared_up, w_shared_down, w_expert_gate, w_expert_up, w_expert_down):
    params = tuple((weight.astype(jnp.float32) for weight in (norm_in, w_query, w_latent, norm_latent, w_expand, w_output, norm_mid, w_shared_gate, w_shared_up, w_shared_down, w_expert_gate, w_expert_up, w_expert_down)))

    def one_tree(grad_sums, inputs):
        tree_tokens, tree_cot, tree_parents, tree_routes, tree_gates = inputs

        def forward(tokens_in, weights):
            return layer_forward(weights, tokens_in, tree_parents, tree_routes, tree_gates)
        result, pullback = jax.vjp(forward, tree_tokens.astype(jnp.float32), params)
        grad_tokens, grad_params = pullback(tree_cot.astype(jnp.float32))
        new_sums = jax.tree.map(jnp.add, grad_sums, grad_params)
        return (new_sums, (result.astype(jnp.bfloat16), grad_tokens.astype(jnp.bfloat16)))
    zero_sums = tuple((jnp.zeros_like(weight) for weight in params))
    grads, (outputs, input_grads) = lax.scan(one_tree, zero_sums, (tokens, out_grad, parents, routes, gates))
    return (outputs, input_grads, grads[0], grads[1], grads[2], grads[3], grads[4], grads[5], grads[6], grads[7], grads[8], grads[9], grads[10], grads[11], grads[12])
```

```python
import jax
import jax.numpy as jnp
from jax import lax
from jax.experimental import pallas as pl
from jax.experimental.pallas import tpu as pltpu
from jax.sharding import PartitionSpec as P

D = 2048
NOPE = 128
ROPE = 64
QK = NOPE + ROPE
VDIM = 128
KVL = 512
TOPK = 6
EXPERTS = 8
MICRO = 2
TRUNK = 1024
BLK = 256
SEGS = 13
ROWS = 16
COLS = 8
TOK = MICRO * BLK
OWN = TOK // COLS
FEAT = D // COLS
QUART = 4
SHARED = 352
ROUTED = 176
HID = 1792
LAT = KVL + ROPE
LATC = LAT // COLS
SCALE = QK**-0.5
EPS = 1e-06
THETA = 10000.0
NEG = -1e30
MIB = 1024 * 1024
F32 = jnp.float32
BF16 = jnp.bfloat16
NT = (((1,), (1,)), ((), ()))
TN = (((0,), (0,)), ((), ()))


def inverse_rms(values):
    return lax.rsqrt(jnp.mean(values * values, axis=-1, keepdims=True) + EPS)


def norm_backward(grad_out, values, inv_scale, norm_gain):
    weighted = grad_out * norm_gain
    inner = jnp.mean(weighted * values, axis=-1, keepdims=True)
    return inv_scale * weighted - values * (inv_scale * inv_scale * inv_scale) * inner


def rotate(values, cos_table, sin_table):
    half = values.shape[-1] // 2
    a, b = values[..., :half], values[..., half:]
    return jnp.concatenate(
        [a * cos_table - b * sin_table, a * sin_table + b * cos_table], axis=-1
    )


def matmul(a, b):
    return jnp.dot(a, b, preferred_element_type=F32)


def matmul_nt(a, b):
    return lax.dot_general(a, b, NT, preferred_element_type=F32)


def matmul_tn(a, b):
    return lax.dot_general(a, b, TN, preferred_element_type=F32)


def swap(values, axis, groups=None):
    return lax.all_to_all(values, axis, 0, 0, tiled=True, axis_index_groups=groups)


def share(values, axis, count):
    return swap(jnp.broadcast_to(values[None], (count,) + values.shape), axis)


def depth_kernel(parents_ref, seg_ref, out_ref):
    seg = seg_ref[0]
    for m in range(MICRO):

        def climb(step, state):
            at, count = state
            return parents_ref[m, at], count + (at > 0).astype(jnp.int32)

        _, count = lax.fori_loop(0, SEGS, climb, (parents_ref[m, seg], jnp.int32(0)))
        out_ref[m] = count


def ancestor_depths(parents, seg):
    smem = pl.BlockSpec(memory_space=pltpu.SMEM)
    return pl.pallas_call(
        depth_kernel,
        out_shape=jax.ShapeDtypeStruct((MICRO,), jnp.int32),
        in_specs=[smem, smem],
        out_specs=smem,
    )(parents, seg)


def list_ancestors(meta, qb, listed):
    def climb(step, state):
        at, count = state
        listed[count] = at + 3
        return meta[at], count + (at > 0).astype(jnp.int32)

    _, count = lax.fori_loop(0, SEGS, climb, (meta[qb - 3], jnp.int32(0)))
    return count


def causal_mask():
    key = lax.broadcasted_iota(jnp.int32, (BLK, BLK), 0)
    query = lax.broadcasted_iota(jnp.int32, (BLK, BLK), 1)
    return key <= query


def attend_kernel(meta, q_ref, k_ref, vt_ref, o_ref, lse_ref, listed):
    quarter = meta[SEGS]
    for i in range(QUART):
        qb = QUART * i + quarter
        q = q_ref[i]
        s = matmul_nt(k_ref[qb], q) * SCALE
        s = jnp.where(causal_mask(), s, NEG)
        top = jnp.max(s, axis=0, keepdims=True)
        p = jnp.exp(s - top)
        total = jnp.sum(p, axis=0, keepdims=True)
        out = matmul(vt_ref[qb], p.astype(BF16))

        def step(kb, state):
            top, total, out = state
            s = matmul_nt(k_ref[kb], q) * SCALE
            new_top = jnp.maximum(top, jnp.max(s, axis=0, keepdims=True))
            shrink = jnp.exp(top - new_top)
            p = jnp.exp(s - new_top)
            total = total * shrink + jnp.sum(p, axis=0, keepdims=True)
            out = out * shrink + matmul(vt_ref[kb], p.astype(BF16))
            return new_top, total, out

        state = (top, total, out)
        if i == 0:
            state = lax.fori_loop(0, quarter, step, state)
        else:
            for kb in range(TRUNK // BLK):
                state = step(kb, state)
            count = list_ancestors(meta, qb, listed)
            state = lax.fori_loop(0, count, lambda t, c: step(listed[t], c), state)
        top, total, out = state
        o_ref[i] = (out * (1.0 / total)).T.astype(BF16)
        lse_ref[i] = top + jnp.log(total)


def attend(meta, q, k, vt):
    smem = pl.BlockSpec(memory_space=pltpu.SMEM)
    vmem = pl.BlockSpec(memory_space=pltpu.VMEM)
    pairs = 32 * BLK * BLK
    return pl.pallas_call(
        attend_kernel,
        out_shape=(
            jax.ShapeDtypeStruct((QUART, BLK, VDIM), BF16),
            jax.ShapeDtypeStruct((QUART, 1, BLK), F32),
        ),
        in_specs=[smem, vmem, vmem, vmem],
        out_specs=(vmem, vmem),
        scratch_shapes=[pltpu.SMEM((16,), jnp.int32)],
        compiler_params=pltpu.CompilerParams(vmem_limit_bytes=32 * MIB),
        cost_estimate=pl.CostEstimate(
            flops=pairs * 2 * (QK + VDIM), bytes_accessed=4 * MIB, transcendentals=pairs
        ),
    )(meta, q, k, vt)


def attend_back_kernel(
    meta, q_ref, k_ref, kt_ref, v_ref, o_ref, lse_ref, do_ref, dq_ref, dkv_ref, dk, dv, listed
):
    quarter = meta[SEGS]
    dk[...] = jnp.zeros_like(dk)
    dv[...] = jnp.zeros_like(dv)
    for i in range(QUART):
        qb = QUART * i + quarter
        q = q_ref[i]
        do = do_ref[i]
        lse = lse_ref[i]
        pairs = do.astype(F32) * o_ref[i].astype(F32)
        delta = jnp.sum(pairs.T, axis=0, keepdims=True)

        def step(kb, dqt, masked=False):
            s = matmul_nt(k_ref[kb], q) * SCALE
            p = jnp.exp(s - lse)
            if masked:
                p = jnp.where(causal_mask(), p, 0.0)
            dp = matmul_nt(v_ref[kb], do)
            ds = (p * (dp - delta) * SCALE).astype(BF16)
            dv[kb] += matmul(p.astype(BF16), do)
            dk[kb] += matmul(ds, q)
            return dqt + matmul(kt_ref[kb], ds)

        dqt = step(qb, jnp.zeros((QK, BLK), F32), True)
        if i == 0:
            dqt = lax.fori_loop(0, quarter, step, dqt)
        else:
            for kb in range(TRUNK // BLK):
                dqt = step(kb, dqt)
            count = list_ancestors(meta, qb, listed)
            dqt = lax.fori_loop(0, count, lambda t, c: step(listed[t], c), dqt)
        dq_ref[i] = dqt.T.astype(BF16)
    dkv_ref[:, :, :NOPE] = dk[:, :, :NOPE].astype(BF16)
    dkv_ref[:, :, NOPE : NOPE + VDIM] = dv[...].astype(BF16)
    dkv_ref[:, :, NOPE + VDIM :] = dk[:, :, NOPE:].astype(BF16)


def attend_back(meta, q, k, kt, v, o, lse, do):
    smem = pl.BlockSpec(memory_space=pltpu.SMEM)
    vmem = pl.BlockSpec(memory_space=pltpu.VMEM)
    pairs = 32 * BLK * BLK
    return pl.pallas_call(
        attend_back_kernel,
        out_shape=(
            jax.ShapeDtypeStruct((QUART, BLK, QK), BF16),
            jax.ShapeDtypeStruct((ROWS, BLK, QK + VDIM), BF16),
        ),
        in_specs=[smem] + [vmem] * 7,
        out_specs=(vmem, vmem),
        scratch_shapes=[
            pltpu.VMEM((ROWS, BLK, QK), F32),
            pltpu.VMEM((ROWS, BLK, VDIM), F32),
            pltpu.SMEM((16,), jnp.int32),
        ],
        compiler_params=pltpu.CompilerParams(vmem_limit_bytes=40 * MIB),
        cost_estimate=pl.CostEstimate(
            flops=pairs * 2 * (3 * QK + 2 * VDIM), bytes_accessed=10 * MIB, transcendentals=pairs
        ),
    )(meta, q, k, kt, v, o, lse, do)


def hidden_kernel(mid_ref, grad_ref, gate_ref, spread_ref, wg_ref, wu_ref, wd_ref, out_ref):
    mid = mid_ref[...]
    pre = matmul(mid, wg_ref[...])
    up = matmul(mid, wu_ref[...])
    back = matmul(grad_ref[...], wd_ref[...])
    gate = matmul(gate_ref[...], spread_ref[...])
    sig = 1.0 / (1.0 + jnp.exp(-pre))
    act = pre * sig
    back = back * gate
    out_ref[0] = (back * up * (sig * (1.0 + pre * (1.0 - sig)))).astype(BF16)
    out_ref[1] = (back * act).astype(BF16)
    out_ref[2] = (act * up * gate).astype(BF16)


def hidden(mid, grad, gates, spread, weights):
    whole = pl.BlockSpec((TOK, D), lambda j: (0, 0))
    parts = HID // BLK

    def weight(at):
        return pl.BlockSpec((D, BLK), lambda j: (0, at * parts + j))

    return pl.pallas_call(
        hidden_kernel,
        grid=(parts,),
        out_shape=jax.ShapeDtypeStruct((3, TOK, HID), BF16),
        in_specs=[
            whole,
            whole,
            pl.BlockSpec(gates.shape, lambda j: (0, 0)),
            pl.BlockSpec((spread.shape[0], BLK), lambda j: (0, j)),
            weight(0),
            weight(1),
            weight(2),
        ],
        out_specs=pl.BlockSpec((3, TOK, BLK), lambda j: (0, 0, j)),
        compiler_params=pltpu.CompilerParams(vmem_limit_bytes=48 * MIB),
        cost_estimate=pl.CostEstimate(
            flops=2 * TOK * D * HID * 3, bytes_accessed=32 * MIB, transcendentals=TOK * HID
        ),
    )(mid, grad, gates, spread, weights, weights, weights)


def model_kernel(hid_ref, w_ref, out_ref, back_ref):
    back = matmul_nt(hid_ref[0], w_ref[:, :HID]) + matmul_nt(hid_ref[1], w_ref[:, HID : 2 * HID])
    back_ref[...] = back.astype(BF16)
    out_ref[0] = matmul_nt(hid_ref[2], w_ref[:, 2 * HID :]).astype(BF16)


def model(hid, weights):
    return pl.pallas_call(
        model_kernel,
        grid=(COLS,),
        out_shape=(
            jax.ShapeDtypeStruct((COLS, TOK, FEAT), BF16),
            jax.ShapeDtypeStruct((TOK, D), BF16),
        ),
        in_specs=[
            pl.BlockSpec((3, TOK, HID), lambda j: (0, 0, 0)),
            pl.BlockSpec((FEAT, 3 * HID), lambda j: (j, 0)),
        ],
        out_specs=(
            pl.BlockSpec((1, TOK, FEAT), lambda j: (j, 0, 0)),
            pl.BlockSpec((TOK, FEAT), lambda j: (0, j)),
        ),
        compiler_params=pltpu.CompilerParams(vmem_limit_bytes=48 * MIB),
        cost_estimate=pl.CostEstimate(
            flops=2 * TOK * D * HID * 3, bytes_accessed=32 * MIB, transcendentals=0
        ),
    )(hid, weights)


def weight_grad_kernel(mid_ref, grad_ref, hid_ref, out_ref):
    part = pl.program_id(0)

    @pl.when(part < 2)
    def _():
        out_ref[...] = matmul(mid_ref[...], hid_ref[0]).astype(BF16)

    @pl.when(part == 2)
    def _():
        out_ref[...] = matmul(grad_ref[...], hid_ref[0]).astype(BF16)


def weight_grads(mid_t, grad_t, hid):
    parts = HID // BLK
    whole = pl.BlockSpec((D, TOK), lambda s, j: (0, 0))
    return pl.pallas_call(
        weight_grad_kernel,
        grid=(3, parts),
        out_shape=jax.ShapeDtypeStruct((D, 3 * HID), BF16),
        in_specs=[whole, whole, pl.BlockSpec((1, TOK, BLK), lambda s, j: (s, 0, j))],
        out_specs=pl.BlockSpec((D, BLK), lambda s, j: (0, s * parts + j)),
        compiler_params=pltpu.CompilerParams(vmem_limit_bytes=48 * MIB),
        cost_estimate=pl.CostEstimate(
            flops=2 * TOK * D * HID * 3, bytes_accessed=32 * MIB, transcendentals=0
        ),
    )(mid_t, grad_t, hid)


def pack_hidden(shared, routed):
    rows = shared.shape[0]
    return jnp.concatenate(
        [
            shared,
            jnp.swapaxes(routed, 0, 1).reshape(rows, EXPERTS * ROUTED),
            jnp.zeros((rows, HID - SHARED - EXPERTS * ROUTED), routed.dtype),
        ],
        axis=1,
    )


def local(
    tokens,
    out_grad,
    parents,
    routes,
    gates,
    norm_in,
    w_query,
    w_latent,
    norm_latent,
    w_expand,
    w_output,
    norm_mid,
    w_shared_gate,
    w_shared_up,
    w_shared_down,
    w_expert_gate,
    w_expert_up,
    w_expert_down,
):
    row = lax.axis_index("row")
    col = lax.axis_index("col")
    quarter = row % QUART
    quarter_groups = [[QUART * i + k for i in range(QUART)] for k in range(QUART)]
    own_start = col * OWN
    gain_in = norm_in.astype(F32)
    gain_latent = norm_latent.astype(F32)
    gain_mid = norm_mid.astype(F32)
    heads = 2

    query_pack = w_query.reshape(D // ROWS, heads, QK)
    attn_pack = jnp.concatenate(
        [
            query_pack[:, :, :NOPE].reshape(D // ROWS, heads * NOPE),
            query_pack[:, :, NOPE:].reshape(D // ROWS, heads * ROPE),
            w_output.T,
            w_expand.reshape(D // ROWS, D // ROWS),
            w_latent,
            jnp.zeros((D // ROWS, 128 - LATC), BF16),
        ],
        axis=1,
    )
    ffn_pack = jnp.concatenate(
        [
            pack_hidden(w_shared_gate, w_expert_gate),
            pack_hidden(w_shared_up, w_expert_up),
            pack_hidden(w_shared_down.T, jnp.swapaxes(w_expert_down, 1, 2)),
        ],
        axis=1,
    )
    attn_full = lax.all_gather(attn_pack, "row", axis=0, tiled=True)
    ffn_full = lax.all_gather(ffn_pack, "row", axis=0, tiled=True)
    query_full = attn_full[:, : heads * QK]
    output_full = attn_full[:, 384:640]
    expand_full = attn_full[:, 640:768].reshape(KVL, heads * (NOPE + VDIM))
    latent_full = attn_full[:, 768 : 768 + LATC]

    seg = jnp.maximum(row - (TRUNK // BLK - 1), 0).astype(jnp.int32)
    depths = ancestor_depths(parents, seg.reshape(1))
    starts = jnp.where(seg > 0, TRUNK + BLK * depths, BLK * row)
    positions = (starts[:, None] + jnp.arange(BLK, dtype=jnp.int32)[None, :]).reshape(TOK)
    frequency = THETA ** (-jnp.arange(ROPE // 2, dtype=F32) / (ROPE // 2))
    angles = positions.astype(F32)[:, None] * frequency[None, :]
    cos_table, sin_table = jnp.cos(angles), jnp.sin(angles)

    inputs = share(tokens.reshape(TOK, FEAT), "col", COLS).transpose(1, 0, 2).reshape(TOK, D)
    inputs_float = inputs.astype(F32)
    scale_in = inverse_rms(inputs_float)
    normed_in = (inputs_float * scale_in * gain_in).astype(BF16)
    latent_part = matmul(normed_in, latent_full).astype(BF16)
    latent = share(latent_part, "col", COLS).transpose(1, 0, 2).reshape(TOK, LAT)
    query_pre = matmul(normed_in, query_full)
    query_nope = query_pre[:, : heads * NOPE].reshape(TOK, heads, NOPE)
    query_rope = rotate(
        query_pre[:, heads * NOPE :].reshape(TOK, heads, ROPE),
        cos_table[:, None, :],
        sin_table[:, None, :],
    )
    query = jnp.concatenate([query_nope, query_rope], axis=-1).astype(BF16)
    query = query.reshape(MICRO, BLK, heads, QK).transpose(2, 0, 1, 3)
    query = swap(query.reshape(heads * MICRO, BLK, QK), "row", quarter_groups)
    compressed = latent[:, :KVL].astype(F32)
    scale_latent = inverse_rms(compressed)
    latent_normed = (compressed * scale_latent * gain_latent).astype(BF16)
    expanded = matmul(latent_normed, expand_full).astype(BF16)
    rope_keys = rotate(latent[:, KVL:].astype(F32), cos_table, sin_table).astype(BF16)
    pack = jnp.concatenate(
        [
            expanded.reshape(MICRO, BLK, heads, NOPE + VDIM).transpose(2, 0, 1, 3),
            jnp.broadcast_to(rope_keys.reshape(1, MICRO, BLK, ROPE), (heads, MICRO, BLK, ROPE)),
        ],
        axis=-1,
    ).reshape(heads * MICRO, 1, BLK, QK + VDIM)
    pack = jnp.broadcast_to(pack, (heads * MICRO, QUART, BLK, QK + VDIM))
    pack = swap(pack.reshape(ROWS, BLK, QK + VDIM), "row")

    keys = jnp.concatenate([pack[:, :, :NOPE], pack[:, :, NOPE + VDIM :]], axis=-1)
    values = pack[:, :, NOPE : NOPE + VDIM]
    keys_t = jnp.swapaxes(keys, 1, 2)
    values_t = jnp.swapaxes(values, 1, 2)
    tree = (row // QUART) % MICRO
    own_parents = lax.dynamic_index_in_dim(parents, tree, 0, keepdims=False)
    meta = jnp.concatenate([own_parents, quarter.astype(jnp.int32).reshape(1)])
    attended_own, lse = attend(meta, query, keys, values_t)

    def to_heads(blocks):
        width = blocks.shape[-1]
        blocks = swap(blocks, "row", quarter_groups).reshape(heads, MICRO, BLK, width)
        return blocks.transpose(1, 2, 0, 3).reshape(TOK, heads, width)

    attended = to_heads(attended_own).reshape(TOK, heads * VDIM)

    attn_part = matmul_nt(attended, output_full).astype(BF16)
    attn_sum = jnp.sum(swap(attn_part.reshape(COLS, OWN, D), "col").astype(F32), axis=0)
    own_inputs = lax.dynamic_slice_in_dim(inputs, own_start, OWN, 0).astype(F32)
    residual = own_inputs + attn_sum
    scale_mid = inverse_rms(residual)
    normed_own = (residual * scale_mid * gain_mid).astype(BF16)
    normed_mid = share(normed_own, "col", COLS).reshape(TOK, D)

    grad_full = share(out_grad.reshape(TOK, FEAT), "col", COLS).transpose(1, 0, 2).reshape(TOK, D)
    named = routes.reshape(TOK, TOPK, 1) == jnp.arange(EXPERTS, dtype=jnp.int32)
    gate_of = jnp.sum(jnp.where(named, gates.reshape(TOK, TOPK, 1), 0.0), axis=1)
    gate_of = jnp.concatenate(
        [jnp.ones((TOK, 1), F32), gate_of, jnp.zeros((TOK, 15 - EXPERTS), F32)], axis=1
    )
    gate_high = gate_of.astype(BF16)
    gate_low = (gate_of - gate_high.astype(F32)).astype(BF16)
    unit = jnp.arange(HID, dtype=jnp.int32)
    group = jnp.where(unit < SHARED, 0, 1 + (unit - SHARED) // ROUTED)
    spread = (group[None, :] == jnp.arange(16, dtype=jnp.int32)[:, None]).astype(BF16)
    hid = hidden(
        normed_mid,
        grad_full,
        jnp.concatenate([gate_high, gate_low], axis=1),
        jnp.concatenate([spread, spread], axis=0),
        ffn_full,
    )
    out_part, mid_part = model(hid, ffn_full)
    d_mid = jnp.sum(swap(mid_part.reshape(COLS, OWN, D), "col").astype(F32), axis=0)
    mid_gain = jnp.sum(d_mid * residual * scale_mid, axis=0)
    own_grad = lax.dynamic_slice_in_dim(grad_full, own_start, OWN, 0).astype(F32)
    d_residual = own_grad + norm_backward(d_mid, residual, scale_mid, gain_mid)
    d_low = share(d_residual.astype(BF16), "col", COLS).reshape(TOK, D)

    def by_feature(own):
        return own.reshape(OWN, COLS, FEAT).transpose(1, 0, 2)

    own_part = lax.dynamic_slice_in_dim(out_part, own_start, OWN, 1)
    own_part = (own_part.astype(F32) + by_feature(residual)).astype(BF16)
    out_part = lax.dynamic_update_slice_in_dim(out_part, own_part, own_start, 1)
    layer_out = jnp.sum(swap(out_part, "col").astype(F32), axis=0).astype(BF16)

    ffn_grads = weight_grads(normed_mid.T, grad_full.T, hid)
    ffn_grads = lax.psum_scatter(ffn_grads, "row", scatter_dimension=0, tiled=True)

    d_attended = matmul(d_low, output_full).astype(BF16)
    d_attended = d_attended.reshape(MICRO, BLK, heads, VDIM).transpose(2, 0, 1, 3)
    d_attended = swap(d_attended.reshape(heads * MICRO, BLK, VDIM), "row", quarter_groups)
    d_query, d_pack = attend_back(
        meta, query, keys, keys_t, values, attended_own, lse, d_attended
    )
    d_query = to_heads(d_query)
    d_query_rope = rotate(
        d_query[:, :, NOPE:].astype(F32), cos_table[:, None, :], -sin_table[:, None, :]
    ).astype(BF16)
    d_query_pre = jnp.concatenate(
        [
            d_query[:, :, :NOPE].reshape(TOK, heads * NOPE),
            d_query_rope.reshape(TOK, heads * ROPE),
        ],
        axis=1,
    )
    d_pack = swap(d_pack, "row").reshape(heads, MICRO, QUART, BLK, QK + VDIM)
    d_pack = jnp.sum(d_pack.astype(F32), axis=2)
    d_expanded = d_pack[..., : NOPE + VDIM].transpose(1, 2, 0, 3)
    d_expanded = d_expanded.reshape(TOK, heads * (NOPE + VDIM)).astype(BF16)
    d_rope_keys = jnp.sum(d_pack[..., NOPE + VDIM :], axis=0).reshape(TOK, ROPE)

    d_latent_normed = matmul_nt(d_expanded, expand_full)
    latent_gain = jnp.sum(d_latent_normed * compressed * scale_latent, axis=0)
    d_latent = jnp.concatenate(
        [
            norm_backward(d_latent_normed, compressed, scale_latent, gain_latent),
            rotate(d_rope_keys, cos_table, -sin_table),
        ],
        axis=1,
    ).astype(BF16)
    d_latent = swap(d_latent.reshape(TOK, COLS, LATC).transpose(1, 0, 2), "col")
    d_latent = jnp.sum(d_latent.astype(F32), axis=0).astype(BF16)

    d_in = matmul_nt(d_query_pre, query_full) + matmul_nt(d_latent, latent_full)
    in_gain = jnp.sum(d_in * inputs_float * scale_in, axis=0)
    d_tokens = norm_backward(d_in, inputs_float, scale_in, gain_in)
    own_tokens = lax.dynamic_slice_in_dim(d_tokens, own_start, OWN, 0) + d_residual
    d_tokens = lax.dynamic_update_slice_in_dim(d_tokens, own_tokens, own_start, 0)
    d_tokens = d_tokens.astype(BF16).reshape(TOK, COLS, FEAT).transpose(1, 0, 2)
    input_grad = jnp.sum(swap(d_tokens, "col").astype(F32), axis=0).astype(BF16)

    attn_grads = jnp.concatenate(
        [
            matmul_tn(normed_in, d_query_pre).astype(BF16),
            matmul_tn(d_low, attended).astype(BF16),
            matmul_tn(latent_normed, d_expanded).astype(BF16).reshape(D, D // ROWS),
            matmul_tn(normed_in, d_latent).astype(BF16),
            jnp.zeros((D, 128 - LATC), BF16),
        ],
        axis=1,
    )
    attn_grads = swap(attn_grads.reshape(ROWS, D // ROWS, attn_grads.shape[1]), "row")
    attn_grads = jnp.sum(attn_grads.astype(F32), axis=0)
    grad_query = jnp.concatenate(
        [
            attn_grads[:, : heads * NOPE].reshape(-1, heads, NOPE),
            attn_grads[:, heads * NOPE : heads * QK].reshape(-1, heads, ROPE),
        ],
        axis=-1,
    ).reshape(-1, heads * QK)
    grad_output = attn_grads[:, 384:640].T
    grad_expand = attn_grads[:, 640:768].reshape(KVL // ROWS, heads * (NOPE + VDIM))
    grad_latent = attn_grads[:, 768 : 768 + LATC]

    def unpack(at):
        part = ffn_grads[:, at * HID : (at + 1) * HID].astype(F32)
        routed = part[:, SHARED : SHARED + EXPERTS * ROUTED]
        return part[:, :SHARED], routed.reshape(-1, EXPERTS, ROUTED)

    grad_shared_gate, grad_expert_gate = unpack(0)
    grad_shared_up, grad_expert_up = unpack(1)
    grad_shared_down, grad_expert_down = unpack(2)

    world = ("row", "col")
    gain = jnp.concatenate([in_gain, latent_gain, mid_gain]).reshape(ROWS * COLS, -1)
    gain = jnp.sum(swap(gain, world), axis=0)
    gain = share(gain, world, ROWS * COLS).reshape(-1)
    return (
        layer_out.reshape(MICRO, BLK, FEAT),
        input_grad.reshape(MICRO, BLK, FEAT),
        gain[:D],
        grad_query,
        grad_latent,
        gain[D : D + KVL],
        grad_expand,
        grad_output,
        gain[D + KVL :],
        grad_shared_gate,
        grad_shared_up,
        grad_shared_down.T,
        jnp.swapaxes(grad_expert_gate, 0, 1),
        jnp.swapaxes(grad_expert_up, 0, 1),
        grad_expert_down.transpose(1, 2, 0),
    )


def solution(mesh):
    in_specs = (
        P(None, "row", "col"),
        P(None, "row", "col"),
        P(),
        P(None, "row", None),
        P(None, "row", None),
        P(),
        P("row", "col"),
        P("row", "col"),
        P(),
        P("row", "col"),
        P("col", "row"),
        P(),
        P("row", "col"),
        P("row", "col"),
        P("col", "row"),
        P(None, "row", "col"),
        P(None, "row", "col"),
        P(None, "col", "row"),
    )
    out_specs = (
        P(None, "row", "col"),
        P(None, "row", "col"),
        P(),
        P("row", "col"),
        P("row", "col"),
        P(),
        P("row", "col"),
        P("col", "row"),
        P(),
        P("row", "col"),
        P("row", "col"),
        P("col", "row"),
        P(None, "row", "col"),
        P(None, "row", "col"),
        P(None, "col", "row"),
    )
    return jax.shard_map(local, mesh=mesh, in_specs=in_specs, out_specs=out_specs, check_vma=False)
```

```python
import functools

import jax
import jax.numpy as jnp
from jax import lax
from jax.experimental import pallas as pl
from jax.experimental.pallas import tpu as pltpu
from jax.sharding import PartitionSpec as P

D = 2048
NOPE = 128
ROPE = 64
QK = NOPE + ROPE
VDIM = 128
KVL = 512
TOPK = 6
EXPERTS = 8
MICRO = 2
TRUNK = 1024
BLK = 256
SEGS = 13
ROWS = 16
COLS = 8
TOK = MICRO * BLK
OWN = TOK // COLS
FEAT = D // COLS
QUART = 4
SHARED = 352
ROUTED = 176
HID = 1792
LAT = KVL + ROPE
HALF = BLK // 2
QKP = 256
PACK = VDIM + QKP
WIDE = 3 * HID
CUT = WIDE // 2
LANES = D // ROWS
LATC = LAT // COLS
SCALE = QK**-0.5
EPS = 1e-06
THETA = 10000.0
NEG = -1e30
MIB = 1024 * 1024
F32 = jnp.float32
BF16 = jnp.bfloat16
NT = (((1,), (1,)), ((), ()))
TN = (((0,), (0,)), ((), ()))


def inverse_rms(values):
    return lax.rsqrt(jnp.mean(values * values, axis=-1, keepdims=True) + EPS)


def norm_backward(grad_out, values, inv_scale, norm_gain):
    weighted = grad_out * norm_gain
    inner = jnp.mean(weighted * values, axis=-1, keepdims=True)
    return inv_scale * weighted - values * (inv_scale * inv_scale * inv_scale) * inner


def matmul(a, b):
    return jnp.dot(a, b, preferred_element_type=F32)


def matmul_nt(a, b):
    return lax.dot_general(a, b, NT, preferred_element_type=F32)


def matmul_tn(a, b):
    return lax.dot_general(a, b, TN, preferred_element_type=F32)


def swap(values, axis, groups=None):
    return lax.all_to_all(values, axis, 0, 0, tiled=True, axis_index_groups=groups)


def share(values, axis, count):
    return swap(jnp.broadcast_to(values[None], (count,) + values.shape), axis)


def trade(values, axis, mask):
    count = ROWS if axis == "row" else COLS
    return lax.ppermute(values, axis, [(i, i ^ mask) for i in range(count)])


def after(values, *others):
    return lax.optimization_barrier((values,) + others)[0]


def together(*values):
    return lax.optimization_barrier(values)


def smem_values(*values):
    return jnp.stack([jnp.asarray(v, jnp.int32) for v in values])


def pick(values, index, axis=0):
    return lax.dynamic_index_in_dim(values, index, axis, keepdims=False)


def pair_up(shard, axis):
    return jnp.stack([shard, trade(shard, axis, 8 if axis == "row" else 1)])


def ring_up(pair, axis):
    return [pair] + [trade(pair, axis, j << 1) for j in (1, 2, 3)]


def sort_rows_kernel(own_ref, near_ref, far_ref, out_ref):
    for core, ref in ((0, near_ref), (1, far_ref)):
        for x in range(4):
            for z in range(2):
                out_ref[own_ref[0] ^ (8 * z + 2 * x + core)] = ref[x, z]


def finish_rows(ring, row):
    near = jnp.stack(ring)
    far = trade(near, "row", 1)
    vmem = pl.BlockSpec(memory_space=pltpu.VMEM)
    out = pl.pallas_call(
        sort_rows_kernel,
        out_shape=jax.ShapeDtypeStruct((ROWS,) + near.shape[2:], near.dtype),
        in_specs=[pl.BlockSpec(memory_space=pltpu.SMEM), vmem, vmem],
        out_specs=vmem,
        compiler_params=pltpu.CompilerParams(vmem_limit_bytes=16 * MIB),
        cost_estimate=pl.CostEstimate(flops=0, bytes_accessed=near.size, transcendentals=0),
    )(smem_values(row), near, far)
    return out.reshape(D, near.shape[3])


def place_of(apart):
    return ((apart & 1) << 3) | ((apart >> 3) << 2) | ((apart >> 1) & 3)


def lanes(at):
    return pl.ds(pl.multiple_of(at * LANES, LANES), LANES)


def features_kernel(own_ref, blocks_ref, out_ref, out_t_ref):
    for c in range(COLS):
        out_ref[:, c * FEAT : (c + 1) * FEAT] = blocks_ref[c]
    for r in range(ROWS):
        block = blocks_ref[r // 2, :, (r % 2) * LANES : (r % 2 + 1) * LANES]
        out_t_ref[lanes(place_of(own_ref[0] ^ r)), :] = block.T


def features(row, blocks):
    vmem = pl.BlockSpec(memory_space=pltpu.VMEM)
    return pl.pallas_call(
        features_kernel,
        out_shape=(
            jax.ShapeDtypeStruct((TOK, D), BF16),
            jax.ShapeDtypeStruct((D, TOK), BF16),
        ),
        in_specs=[pl.BlockSpec(memory_space=pltpu.SMEM), vmem],
        out_specs=(vmem, vmem),
        compiler_params=pltpu.CompilerParams(vmem_limit_bytes=60 * MIB),
        cost_estimate=pl.CostEstimate(flops=0, bytes_accessed=MIB, transcendentals=0),
    )(smem_values(row), blocks)


def turn_kernel(own_ref, x_ref, out_ref):
    for r in range(ROWS):
        block = x_ref[:, r * LANES : (r + 1) * LANES]
        out_ref[lanes(place_of(own_ref[0] ^ r)), :] = block.T


def turn(row, values):
    vmem = pl.BlockSpec(memory_space=pltpu.VMEM)
    return pl.pallas_call(
        turn_kernel,
        out_shape=jax.ShapeDtypeStruct((D, TOK), BF16),
        in_specs=[pl.BlockSpec(memory_space=pltpu.SMEM), vmem],
        out_specs=vmem,
        compiler_params=pltpu.CompilerParams(vmem_limit_bytes=60 * MIB),
        cost_estimate=pl.CostEstimate(flops=0, bytes_accessed=MIB, transcendentals=0),
    )(smem_values(row), values)


def near_shards(shard):
    return trade(shard, "row", 2), trade(shard, "row", 6)


def far_halves(near):
    return trade(near[1][:, :CUT], "row", 2), trade(near[0][:, CUT:], "row", 6)


def put_kernel(places, own_ref, *refs):
    out_ref, sems = refs[-2:]
    copies = []
    for i, (apart, first) in enumerate(places):
        rows = lanes(own_ref[0] ^ apart)
        columns = pl.ds(first, refs[i].shape[1])
        copy = pltpu.make_async_copy(refs[i], out_ref.at[rows, columns], sems.at[i])
        copy.start()
        copies.append(copy)
    for copy in copies:
        copy.wait()


def put_shards(row, whole, pieces):
    values = [piece for piece, _, _ in pieces]
    places = [(apart, first) for _, apart, first in pieces]
    fresh = whole is None
    return pl.pallas_call(
        functools.partial(put_kernel, places),
        out_shape=jax.ShapeDtypeStruct((D, WIDE), BF16),
        in_specs=[pl.BlockSpec(memory_space=pltpu.SMEM)]
        + [pl.BlockSpec(memory_space=pltpu.VMEM)] * len(values)
        + ([] if fresh else [pl.BlockSpec(memory_space=pl.ANY)]),
        out_specs=pl.BlockSpec(memory_space=pl.ANY),
        scratch_shapes=[pltpu.SemaphoreType.DMA((len(values),))],
        input_output_aliases={} if fresh else {1 + len(values): 0},
        compiler_params=pltpu.CompilerParams(vmem_limit_bytes=60 * MIB),
        cost_estimate=pl.CostEstimate(flops=0, bytes_accessed=MIB, transcendentals=0),
    )(smem_values(row), *values, *([] if fresh else [whole]))


def sum_opposite(blocks):
    return trade(blocks[2][:, :CUT], "row", 2), trade(blocks[2][:, CUT:], "row", 6)


def add_low(a, b):
    return (a.astype(F32) + b.astype(F32)).astype(BF16)


def sides_kernel(b1_ref, b3_ref, h1_ref, h3_ref, left_ref, right_ref):
    left_ref[:, :CUT] = b1_ref[:, :CUT]
    left_ref[:, CUT:] = (b1_ref[:, CUT:].astype(F32) + h3_ref[...].astype(F32)).astype(BF16)
    right_ref[:, :CUT] = (b3_ref[:, :CUT].astype(F32) + h1_ref[...].astype(F32)).astype(BF16)
    right_ref[:, CUT:] = b3_ref[:, CUT:]


def with_opposite(blocks, halves):
    return pl.pallas_call(
        sides_kernel,
        out_shape=[jax.ShapeDtypeStruct((LANES, WIDE), BF16)] * 2,
        compiler_params=pltpu.CompilerParams(vmem_limit_bytes=60 * MIB),
        cost_estimate=pl.CostEstimate(flops=0, bytes_accessed=MIB, transcendentals=0),
    )(blocks[1], blocks[3], *halves)


def sum_neighbours(sides):
    return trade(sides[0], "row", 2), trade(sides[1], "row", 6)


def reduce_row(keep, send):
    shape = (4, 2) + keep.shape[1:]
    blocks = add_low(keep, trade(send, "row", 1)).reshape(shape)
    got = [trade(blocks[j], "row", j << 1).astype(F32) for j in (1, 2, 3)]
    blocks = (blocks[0].astype(F32) + got[0] + got[1] + got[2]).astype(BF16)
    return blocks[0].astype(F32) + trade(blocks[1], "row", 8).astype(F32)


def attn_grads_kernel(
    own_ref, x_ref, dq_ref, dl_ref, low_ref, att_ref, lat_ref, de_ref, keep_ref, send_ref, out
):
    out[:, :384] = matmul_tn(x_ref[...], dq_ref[...])
    out[:, 384:640] = matmul_tn(low_ref[...], att_ref[...])
    expand_grad = matmul(lat_ref[...], de_ref[...])
    for half in range(2):
        for i in range(4):
            rows = slice(half * LANES + 32 * i, half * LANES + 32 * (i + 1))
            part = expand_grad[32 * half : 32 * (half + 1), 128 * i : 128 * (i + 1)]
            out[rows, 640:768] = part
    out[:, 768:] = matmul_tn(x_ref[...], dl_ref[...])
    core = own_ref[0] & 1
    keep_ref[0] = out[lanes(core), :].astype(BF16)
    send_ref[0] = out[lanes(1 - core), :].astype(BF16)


def attn_weight_grads(row, normed, d_query, d_latent, d_low, attended, latent_t, d_expanded):
    def whole(shape):
        return pl.BlockSpec(shape, lambda i, own: (0, 0))

    def place(i, own):
        apart = i ^ (own[0] >> 1)
        return (apart & 3) * 2 + (apart >> 2), 0, 0

    columns = pl.BlockSpec((TOK, 2 * LANES), lambda i, own: (0, i))
    block = pl.BlockSpec((1, LANES, 896), place)
    return pl.pallas_call(
        attn_grads_kernel,
        out_shape=[jax.ShapeDtypeStruct((ROWS // 2, LANES, 896), BF16)] * 2,
        grid_spec=pltpu.PrefetchScalarGridSpec(
            num_scalar_prefetch=1,
            grid=(ROWS // 2,),
            in_specs=[
                columns,
                whole(d_query.shape),
                whole(d_latent.shape),
                columns,
                whole(attended.shape),
                pl.BlockSpec((2 * KVL // ROWS, TOK), lambda i, own: (i, 0)),
                whole(d_expanded.shape),
            ],
            out_specs=[block, block],
            scratch_shapes=[pltpu.VMEM((2 * LANES, 896), F32)],
        ),
        compiler_params=pltpu.CompilerParams(vmem_limit_bytes=60 * MIB),
        cost_estimate=pl.CostEstimate(flops=TOK * D * 64, bytes_accessed=MIB, transcendentals=0),
    )(smem_values(row), normed, d_query, d_latent, d_low, attended, latent_t, d_expanded)


def collect_y(blocks, y):
    blocks = blocks.reshape((4, 2) + blocks.shape[1:])
    return [pick(blocks, y)] + [trade(pick(blocks, y ^ j), "col", j << 1) for j in (1, 2, 3)]


def collect_z(blocks, z):
    blocks = [block.astype(F32) for block in blocks]
    blocks = (blocks[0] + blocks[1] + (blocks[2] + blocks[3])).astype(BF16)
    got = trade(pick(blocks, 1 - z), "col", 1)
    return pick(blocks, z).astype(F32) + got.astype(F32)


def trade_quarter(blocks):
    return [blocks[0]] + [trade(blocks[j], "row", j << 2) for j in (1, 2, 3)]


def depth_kernel(parents_ref, seg_ref, out_ref):
    seg = seg_ref[0]
    for m in range(MICRO):

        def climb(step, state):
            at, count = state
            return parents_ref[m, at], count + (at > 0).astype(jnp.int32)

        _, count = lax.fori_loop(0, SEGS, climb, (parents_ref[m, seg], jnp.int32(0)))
        out_ref[m] = count


def ancestor_depths(parents, seg):
    smem = pl.BlockSpec(memory_space=pltpu.SMEM)
    return pl.pallas_call(
        depth_kernel,
        out_shape=jax.ShapeDtypeStruct((MICRO,), jnp.int32),
        in_specs=[smem, smem],
        out_specs=smem,
    )(parents, seg)


def list_ancestors(meta, qb, listed):
    def climb(step, state):
        at, count = state
        listed[count] = at + 3
        return meta[at], count + (at > 0).astype(jnp.int32)

    _, count = lax.fori_loop(0, SEGS, climb, (meta[qb - 3], jnp.int32(0)))
    return count


def causal_mask():
    key = lax.broadcasted_iota(jnp.int32, (BLK, BLK), 0)
    query = lax.broadcasted_iota(jnp.int32, (BLK, BLK), 1)
    return key <= query


def join_halves(meta, near_ref, far_ref, pack):
    core = meta[SEGS] % 2
    pack[:, pl.ds(pl.multiple_of(core * HALF, HALF), HALF), :] = near_ref[...]
    pack[:, pl.ds(pl.multiple_of((1 - core) * HALF, HALF), HALF), :] = far_ref[...]


def attend_kernel(meta, q0, q1, q2, q3, near_ref, far_ref, o0, o1, o2, o3, lse_ref, *scratch):
    q_ref, o_ref, pack, listed = scratch
    quarter, own = meta[SEGS], meta[SEGS + 1]
    join_halves(meta, near_ref, far_ref, pack)
    for j, ref in enumerate((q0, q1, q2, q3)):
        q_ref[own ^ j] = ref[...]
    for i in range(QUART):
        qb = QUART * i + quarter
        q = q_ref[i]
        s = matmul_nt(pack[qb, :, VDIM:], q) * SCALE
        s = jnp.where(causal_mask(), s, NEG)
        top = jnp.max(s, axis=0, keepdims=True)
        p = jnp.exp(s - top)
        total = jnp.sum(p, axis=0, keepdims=True)
        out = matmul_tn(pack[qb, :, :VDIM], p.astype(BF16))

        def step(kb, state):
            top, total, out = state
            s = matmul_nt(pack[kb, :, VDIM:], q) * SCALE
            new_top = jnp.maximum(top, jnp.max(s, axis=0, keepdims=True))
            shrink = jnp.exp(top - new_top)
            p = jnp.exp(s - new_top)
            total = total * shrink + jnp.sum(p, axis=0, keepdims=True)
            out = out * shrink + matmul_tn(pack[kb, :, :VDIM], p.astype(BF16))
            return new_top, total, out

        state = (top, total, out)
        if i == 0:
            state = lax.fori_loop(0, quarter, step, state)
        else:
            for kb in range(TRUNK // BLK):
                state = step(kb, state)
            count = list_ancestors(meta, qb, listed)
            state = lax.fori_loop(0, count, lambda t, c: step(listed[t], c), state)
        top, total, out = state
        o_ref[i] = (out * (1.0 / total)).T.astype(BF16)
        lse_ref[i] = top + jnp.log(total)
    for j, ref in enumerate((o0, o1, o2, o3)):
        ref[...] = o_ref[own ^ j]


def attend(meta, q, near, far):
    smem = pl.BlockSpec(memory_space=pltpu.SMEM)
    vmem = pl.BlockSpec(memory_space=pltpu.VMEM)
    pairs = 32 * BLK * BLK
    return pl.pallas_call(
        attend_kernel,
        out_shape=[jax.ShapeDtypeStruct((BLK, VDIM), BF16)] * QUART
        + [jax.ShapeDtypeStruct((QUART, 1, BLK), F32)],
        in_specs=[smem] + [vmem] * 6,
        out_specs=[vmem] * 5,
        scratch_shapes=[
            pltpu.VMEM((QUART, BLK, QKP), BF16),
            pltpu.VMEM((QUART, BLK, VDIM), BF16),
            pltpu.VMEM((ROWS, BLK, PACK), BF16),
            pltpu.SMEM((16,), jnp.int32),
        ],
        compiler_params=pltpu.CompilerParams(vmem_limit_bytes=60 * MIB),
        cost_estimate=pl.CostEstimate(
            flops=pairs * 2 * (QK + VDIM), bytes_accessed=4 * MIB, transcendentals=pairs
        ),
    )(meta, *q, near, far)


def attend_back_kernel(meta, *refs):
    ins, outs, scratch = refs[:15], refs[15:21], refs[21:]
    near_ref, far_ref, lse_ref = ins[12:]
    keep_ref, send_ref = outs[4:]
    q_ref, o_ref, do_ref, dq_ref, pack, dk, dv, listed = scratch
    quarter, own = meta[SEGS], meta[SEGS + 1]
    core = quarter % 2
    join_halves(meta, near_ref, far_ref, pack)
    for j in range(QUART):
        q_ref[own ^ j] = ins[j][...]
        o_ref[own ^ j] = ins[QUART + j][...]
        do_ref[own ^ j] = ins[2 * QUART + j][...]
    dk[...] = jnp.zeros_like(dk)
    dv[...] = jnp.zeros_like(dv)
    for i in range(QUART):
        qb = QUART * i + quarter
        q = q_ref[i]
        do = do_ref[i]
        lse = lse_ref[i]
        pairs = do.astype(F32) * o_ref[i].astype(F32)
        delta = jnp.sum(pairs.T, axis=0, keepdims=True)

        def step(kb, dqt, masked=False):
            key = pack[kb, :, VDIM:]
            s = matmul_nt(key, q) * SCALE
            p = jnp.exp(s - lse)
            if masked:
                p = jnp.where(causal_mask(), p, 0.0)
            dp = matmul_nt(pack[kb, :, :VDIM], do)
            ds = (p * (dp - delta) * SCALE).astype(BF16)
            dv[kb] += matmul(p.astype(BF16), do)
            dk[kb] += matmul(ds, q)
            return dqt + matmul_tn(key, ds)

        dqt = step(qb, jnp.zeros((QKP, BLK), F32), True)
        if i == 0:
            dqt = lax.fori_loop(0, quarter, step, dqt)
        else:
            for kb in range(TRUNK // BLK):
                dqt = step(kb, dqt)
            count = list_ancestors(meta, qb, listed)
            dqt = lax.fori_loop(0, count, lambda t, c: step(listed[t], c), dqt)
        dq_ref[i] = dqt.T.astype(BF16)
    for j in range(QUART):
        outs[j][...] = dq_ref[own ^ j]
    for half, ref in ((core, keep_ref), (1 - core, send_ref)):
        part = pl.ds(pl.multiple_of(half * HALF, HALF), HALF)
        ref[:, :, :VDIM] = dv[:, part, :].astype(BF16)
        ref[:, :, VDIM:] = dk[:, part, :].astype(BF16)


def attend_back(meta, q, o, d_o, near, far, lse):
    smem = pl.BlockSpec(memory_space=pltpu.SMEM)
    vmem = pl.BlockSpec(memory_space=pltpu.VMEM)
    pairs = 32 * BLK * BLK
    return pl.pallas_call(
        attend_back_kernel,
        out_shape=[jax.ShapeDtypeStruct((BLK, QKP), BF16)] * QUART
        + [jax.ShapeDtypeStruct((ROWS, HALF, PACK), BF16)] * 2,
        in_specs=[smem] + [vmem] * 15,
        out_specs=[vmem] * 6,
        scratch_shapes=[
            pltpu.VMEM((QUART, BLK, QKP), BF16),
            pltpu.VMEM((QUART, BLK, VDIM), BF16),
            pltpu.VMEM((QUART, BLK, VDIM), BF16),
            pltpu.VMEM((QUART, BLK, QKP), BF16),
            pltpu.VMEM((ROWS, BLK, PACK), BF16),
            pltpu.VMEM((ROWS, BLK, QKP), F32),
            pltpu.VMEM((ROWS, BLK, VDIM), F32),
            pltpu.SMEM((16,), jnp.int32),
        ],
        compiler_params=pltpu.CompilerParams(vmem_limit_bytes=60 * MIB),
        cost_estimate=pl.CostEstimate(
            flops=pairs * 2 * (3 * QK + 2 * VDIM), bytes_accessed=10 * MIB, transcendentals=pairs
        ),
    )(meta, *q, *o, *d_o, near, far, lse)


def project_kernel(own_ref, b0, b1, b2, b3, w_ref, attended_ref, out_ref, blocks):
    for j, ref in enumerate((b0, b1, b2, b3)):
        blocks[own_ref[0] ^ j] = ref[...]
    for h in range(2):
        for m in range(MICRO):
            attended_ref[m * BLK : (m + 1) * BLK, h * VDIM : (h + 1) * VDIM] = blocks[2 * h + m]
    out = matmul_nt(attended_ref[...], w_ref[...]).astype(BF16)
    for c in range(COLS):
        out_ref[c] = out[c * OWN : (c + 1) * OWN]


def project(own, blocks, w_output):
    vmem = pl.BlockSpec(memory_space=pltpu.VMEM)
    return pl.pallas_call(
        project_kernel,
        out_shape=(
            jax.ShapeDtypeStruct((TOK, 2 * VDIM), BF16),
            jax.ShapeDtypeStruct((COLS, OWN, D), BF16),
        ),
        in_specs=[pl.BlockSpec(memory_space=pltpu.SMEM)] + [vmem] * 5,
        out_specs=(vmem, vmem),
        scratch_shapes=[pltpu.VMEM((QUART, BLK, VDIM), BF16)],
        compiler_params=pltpu.CompilerParams(vmem_limit_bytes=60 * MIB),
        cost_estimate=pl.CostEstimate(flops=TOK * D * 512, bytes_accessed=MIB, transcendentals=0),
    )(smem_values(own), *blocks, w_output)


def project_back_kernel(own_ref, d_ref, w_ref, o0, o1, o2, o3, blocks):
    for c in range(COLS):
        rows = slice((c % QUART) * OWN, (c % QUART + 1) * OWN)
        part = matmul(d_ref[c], w_ref[...]).astype(BF16)
        for h in range(2):
            blocks[2 * h + c // QUART, rows, :] = part[:, h * VDIM : (h + 1) * VDIM]
    for j, ref in enumerate((o0, o1, o2, o3)):
        ref[...] = blocks[own_ref[0] ^ j]


def project_back(own, d_low, w_output):
    vmem = pl.BlockSpec(memory_space=pltpu.VMEM)
    return pl.pallas_call(
        project_back_kernel,
        out_shape=[jax.ShapeDtypeStruct((BLK, VDIM), BF16)] * QUART,
        in_specs=[pl.BlockSpec(memory_space=pltpu.SMEM)] + [vmem] * 2,
        out_specs=[vmem] * QUART,
        scratch_shapes=[pltpu.VMEM((QUART, BLK, VDIM), BF16)],
        compiler_params=pltpu.CompilerParams(vmem_limit_bytes=60 * MIB),
        cost_estimate=pl.CostEstimate(flops=TOK * D * 512, bytes_accessed=MIB, transcendentals=0),
    )(smem_values(own), d_low, w_output)


def front_kernel(col_ref, p0, p1, p2, p3, gain_ref, wl_ref, x_ref, normed_ref, scale_ref, lat_ref):
    for y, ref in enumerate((p0, p1, p2, p3)):
        for z in range(2):
            at = (col_ref[0] ^ (2 * y + z)) * FEAT
            x_ref[:, pl.ds(pl.multiple_of(at, FEAT), FEAT)] = ref[z]
    x = x_ref[...].astype(F32)
    scale = inverse_rms(x)
    scale_ref[...] = scale
    normed = (x * scale * gain_ref[...]).astype(BF16)
    normed_ref[...] = normed
    latent = matmul(normed, wl_ref[...]).T[:LATC].astype(BF16)
    for c in range(COLS):
        lat_ref[c] = latent


def front(col, ring, gain, w_latent):
    rows = 128
    return pl.pallas_call(
        front_kernel,
        grid=(TOK // rows,),
        out_shape=(
            jax.ShapeDtypeStruct((TOK, D), BF16),
            jax.ShapeDtypeStruct((TOK, D), BF16),
            jax.ShapeDtypeStruct((TOK, 1), F32),
            jax.ShapeDtypeStruct((COLS, LATC, TOK), BF16),
        ),
        in_specs=[pl.BlockSpec(memory_space=pltpu.SMEM)]
        + [pl.BlockSpec((2, rows, FEAT), lambda j: (0, j, 0))] * 4
        + [
            pl.BlockSpec((1, D), lambda j: (0, 0)),
            pl.BlockSpec((D, 128), lambda j: (0, 0)),
        ],
        out_specs=(
            pl.BlockSpec((rows, D), lambda j: (j, 0)),
            pl.BlockSpec((rows, D), lambda j: (j, 0)),
            pl.BlockSpec((rows, 1), lambda j: (j, 0)),
            pl.BlockSpec((COLS, LATC, rows), lambda j: (0, 0, j)),
        ),
        compiler_params=pltpu.CompilerParams(vmem_limit_bytes=60 * MIB),
        cost_estimate=pl.CostEstimate(flops=TOK * D * 256, bytes_accessed=MIB, transcendentals=0),
    )(smem_values(col), *ring, gain.reshape(1, D), w_latent)


def half_turn():
    source = lax.broadcasted_iota(jnp.int32, (2 * ROPE, 2 * ROPE), 0)
    target = lax.broadcasted_iota(jnp.int32, (2 * ROPE, 2 * ROPE), 1)
    half = ROPE // 2
    first = target % ROPE < half
    value = jnp.where(
        first & (source == target + half),
        -1.0,
        jnp.where((target % ROPE >= half) & (source == target - half), 1.0, 0.0),
    )
    return value.astype(BF16)


def query_kernel(own_ref, normed_ref, w_ref, cos_ref, sin_ref, o0, o1, o2, o3, blocks):
    normed = normed_ref[...]
    w_rope = w_ref[:, 2 * NOPE :]
    turned = matmul(w_rope, half_turn()).astype(BF16)
    rope = matmul(normed, w_rope) * cos_ref[...] + matmul(normed, turned) * sin_ref[...]
    rope = rope.astype(BF16)
    nope = matmul(normed, w_ref[:, : 2 * NOPE]).astype(BF16)
    blank = jnp.zeros((BLK, QKP - QK), BF16)
    for h in range(2):
        for m in range(MICRO):
            rows = slice(m * BLK, (m + 1) * BLK)
            blocks[2 * h + m, :, :NOPE] = nope[rows, h * NOPE : (h + 1) * NOPE]
            blocks[2 * h + m, :, NOPE:QK] = rope[rows, h * ROPE : (h + 1) * ROPE]
            blocks[2 * h + m, :, QK:] = blank
    for j, ref in enumerate((o0, o1, o2, o3)):
        ref[...] = blocks[own_ref[0] ^ j]


def project_query(own, normed, w_query, cos_wide, sin_wide):
    vmem = pl.BlockSpec(memory_space=pltpu.VMEM)
    return pl.pallas_call(
        query_kernel,
        out_shape=[jax.ShapeDtypeStruct((BLK, QKP), BF16)] * QUART,
        in_specs=[pl.BlockSpec(memory_space=pltpu.SMEM)] + [vmem] * 4,
        out_specs=[vmem] * QUART,
        scratch_shapes=[pltpu.VMEM((QUART, BLK, QKP), BF16)],
        compiler_params=pltpu.CompilerParams(vmem_limit_bytes=60 * MIB),
        cost_estimate=pl.CostEstimate(flops=TOK * D * 256, bytes_accessed=MIB, transcendentals=0),
    )(smem_values(own), normed, w_query, cos_wide, sin_wide)


def query_back_kernel(own_ref, b0, b1, b2, b3, cos_ref, sin_ref, out_ref, blocks):
    turn = half_turn()
    for j, ref in enumerate((b0, b1, b2, b3)):
        blocks[own_ref[0] ^ j] = ref[...]
    for m in range(MICRO):
        rows = slice(m * BLK, (m + 1) * BLK)
        for h in range(2):
            out_ref[rows, h * NOPE : (h + 1) * NOPE] = blocks[2 * h + m, :, :NOPE]
        rope = jnp.concatenate([blocks[m, :, NOPE:QK], blocks[2 + m, :, NOPE:QK]], axis=1)
        rope = rope.astype(F32) * cos_ref[rows, :] + matmul_nt(rope, turn) * sin_ref[rows, :]
        out_ref[rows, 2 * NOPE :] = rope.astype(BF16)


def query_back(own, blocks, cos_wide, sin_wide):
    vmem = pl.BlockSpec(memory_space=pltpu.VMEM)
    return pl.pallas_call(
        query_back_kernel,
        out_shape=jax.ShapeDtypeStruct((TOK, 2 * QK), BF16),
        in_specs=[pl.BlockSpec(memory_space=pltpu.SMEM)] + [vmem] * 6,
        out_specs=vmem,
        scratch_shapes=[pltpu.VMEM((QUART, BLK, QKP), BF16)],
        compiler_params=pltpu.CompilerParams(vmem_limit_bytes=60 * MIB),
        cost_estimate=pl.CostEstimate(flops=TOK * D * 16, bytes_accessed=MIB, transcendentals=0),
    )(smem_values(own), *blocks, cos_wide, sin_wide)


def expand_kernel(latent_ref, cos_ref, sin_ref, gain_ref, w_ref, normed_ref, out_ref):
    c = latent_ref[:KVL, :].astype(F32)
    scale = lax.rsqrt(jnp.mean(c * c, axis=0, keepdims=True) + EPS)
    normed = (c * scale * gain_ref[...]).astype(BF16)
    normed_ref[...] = normed
    expanded = matmul_tn(normed, w_ref[...]).astype(BF16)
    half = ROPE // 2
    a = latent_ref[KVL : KVL + half, :].astype(F32)
    b = latent_ref[KVL + half :, :].astype(F32)
    cos, sin = cos_ref[...], sin_ref[...]
    rope = jnp.concatenate(
        [a * cos - b * sin, a * sin + b * cos, jnp.zeros((QKP - QK, TOK), F32)], axis=0
    )
    rope = rope.T.astype(BF16)
    for h in range(2):
        key = h * (NOPE + VDIM)
        value = key + NOPE
        for m in range(MICRO):
            for core in range(2):
                rows = slice(m * BLK + core * HALF, m * BLK + (core + 1) * HALF)
                for chip in range(2):
                    at = 8 * h + 4 * m + 2 * chip + core
                    out_ref[at, :, :VDIM] = expanded[rows, value : value + VDIM]
                    out_ref[at, :, VDIM : VDIM + NOPE] = expanded[rows, key : key + NOPE]
                    out_ref[at, :, VDIM + NOPE :] = rope[rows, :]


def expand(latent_t, cos_t, sin_t, gain, w_expand):
    return pl.pallas_call(
        expand_kernel,
        out_shape=(
            jax.ShapeDtypeStruct((KVL, TOK), BF16),
            jax.ShapeDtypeStruct((ROWS, HALF, PACK), BF16),
        ),
        compiler_params=pltpu.CompilerParams(vmem_limit_bytes=60 * MIB),
        cost_estimate=pl.CostEstimate(flops=TOK * D * 256, bytes_accessed=MIB, transcendentals=0),
    )(latent_t, cos_t, sin_t, gain.reshape(KVL, 1), w_expand)


def latent_back_kernel(
    pack_ref, latent_ref, cos_ref, sin_ref, gain_ref, w_ref, d_exp_ref, d_latent_ref, gg_ref
):
    rope = [None] * (2 * MICRO)
    for h in range(2):
        for m in range(MICRO):
            for core in range(2):
                at = 8 * h + 4 * m + core
                part = pack_ref[at].astype(F32) + pack_ref[at + 2].astype(F32)
                rows = slice(m * BLK + core * HALF, m * BLK + (core + 1) * HALF)
                key = h * (NOPE + VDIM)
                d_exp_ref[rows, key : key + NOPE] = part[:, VDIM : VDIM + NOPE].astype(BF16)
                d_exp_ref[rows, key + NOPE : key + NOPE + VDIM] = part[:, :VDIM].astype(BF16)
                piece = part[:, VDIM + NOPE :]
                at = 2 * m + core
                rope[at] = piece if h == 0 else rope[at] + piece
    rope = jnp.concatenate(rope, axis=0).T
    half = ROPE // 2
    a, b = rope[:half], rope[half:ROPE]
    cos, sin = cos_ref[...], sin_ref[...]
    d_latent_ref[KVL : KVL + half, :] = (a * cos + b * sin).astype(BF16)
    d_latent_ref[KVL + half :, :] = (b * cos - a * sin).astype(BF16)
    d_normed = matmul_nt(w_ref[...], d_exp_ref[...])
    c = latent_ref[:KVL, :].astype(F32)
    scale = lax.rsqrt(jnp.mean(c * c, axis=0, keepdims=True) + EPS)
    gg_ref[...] = jnp.sum(d_normed * c * scale, axis=1, keepdims=True)
    weighted = d_normed * gain_ref[...]
    inner = jnp.mean(weighted * c, axis=0, keepdims=True)
    d_latent_ref[:KVL, :] = (scale * weighted - c * (scale * scale * scale) * inner).astype(BF16)


def latent_back(pack, latent_t, cos_t, sin_t, gain, w_expand):
    return pl.pallas_call(
        latent_back_kernel,
        out_shape=(
            jax.ShapeDtypeStruct((TOK, 2 * (NOPE + VDIM)), BF16),
            jax.ShapeDtypeStruct((LAT, TOK), BF16),
            jax.ShapeDtypeStruct((KVL, 1), F32),
        ),
        compiler_params=pltpu.CompilerParams(vmem_limit_bytes=60 * MIB),
        cost_estimate=pl.CostEstimate(flops=TOK * D * 256, bytes_accessed=MIB, transcendentals=0),
    )(pack, latent_t, cos_t, sin_t, gain.reshape(KVL, 1), w_expand)


def hidden_kernel(mid_ref, grad_ref, gate_ref, spread_ref, wg_ref, wu_ref, wd_ref, out_ref):
    mid = mid_ref[...]
    pre = matmul(mid, wg_ref[...])
    up = matmul(mid, wu_ref[...])
    back = matmul(grad_ref[...], wd_ref[...])
    gate = matmul(gate_ref[...], spread_ref[...])
    sig = 1.0 / (1.0 + jnp.exp(-pre))
    act = pre * sig
    back = back * gate
    out_ref[0] = (back * up * (sig * (1.0 + pre * (1.0 - sig)))).astype(BF16)
    out_ref[1] = (back * act).astype(BF16)
    out_ref[2] = (act * up * gate).astype(BF16)


def hidden(mid, grad, gates, spread, weights):
    whole = pl.BlockSpec((TOK, D), lambda j: (0, 0))
    parts = HID // BLK

    def weight(at):
        return pl.BlockSpec((D, BLK), lambda j: (0, at * parts + j))

    return pl.pallas_call(
        hidden_kernel,
        grid=(parts,),
        out_shape=jax.ShapeDtypeStruct((3, TOK, HID), BF16),
        in_specs=[
            whole,
            whole,
            pl.BlockSpec(gates.shape, lambda j: (0, 0)),
            pl.BlockSpec((spread.shape[0], BLK), lambda j: (0, j)),
            weight(0),
            weight(1),
            weight(2),
        ],
        out_specs=pl.BlockSpec((3, TOK, BLK), lambda j: (0, 0, j)),
        compiler_params=pltpu.CompilerParams(vmem_limit_bytes=60 * MIB),
        cost_estimate=pl.CostEstimate(
            flops=2 * TOK * D * HID * 3, bytes_accessed=32 * MIB, transcendentals=TOK * HID
        ),
    )(mid, grad, gates, spread, weights, weights, weights)


def mid_grad_kernel(hid_ref, w_ref, out_ref):
    out = matmul_nt(hid_ref[0], w_ref[:, :HID]) + matmul_nt(hid_ref[1], w_ref[:, HID:])
    out_ref[...] = out.astype(BF16)


def mid_grad(hid, weights):
    return pl.pallas_call(
        mid_grad_kernel,
        grid=(COLS,),
        out_shape=jax.ShapeDtypeStruct((TOK, D), BF16),
        in_specs=[
            pl.BlockSpec((2, TOK, HID), lambda j: (0, 0, 0)),
            pl.BlockSpec((FEAT, 2 * HID), lambda j: (j, 0)),
        ],
        out_specs=pl.BlockSpec((TOK, FEAT), lambda j: (0, j)),
        compiler_params=pltpu.CompilerParams(vmem_limit_bytes=60 * MIB),
        cost_estimate=pl.CostEstimate(
            flops=2 * TOK * D * HID * 2, bytes_accessed=20 * MIB, transcendentals=0
        ),
    )(hid, weights)


def output_kernel(col_ref, hid_ref, w_ref, residual_ref, out_ref):
    out_ref[0] = matmul_nt(hid_ref[0], w_ref[...]).astype(BF16)
    own = pl.ds(pl.multiple_of(col_ref[0] * OWN, OWN), OWN)
    out_ref[0, own, :] = (
        matmul_nt(hid_ref[0, own, :], w_ref[...]) + residual_ref[...]
    ).astype(BF16)


def output(col, hid, weights, residual):
    return pl.pallas_call(
        output_kernel,
        grid=(COLS,),
        out_shape=jax.ShapeDtypeStruct((COLS, TOK, FEAT), BF16),
        in_specs=[
            pl.BlockSpec(memory_space=pltpu.SMEM),
            pl.BlockSpec((1, TOK, HID), lambda j: (2, 0, 0)),
            pl.BlockSpec((FEAT, HID), lambda j: (j, 2)),
            pl.BlockSpec((OWN, FEAT), lambda j: (0, j)),
        ],
        out_specs=pl.BlockSpec((1, TOK, FEAT), lambda j: (j, 0, 0)),
        compiler_params=pltpu.CompilerParams(vmem_limit_bytes=60 * MIB),
        cost_estimate=pl.CostEstimate(
            flops=TOK * D * HID // 8, bytes_accessed=MIB, transcendentals=0
        ),
    )(col.astype(jnp.int32).reshape(1), hid, weights, residual)


def mid_kernel(parts_ref, inputs_ref, gain_ref, residual_ref, scale_ref, normed_ref):
    total = inputs_ref[...].astype(F32)
    for c in range(COLS):
        total = total + parts_ref[c].astype(F32)
    scale = inverse_rms(total)
    residual_ref[...] = total
    scale_ref[...] = scale
    normed = (total * scale * gain_ref[...]).astype(BF16)
    for c in range(COLS):
        normed_ref[c] = normed


def mid(parts, inputs, gain):
    return pl.pallas_call(
        mid_kernel,
        out_shape=(
            jax.ShapeDtypeStruct((OWN, D), F32),
            jax.ShapeDtypeStruct((OWN, 1), F32),
            jax.ShapeDtypeStruct((COLS, OWN, D), BF16),
        ),
        compiler_params=pltpu.CompilerParams(vmem_limit_bytes=60 * MIB),
        cost_estimate=pl.CostEstimate(
            flops=OWN * D * 16, bytes_accessed=5 * MIB, transcendentals=0
        ),
    )(parts, inputs, gain.reshape(1, D))


def mid_back_kernel(
    parts_ref, residual_ref, scale_ref, grad_ref, gain_ref, out_ref, low_ref, gain_grad_ref
):
    d_mid = parts_ref[0].astype(F32)
    for c in range(1, COLS):
        d_mid = d_mid + parts_ref[c].astype(F32)
    residual, scale = residual_ref[...], scale_ref[...]
    gain_grad_ref[...] = jnp.sum(d_mid * residual * scale, axis=0, keepdims=True)
    out = grad_ref[...].astype(F32) + norm_backward(d_mid, residual, scale, gain_ref[...])
    out_ref[...] = out
    low = out.astype(BF16)
    for c in range(COLS):
        low_ref[c] = low


def mid_back(parts, residual, scale, grad, gain):
    return pl.pallas_call(
        mid_back_kernel,
        out_shape=(
            jax.ShapeDtypeStruct((OWN, D), F32),
            jax.ShapeDtypeStruct((COLS, OWN, D), BF16),
            jax.ShapeDtypeStruct((1, D), F32),
        ),
        compiler_params=pltpu.CompilerParams(vmem_limit_bytes=60 * MIB),
        cost_estimate=pl.CostEstimate(
            flops=OWN * D * 24, bytes_accessed=5 * MIB, transcendentals=0
        ),
    )(parts, residual, scale, grad, gain.reshape(1, D))


def input_back_kernel(
    col_ref, dq_ref, dl_ref, wq_ref, wl_ref, x_ref, scale_ref, gain_ref, own_ref, out_ref, gg_ref
):
    step = pl.program_id(0)
    first = col_ref[1]
    d_in = matmul_nt(dq_ref[...], wq_ref[...]) + matmul_nt(dl_ref[...], wl_ref[...])
    x, scale = x_ref[...].astype(F32), scale_ref[...]
    gain_grad = jnp.sum(d_in * x * scale, axis=0, keepdims=True)

    @pl.when(step == 0)
    def _():
        gg_ref[...] = gain_grad

    @pl.when(step > 0)
    def _():
        gg_ref[...] += gain_grad

    out = norm_backward(d_in, x, scale, gain_ref[...])
    for half in range(2):
        mine = (col_ref[0] == first + 2 * step + half).astype(F32)
        rows = slice(half * OWN, (half + 1) * OWN)
        part = (out[rows] + mine * own_ref[...]).astype(BF16)
        for c in range(COLS):
            out_ref[c, rows, :] = part[:, c * FEAT : (c + 1) * FEAT]


def input_back(col, tree, d_query, d_latent, w_query, w_latent, inputs, scale, gain, own):
    rows = 2 * OWN
    steps = BLK // rows
    widths = (d_query.shape[1], d_latent.shape[1])
    return pl.pallas_call(
        input_back_kernel,
        grid=(steps,),
        out_shape=(
            jax.ShapeDtypeStruct((COLS, BLK, FEAT), BF16),
            jax.ShapeDtypeStruct((1, D), F32),
        ),
        in_specs=[
            pl.BlockSpec(memory_space=pltpu.SMEM),
            pl.BlockSpec((rows, widths[0]), lambda j: (steps * tree + j, 0)),
            pl.BlockSpec((rows, widths[1]), lambda j: (steps * tree + j, 0)),
            pl.BlockSpec((D, widths[0]), lambda j: (0, 0)),
            pl.BlockSpec((D, widths[1]), lambda j: (0, 0)),
            pl.BlockSpec((rows, D), lambda j: (steps * tree + j, 0)),
            pl.BlockSpec((rows, 1), lambda j: (steps * tree + j, 0)),
            pl.BlockSpec((1, D), lambda j: (0, 0)),
            pl.BlockSpec((OWN, D), lambda j: (0, 0)),
        ],
        out_specs=(
            pl.BlockSpec((COLS, rows, FEAT), lambda j: (0, j, 0)),
            pl.BlockSpec((1, D), lambda j: (0, 0)),
        ),
        compiler_params=pltpu.CompilerParams(vmem_limit_bytes=60 * MIB),
        cost_estimate=pl.CostEstimate(
            flops=2 * TOK * D * 640, bytes_accessed=9 * MIB, transcendentals=0
        ),
    )(
        jnp.stack([col.astype(jnp.int32), jnp.int32(tree * BLK // OWN)]),
        d_query,
        d_latent,
        w_query,
        w_latent,
        inputs,
        scale,
        gain.reshape(1, D),
        own,
    )


def weight_grad(mid_ref, grad_ref, hid_ref):
    lhs = jnp.where(pl.program_id(0) == 2, grad_ref[...], mid_ref[...])
    return matmul(lhs, hid_ref[0])


def send_grad_kernel(mid_ref, grad_ref, hid_ref, out_ref):
    out_ref[...] = weight_grad(mid_ref, grad_ref, hid_ref).astype(BF16)


def keep_grad_kernel(mid_ref, grad_ref, hid_ref, got_ref, o0, o1, o2, o3):
    out = weight_grad(mid_ref, grad_ref, hid_ref) + got_ref[...].astype(F32)
    for j, ref in enumerate((o0, o1, o2, o3)):
        ref[...] = out[j * LANES : (j + 1) * LANES].astype(BF16)


def send_grads(mid_t, grad_t, hid):
    width = HID // 2
    rows = D // 2
    whole = pl.BlockSpec((rows, TOK), lambda s, j: (1, 0))
    return pl.pallas_call(
        send_grad_kernel,
        grid=(3, 2),
        out_shape=jax.ShapeDtypeStruct((rows, WIDE), BF16),
        in_specs=[whole, whole, pl.BlockSpec((1, TOK, width), lambda s, j: (s, 0, j))],
        out_specs=pl.BlockSpec((rows, width), lambda s, j: (0, 2 * s + j)),
        compiler_params=pltpu.CompilerParams(vmem_limit_bytes=60 * MIB),
        cost_estimate=pl.CostEstimate(
            flops=TOK * D * HID // 32, bytes_accessed=MIB, transcendentals=0
        ),
    )(mid_t, grad_t, hid)


def keep_grads(z, mid_t, grad_t, hid, got):
    width = HID // 2
    rows = D // 4
    whole = pl.BlockSpec((rows, TOK), lambda s, j: (z, 0))
    block = pl.BlockSpec((LANES, width), lambda s, j: (0, 2 * s + j))
    return pl.pallas_call(
        keep_grad_kernel,
        grid=(3, 2),
        out_shape=[jax.ShapeDtypeStruct((LANES, WIDE), BF16)] * 4,
        in_specs=[
            whole,
            whole,
            pl.BlockSpec((1, TOK, width), lambda s, j: (s, 0, j)),
            pl.BlockSpec((rows, width), lambda s, j: (z, 2 * s + j)),
        ],
        out_specs=[block] * 4,
        compiler_params=pltpu.CompilerParams(vmem_limit_bytes=60 * MIB),
        cost_estimate=pl.CostEstimate(
            flops=TOK * D * HID // 32, bytes_accessed=MIB, transcendentals=0
        ),
    )(mid_t, grad_t, hid, got)


def pack_hidden(shared, routed):
    rows = shared.shape[0]
    return jnp.concatenate(
        [
            shared,
            jnp.swapaxes(routed, 0, 1).reshape(rows, EXPERTS * ROUTED),
            jnp.zeros((rows, HID - SHARED - EXPERTS * ROUTED), routed.dtype),
        ],
        axis=1,
    )


def local(
    tokens,
    out_grad,
    parents,
    routes,
    gates,
    norm_in,
    w_query,
    w_latent,
    norm_latent,
    w_expand,
    w_output,
    norm_mid,
    w_shared_gate,
    w_shared_up,
    w_shared_down,
    w_expert_gate,
    w_expert_up,
    w_expert_down,
):
    row = lax.axis_index("row")
    col = lax.axis_index("col")
    group = row // QUART
    own_start = col * OWN
    gain_in = norm_in.astype(F32)
    gain_latent = norm_latent.astype(F32)
    gain_mid = norm_mid.astype(F32)
    heads = 2

    query_pack = w_query.reshape(D // ROWS, heads, QK)
    attn_pack = jnp.concatenate(
        [
            query_pack[:, :, :NOPE].reshape(D // ROWS, heads * NOPE),
            query_pack[:, :, NOPE:].reshape(D // ROWS, heads * ROPE),
            w_expand.reshape(KVL // ROWS, 4, 128).transpose(1, 0, 2).reshape(D // ROWS, 128),
            w_latent,
            jnp.zeros((D // ROWS, 128 - LATC), BF16),
            w_output.T,
        ],
        axis=1,
    )
    ffn_pack = jnp.concatenate(
        [
            pack_hidden(w_shared_gate, w_expert_gate),
            pack_hidden(w_shared_up, w_expert_up),
            pack_hidden(w_shared_down.T, jnp.swapaxes(w_expert_down, 1, 2)),
        ],
        axis=1,
    )
    attn_pair, input_pair, ffn_pack = together(
        pair_up(attn_pack, "row"), pair_up(tokens.reshape(TOK, FEAT), "col"), ffn_pack
    )
    attn_ring = ring_up(attn_pair, "row")
    input_ring = ring_up(input_pair, "col")
    ffn_other = trade(ffn_pack, "row", 8)
    ffn_pack, attn_ring, input_ring = together(ffn_pack, attn_ring, input_ring)
    ffn_near = near_shards(ffn_pack)
    attn_full = finish_rows(attn_ring, row)
    query_full = attn_full[:, : heads * QK]
    expand_full = attn_full[:, 384:512].reshape(ROWS, 4, KVL // ROWS, 128)
    expand_full = expand_full.transpose(0, 2, 1, 3).reshape(KVL, heads * (NOPE + VDIM))
    latent_full = attn_full[:, 512:640]
    output_full = attn_full[:, 640:]

    seg = jnp.maximum(row - (TRUNK // BLK - 1), 0).astype(jnp.int32)
    depths = ancestor_depths(parents, seg.reshape(1))
    starts = jnp.where(seg > 0, TRUNK + BLK * depths, BLK * row)
    positions = (starts[:, None] + jnp.arange(BLK, dtype=jnp.int32)[None, :]).reshape(TOK)
    frequency = THETA ** (-jnp.arange(ROPE // 2, dtype=F32) / (ROPE // 2))
    angles = positions.astype(F32)[:, None] * frequency[None, :]
    cos_table, sin_table = jnp.cos(angles), jnp.sin(angles)

    cos_t, sin_t = cos_table.T, sin_table.T
    cos_wide, sin_wide = jnp.tile(cos_table, (1, 4)), jnp.tile(sin_table, (1, 4))

    inputs, normed_in, scale_in, latent_parts = front(col, input_ring, gain_in, latent_full)
    query = project_query(group, normed_in, query_full, cos_wide, sin_wide)
    latent_t, query, normed_in, ffn_near, ffn_other = together(
        swap(latent_parts, "col"), trade_quarter(query), normed_in, ffn_near, ffn_other
    )
    latent_t = latent_t.reshape(LAT, TOK)
    latent_normed_t, pack = expand(latent_t, cos_t, sin_t, gain_latent, expand_full)
    near, ffn_near = together(swap(pack, "row"), ffn_near)
    ffn_far = far_halves(ffn_near)
    grad_blocks = share(after(out_grad, near).reshape(TOK, FEAT), "col", COLS)
    far = trade(near, "row", 1)

    meta = jnp.concatenate([pick(parents, group % MICRO), smem_values(row % QUART, group)])
    *attended_own, lse = attend(meta, query, near, far)
    attended_own, lse, ffn_far = together(attended_own, lse, ffn_far)
    attended_parts, grad_blocks, ffn_far, ffn_other = together(
        trade_quarter(attended_own), grad_blocks, ffn_far, ffn_other
    )
    attended, attn_parts = project(group, attended_parts, output_full)
    grad_full, grad_t = features(row, grad_blocks)

    def both_cores(pieces):
        far_pieces = [(trade(v, "row", 1), apart ^ 1, first) for v, apart, first in pieces]
        return list(pieces) + far_pieces

    pieces = both_cores(
        [(ffn_pack, 0, 0), (ffn_near[0], 2, 0), (ffn_near[1], 6, 0)]
        + [(ffn_far[0], 4, 0), (ffn_far[1], 4, CUT)]
    )
    own_inputs = lax.dynamic_slice_in_dim(inputs, own_start, OWN, 0)
    attn_parts, grad_full, grad_t, other_near, values = together(
        swap(attn_parts, "col"),
        grad_full,
        grad_t,
        near_shards(ffn_other),
        [v for v, _, _ in pieces],
    )
    residual, scale_mid, normed_mid = mid(attn_parts, own_inputs, gain_mid)
    pieces = [(v, apart, first) for v, (_, apart, first) in zip(values, pieces)]
    ffn_full = put_shards(row, None, pieces)
    pieces = both_cores([(ffn_other, 8, 0), (other_near[0], 10, 0), (other_near[1], 14, 0)])
    ffn_full = put_shards(row, ffn_full, pieces)
    normed_mid, ffn_full, other_far = together(
        swap(normed_mid, "col"), ffn_full, far_halves(other_near)
    )
    normed_mid = normed_mid.reshape(TOK, D)
    pieces = both_cores([(other_far[0], 12, 0), (other_far[1], 12, CUT)])
    ffn_full = put_shards(row, ffn_full, pieces)

    named = routes.reshape(TOK, TOPK, 1) == jnp.arange(EXPERTS, dtype=jnp.int32)
    gate_of = jnp.sum(jnp.where(named, gates.reshape(TOK, TOPK, 1), 0.0), axis=1)
    gate_of = jnp.concatenate(
        [jnp.ones((TOK, 1), F32), gate_of, jnp.zeros((TOK, 15 - EXPERTS), F32)], axis=1
    )
    gate_high = gate_of.astype(BF16)
    gate_low = (gate_of - gate_high.astype(F32)).astype(BF16)
    unit = jnp.arange(HID, dtype=jnp.int32)
    expert = jnp.where(unit < SHARED, 0, 1 + (unit - SHARED) // ROUTED)
    spread = (expert[None, :] == jnp.arange(16, dtype=jnp.int32)[:, None]).astype(BF16)
    hid = hidden(
        normed_mid,
        grad_full,
        jnp.concatenate([gate_high, gate_low], axis=1),
        jnp.concatenate([spread, spread], axis=0),
        ffn_full,
    )
    normed_t = turn(row, after(normed_mid, hid))
    send = send_grads(normed_t, grad_t, hid)
    hid, send, normed_t = together(hid, send, normed_t)
    mid_parts = mid_grad(hid, ffn_full)
    hid, normed_t, mid_parts = together(hid, normed_t, mid_parts)
    got = trade(send, "row", 1)
    blocks = keep_grads(1, normed_t, grad_t, hid, got)
    own_blocks = keep_grads(0, normed_t, grad_t, after(hid, blocks), got)
    mid_parts, hid, blocks, halves, own_blocks = together(
        swap(mid_parts.reshape(COLS, OWN, D), "col"), hid, blocks, sum_opposite(blocks), own_blocks
    )
    own_grad = lax.dynamic_slice_in_dim(grad_full, own_start, OWN, 0)
    d_residual, d_low, mid_gain = mid_back(mid_parts, residual, scale_mid, own_grad, gain_mid)
    d_low, hid, sides = together(d_low, hid, with_opposite(blocks, halves))
    d_low, out_parts, sides = together(
        swap(d_low, "col"), output(col, hid, ffn_full, residual), sum_neighbours(sides)
    )
    other_sum = add_low(blocks[0].astype(F32) + sides[0].astype(F32), sides[1])

    d_attended = trade_quarter(project_back(group, d_low, output_full))
    out_parts = collect_y(out_parts, col // 2)
    d_attended, other_sum = together(d_attended, other_sum)
    *d_query, d_near, d_far = attend_back(
        meta, query, attended_own, d_attended, near, far, lse
    )
    d_query, d_near, d_far, halves, other_low, out_parts = together(
        d_query,
        d_near,
        d_far,
        sum_opposite(own_blocks),
        trade(other_sum[:, :CUT], "row", 8),
        out_parts,
    )
    d_far = trade(d_far, "row", 1)
    d_query, d_pack, out_parts = together(
        trade_quarter(d_query), add_low(d_near, d_far), out_parts
    )
    layer_out = collect_z(out_parts, col % 2).astype(BF16)
    d_pack, layer_out, sides = together(
        swap(d_pack, "row"), layer_out, with_opposite(own_blocks, halves)
    )
    sides = sum_neighbours(sides)

    d_expanded, d_latent, latent_gain = latent_back(
        d_pack, latent_t, cos_t, sin_t, gain_latent, expand_full
    )
    d_query = query_back(group, d_query, cos_wide, sin_wide)
    d_latent, d_query = together(swap(d_latent.reshape(COLS, LATC, TOK), "col"), d_query)
    d_latent = jnp.sum(d_latent.astype(F32), axis=0).astype(BF16)
    d_latent = jnp.concatenate([d_latent, jnp.zeros((128 - LATC, TOK), BF16)], axis=0).T

    d_tokens = []
    for tree in range(MICRO):
        part, gain_part = input_back(
            col,
            tree,
            d_query,
            d_latent,
            query_full,
            latent_full,
            inputs,
            scale_in,
            gain_in,
            d_residual,
        )
        in_gain = gain_part if tree == 0 else in_gain + gain_part
        d_tokens.append(part)
    attn_grads = attn_weight_grads(
        row, normed_in, d_query, d_latent, d_low.reshape(TOK, D), attended, latent_normed_t, d_expanded
    )
    first, second, in_gain, attn_grads, sides = together(
        swap(d_tokens[0], "col"), d_tokens[1], in_gain, attn_grads, sides
    )
    attn_grads = reduce_row(*attn_grads)
    gain = jnp.concatenate([in_gain.reshape(D), latent_gain.reshape(KVL), mid_gain.reshape(D)])
    second = swap(second, "col")
    gain = share(after(gain.astype(BF16).reshape(-1, 128), second), ("row", "col"), ROWS * COLS)
    gain = jnp.sum(gain.astype(F32), axis=0).reshape(-1)
    other_high = trade(after(other_sum, second)[:, CUT:], "row", 8)
    grad_query = jnp.concatenate(
        [
            attn_grads[:, : heads * NOPE].reshape(-1, heads, NOPE),
            attn_grads[:, heads * NOPE : heads * QK].reshape(-1, heads, ROPE),
        ],
        axis=-1,
    ).reshape(-1, heads * QK)
    grad_output = attn_grads[:, 384:640].T
    grad_expand = attn_grads[:, 640:768].reshape(4, KVL // ROWS, 128)
    grad_expand = grad_expand.transpose(1, 0, 2).reshape(KVL // ROWS, heads * (NOPE + VDIM))
    grad_latent = attn_grads[:, 768 : 768 + LATC]

    ffn_grads = own_blocks[0].astype(F32) + sides[0].astype(F32) + sides[1].astype(F32)
    other_sum = jnp.concatenate([other_low, other_high], axis=1)
    ffn_grads = ffn_grads + other_sum.astype(F32)

    def unpack(at):
        part = ffn_grads[:, at * HID : (at + 1) * HID]
        routed = part[:, SHARED : SHARED + EXPERTS * ROUTED]
        return part[:, :SHARED], routed.reshape(-1, EXPERTS, ROUTED)

    grad_shared_gate, grad_expert_gate = unpack(0)
    grad_shared_up, grad_expert_up = unpack(1)
    grad_shared_down, grad_expert_down = unpack(2)
    ffn_outs = (
        grad_shared_gate,
        grad_shared_up,
        grad_shared_down.T,
        jnp.swapaxes(grad_expert_gate, 0, 1),
        jnp.swapaxes(grad_expert_up, 0, 1),
        grad_expert_down.transpose(1, 2, 0),
    )
    input_grad = jnp.stack([first, second])
    input_grad = jnp.sum(input_grad.astype(F32), axis=1).astype(BF16)
    return (
        layer_out.reshape(MICRO, BLK, FEAT),
        input_grad,
        gain[:D],
        grad_query,
        grad_latent,
        gain[D : D + KVL],
        grad_expand,
        grad_output,
        gain[D + KVL :],
        *ffn_outs,
    )


def solution(mesh):
    in_specs = (
        P(None, "row", "col"),
        P(None, "row", "col"),
        P(),
        P(None, "row", None),
        P(None, "row", None),
        P(),
        P("row", "col"),
        P("row", "col"),
        P(),
        P("row", "col"),
        P("col", "row"),
        P(),
        P("row", "col"),
        P("row", "col"),
        P("col", "row"),
        P(None, "row", "col"),
        P(None, "row", "col"),
        P(None, "col", "row"),
    )
    out_specs = (
        P(None, "row", "col"),
        P(None, "row", "col"),
        P(),
        P("row", "col"),
        P("row", "col"),
        P(),
        P("row", "col"),
        P("col", "row"),
        P(),
        P("row", "col"),
        P("row", "col"),
        P("col", "row"),
        P(None, "row", "col"),
        P(None, "row", "col"),
        P(None, "col", "row"),
    )
    return jax.shard_map(local, mesh=mesh, in_specs=in_specs, out_specs=out_specs, check_vma=False)
```

```python
import functools

import jax
import jax.numpy as jnp
from jax import lax
from jax.experimental import pallas as pl
from jax.experimental.pallas import tpu as pltpu
from jax.sharding import PartitionSpec as P

D = 2048
NOPE = 128
ROPE = 64
QK = NOPE + ROPE
VDIM = 128
KVL = 512
TOPK = 6
EXPERTS = 8
MICRO = 2
TRUNK = 1024
BLK = 256
SEGS = 13
ROWS = 16
COLS = 8
TOK = MICRO * BLK
OWN = TOK // COLS
FEAT = D // COLS
QUART = 4
SHARED = 352
ROUTED = 176
HID = 1792
LAT = KVL + ROPE
HALF = BLK // 2
QKP = 256
PACK = VDIM + QKP
WIDE = 3 * HID
LANES = D // ROWS
CUT = LANES // 2
LATC = LAT // COLS
SCALE = QK**-0.5
EPS = 1e-06
THETA = 10000.0
NEG = -1e30
MIB = 1024 * 1024
F32 = jnp.float32
BF16 = jnp.bfloat16
NT = (((1,), (1,)), ((), ()))
TN = (((0,), (0,)), ((), ()))


def inverse_rms(values):
    return lax.rsqrt(jnp.mean(values * values, axis=-1, keepdims=True) + EPS)


def norm_backward(grad_out, values, inv_scale, norm_gain):
    weighted = grad_out * norm_gain
    inner = jnp.mean(weighted * values, axis=-1, keepdims=True)
    return inv_scale * weighted - values * (inv_scale * inv_scale * inv_scale) * inner


def matmul(a, b):
    return jnp.dot(a, b, preferred_element_type=F32)


def matmul_nt(a, b):
    return lax.dot_general(a, b, NT, preferred_element_type=F32)


def matmul_tn(a, b):
    return lax.dot_general(a, b, TN, preferred_element_type=F32)


def swap(values, axis, groups=None):
    return lax.all_to_all(values, axis, 0, 0, tiled=True, axis_index_groups=groups)


def share(values, axis, count):
    return swap(jnp.broadcast_to(values[None], (count,) + values.shape), axis)


def trade(values, axis, mask):
    count = ROWS if axis == "row" else COLS
    return lax.ppermute(values, axis, [(i, i ^ mask) for i in range(count)])


def after(values, *others):
    return lax.optimization_barrier((values,) + others)[0]


def together(*values):
    return lax.optimization_barrier(values)


def smem_values(*values):
    return jnp.stack([jnp.asarray(v, jnp.int32) for v in values])


def pick(values, index, axis=0):
    return lax.dynamic_index_in_dim(values, index, axis, keepdims=False)


def pair_up(shard, axis):
    return jnp.stack([shard, trade(shard, axis, 8 if axis == "row" else 1)])


def ring_up(pair, axis):
    return [pair] + [trade(pair, axis, j << 1) for j in (1, 2, 3)]


def sort_rows_kernel(own_ref, near_ref, far_ref, out_ref):
    for core, ref in ((0, near_ref), (1, far_ref)):
        for x in range(4):
            for z in range(2):
                out_ref[own_ref[0] ^ (8 * z + 2 * x + core)] = ref[x, z]


def finish_rows(ring, row):
    near = jnp.stack(ring)
    far = trade(near, "row", 1)
    vmem = pl.BlockSpec(memory_space=pltpu.VMEM)
    out = pl.pallas_call(
        sort_rows_kernel,
        out_shape=jax.ShapeDtypeStruct((ROWS,) + near.shape[2:], near.dtype),
        in_specs=[pl.BlockSpec(memory_space=pltpu.SMEM), vmem, vmem],
        out_specs=vmem,
        compiler_params=pltpu.CompilerParams(vmem_limit_bytes=16 * MIB),
        cost_estimate=pl.CostEstimate(flops=0, bytes_accessed=near.size, transcendentals=0),
    )(smem_values(row), near, far)
    return out.reshape(D, near.shape[3])


def place_of(apart):
    return ((apart & 1) << 3) | ((apart >> 3) << 2) | ((apart >> 1) & 3)


def lanes(at):
    return pl.ds(pl.multiple_of(at * LANES, LANES), LANES)


def features_kernel(own_ref, blocks_ref, out_ref, out_t_ref):
    for c in range(COLS):
        out_ref[:, c * FEAT : (c + 1) * FEAT] = blocks_ref[c]
    for r in range(ROWS):
        block = blocks_ref[r // 2, :, (r % 2) * LANES : (r % 2 + 1) * LANES]
        out_t_ref[lanes(place_of(own_ref[0] ^ r)), :] = block.T


def features(row, blocks):
    vmem = pl.BlockSpec(memory_space=pltpu.VMEM)
    return pl.pallas_call(
        features_kernel,
        out_shape=(
            jax.ShapeDtypeStruct((TOK, D), BF16),
            jax.ShapeDtypeStruct((D, TOK), BF16),
        ),
        in_specs=[pl.BlockSpec(memory_space=pltpu.SMEM), vmem],
        out_specs=(vmem, vmem),
        compiler_params=pltpu.CompilerParams(vmem_limit_bytes=60 * MIB),
        cost_estimate=pl.CostEstimate(flops=0, bytes_accessed=MIB, transcendentals=0),
    )(smem_values(row), blocks)


def near_shards(shard):
    return trade(shard, "row", 2), trade(shard, "row", 6)


def cut_near(near):
    return near[1][:CUT], near[0][CUT:]


def far_halves(parts):
    return trade(parts[0], "row", 2), trade(parts[1], "row", 6)


def put_kernel(places, own_ref, *refs):
    out_ref, sems = refs[-2:]
    copies = []
    for i, (apart, first) in enumerate(places):
        at = (own_ref[0] ^ apart) * LANES + first
        rows = pl.ds(pl.multiple_of(at, CUT), refs[i].shape[0])
        copy = pltpu.make_async_copy(refs[i], out_ref.at[rows], sems.at[i])
        copy.start()
        copies.append(copy)
    for copy in copies:
        copy.wait()


def put_shards(row, whole, pieces):
    values = [piece for piece, _, _ in pieces]
    places = [(apart, first) for _, apart, first in pieces]
    fresh = whole is None
    return pl.pallas_call(
        functools.partial(put_kernel, places),
        out_shape=jax.ShapeDtypeStruct((D, WIDE), BF16),
        in_specs=[pl.BlockSpec(memory_space=pltpu.SMEM)]
        + [pl.BlockSpec(memory_space=pltpu.VMEM)] * len(values)
        + ([] if fresh else [pl.BlockSpec(memory_space=pl.ANY)]),
        out_specs=pl.BlockSpec(memory_space=pl.ANY),
        scratch_shapes=[pltpu.SemaphoreType.DMA((len(values),))],
        input_output_aliases={} if fresh else {1 + len(values): 0},
        compiler_params=pltpu.CompilerParams(vmem_limit_bytes=60 * MIB),
        cost_estimate=pl.CostEstimate(flops=0, bytes_accessed=MIB, transcendentals=0),
    )(smem_values(row), *values, *([] if fresh else [whole]))


def sum_opposite(blocks):
    return trade(blocks[2], "row", 2), trade(blocks[3], "row", 6)


def add_low(a, b):
    return (a.astype(F32) + b.astype(F32)).astype(BF16)


def sides_kernel(b1_ref, b3_ref, h1_ref, h3_ref, left_ref, right_ref):
    left_ref[:CUT] = b1_ref[:CUT]
    left_ref[CUT:] = (b1_ref[CUT:].astype(F32) + h3_ref[...].astype(F32)).astype(BF16)
    right_ref[:CUT] = (b3_ref[:CUT].astype(F32) + h1_ref[...].astype(F32)).astype(BF16)
    right_ref[CUT:] = b3_ref[CUT:]


def with_opposite(blocks, halves):
    return pl.pallas_call(
        sides_kernel,
        out_shape=[jax.ShapeDtypeStruct((LANES, WIDE), BF16)] * 2,
        compiler_params=pltpu.CompilerParams(vmem_limit_bytes=60 * MIB),
        cost_estimate=pl.CostEstimate(flops=0, bytes_accessed=MIB, transcendentals=0),
    )(blocks[1], blocks[4], *halves)


def sum_neighbours(sides):
    return trade(sides[0], "row", 2), trade(sides[1], "row", 6)


def reduce_x(blocks, j):
    blocks = blocks.reshape((4, 2) + blocks.shape[1:])
    return trade(blocks[j], "row", j << 1) if j else blocks[0]


def reduce_z(*packs):
    sums = []
    for parts in packs:
        parts = [part.astype(F32) for part in parts]
        sums.append(parts[0] + parts[1] + (parts[2] + parts[3]))
    blocks = jnp.concatenate(sums, axis=-1).astype(BF16)
    return blocks[0].astype(F32) + trade(blocks[1], "row", 8).astype(F32)


def attn_grads_kernel(own_ref, x_ref, dq_ref, low_ref, att_ref, keep_ref, send_ref, out):
    out[:, :384] = matmul_tn(x_ref[...], dq_ref[...])
    out[:, 384:] = matmul_tn(low_ref[...], att_ref[...])
    core = own_ref[0] & 1
    keep_ref[0] = out[lanes(core), :].astype(BF16)
    send_ref[0] = out[lanes(1 - core), :].astype(BF16)


def latent_grads_kernel(own_ref, x_ref, dl_ref, lat_ref, de_ref, keep_ref, send_ref, out):
    out[:, 128:] = matmul_tn(x_ref[...], dl_ref[...])
    expand_grad = matmul(lat_ref[...], de_ref[...])
    for half in range(2):
        for i in range(4):
            rows = slice(half * LANES + 32 * i, half * LANES + 32 * (i + 1))
            part = expand_grad[32 * half : 32 * (half + 1), 128 * i : 128 * (i + 1)]
            out[rows, :128] = part
    core = own_ref[0] & 1
    keep_ref[0] = out[lanes(core), :].astype(BF16)
    send_ref[0] = out[lanes(1 - core), :].astype(BF16)


def place_pair(i, own):
    apart = i ^ (own[0] >> 1)
    return (apart & 3) * 2 + (apart >> 2), 0, 0


def weight_grad_pairs(kernel, width, row, ins, specs):
    block = pl.BlockSpec((1, LANES, width), place_pair)
    return pl.pallas_call(
        kernel,
        out_shape=[jax.ShapeDtypeStruct((ROWS // 2, LANES, width), BF16)] * 2,
        grid_spec=pltpu.PrefetchScalarGridSpec(
            num_scalar_prefetch=1,
            grid=(ROWS // 2,),
            in_specs=specs,
            out_specs=[block, block],
            scratch_shapes=[pltpu.VMEM((2 * LANES, width), F32)],
        ),
        compiler_params=pltpu.CompilerParams(vmem_limit_bytes=60 * MIB),
        cost_estimate=pl.CostEstimate(flops=TOK * D * 16, bytes_accessed=MIB, transcendentals=0),
    )(smem_values(row), *ins)


def whole_block(values):
    return pl.BlockSpec(values.shape, lambda i, own: (0, 0))


def attn_weight_grads(row, normed, d_query, d_low, attended):
    columns = pl.BlockSpec((TOK, 2 * LANES), lambda i, own: (0, i))
    specs = [columns, whole_block(d_query), columns, whole_block(attended)]
    ins = (normed, d_query, d_low, attended)
    return weight_grad_pairs(attn_grads_kernel, 640, row, ins, specs)


def latent_weight_grads(row, normed, d_latent, latent_t, d_expanded):
    columns = pl.BlockSpec((TOK, 2 * LANES), lambda i, own: (0, i))
    lines = pl.BlockSpec((2 * KVL // ROWS, TOK), lambda i, own: (i, 0))
    specs = [columns, whole_block(d_latent), lines, whole_block(d_expanded)]
    ins = (normed, d_latent, latent_t, d_expanded)
    return weight_grad_pairs(latent_grads_kernel, 256, row, ins, specs)


def collect_y(blocks, y, j):
    blocks = blocks.reshape((4, 2) + blocks.shape[1:])
    return trade(pick(blocks, y ^ j), "col", j << 1) if j else pick(blocks, y)


def collect_z(blocks, z):
    blocks = [block.astype(F32) for block in blocks]
    blocks = (blocks[0] + blocks[1] + (blocks[2] + blocks[3])).astype(BF16)
    got = trade(pick(blocks, 1 - z), "col", 1)
    return pick(blocks, z).astype(F32) + got.astype(F32)


def trade_quarter(blocks):
    return [blocks[0]] + [trade(blocks[j], "row", j << 2) for j in (1, 2, 3)]


def depth_kernel(parents_ref, seg_ref, out_ref):
    seg = seg_ref[0]
    for m in range(MICRO):

        def climb(step, state):
            at, count = state
            return parents_ref[m, at], count + (at > 0).astype(jnp.int32)

        _, count = lax.fori_loop(0, SEGS, climb, (parents_ref[m, seg], jnp.int32(0)))
        out_ref[m] = count


def ancestor_depths(parents, seg):
    smem = pl.BlockSpec(memory_space=pltpu.SMEM)
    return pl.pallas_call(
        depth_kernel,
        out_shape=jax.ShapeDtypeStruct((MICRO,), jnp.int32),
        in_specs=[smem, smem],
        out_specs=smem,
    )(parents, seg)


def list_ancestors(meta, qb, listed):
    def climb(step, state):
        at, count = state
        listed[count] = at + 3
        return meta[at], count + (at > 0).astype(jnp.int32)

    _, count = lax.fori_loop(0, SEGS, climb, (meta[qb - 3], jnp.int32(0)))
    return count


def causal_mask():
    key = lax.broadcasted_iota(jnp.int32, (BLK, BLK), 0)
    query = lax.broadcasted_iota(jnp.int32, (BLK, BLK), 1)
    return key <= query


def join_halves(meta, near_ref, far_ref, pack):
    core = meta[SEGS] % 2
    pack[:, pl.ds(pl.multiple_of(core * HALF, HALF), HALF), :] = near_ref[...]
    pack[:, pl.ds(pl.multiple_of((1 - core) * HALF, HALF), HALF), :] = far_ref[...]


def attend_kernel(meta, q0, q1, q2, q3, near_ref, far_ref, o0, o1, o2, o3, lse_ref, *scratch):
    q_ref, o_ref, pack, listed = scratch
    quarter, own = meta[SEGS], meta[SEGS + 1]
    join_halves(meta, near_ref, far_ref, pack)
    for j, ref in enumerate((q0, q1, q2, q3)):
        q_ref[own ^ j] = ref[...]
    for i in range(QUART):
        qb = QUART * i + quarter
        q = q_ref[i]
        s = matmul_nt(pack[qb, :, VDIM:], q) * SCALE
        s = jnp.where(causal_mask(), s, NEG)
        top = jnp.max(s, axis=0, keepdims=True)
        p = jnp.exp(s - top)
        total = jnp.sum(p, axis=0, keepdims=True)
        out = matmul_tn(pack[qb, :, :VDIM], p.astype(BF16))

        def step(kb, state):
            top, total, out = state
            s = matmul_nt(pack[kb, :, VDIM:], q) * SCALE
            new_top = jnp.maximum(top, jnp.max(s, axis=0, keepdims=True))
            shrink = jnp.exp(top - new_top)
            p = jnp.exp(s - new_top)
            total = total * shrink + jnp.sum(p, axis=0, keepdims=True)
            out = out * shrink + matmul_tn(pack[kb, :, :VDIM], p.astype(BF16))
            return new_top, total, out

        state = (top, total, out)
        if i == 0:
            state = lax.fori_loop(0, quarter, step, state)
        else:
            for kb in range(TRUNK // BLK):
                state = step(kb, state)
            count = list_ancestors(meta, qb, listed)
            state = lax.fori_loop(0, count, lambda t, c: step(listed[t], c), state)
        top, total, out = state
        o_ref[i] = (out * (1.0 / total)).T.astype(BF16)
        lse_ref[i] = top + jnp.log(total)
    for j, ref in enumerate((o0, o1, o2, o3)):
        ref[...] = o_ref[own ^ j]


def attend(meta, q, near, far):
    smem = pl.BlockSpec(memory_space=pltpu.SMEM)
    vmem = pl.BlockSpec(memory_space=pltpu.VMEM)
    pairs = 32 * BLK * BLK
    return pl.pallas_call(
        attend_kernel,
        out_shape=[jax.ShapeDtypeStruct((BLK, VDIM), BF16)] * QUART
        + [jax.ShapeDtypeStruct((QUART, 1, BLK), F32)],
        in_specs=[smem] + [vmem] * 6,
        out_specs=[vmem] * 5,
        scratch_shapes=[
            pltpu.VMEM((QUART, BLK, QKP), BF16),
            pltpu.VMEM((QUART, BLK, VDIM), BF16),
            pltpu.VMEM((ROWS, BLK, PACK), BF16),
            pltpu.SMEM((16,), jnp.int32),
        ],
        compiler_params=pltpu.CompilerParams(vmem_limit_bytes=60 * MIB),
        cost_estimate=pl.CostEstimate(
            flops=pairs * 2 * (QK + VDIM), bytes_accessed=4 * MIB, transcendentals=pairs
        ),
    )(meta, *q, near, far)


def attend_back_kernel(meta, *refs):
    ins, outs, scratch = refs[:15], refs[15:21], refs[21:]
    near_ref, far_ref, lse_ref = ins[12:]
    keep_ref, send_ref = outs[4:]
    q_ref, o_ref, do_ref, dq_ref, pack, dk, dv, listed = scratch
    quarter, own = meta[SEGS], meta[SEGS + 1]
    core = quarter % 2
    join_halves(meta, near_ref, far_ref, pack)
    for j in range(QUART):
        q_ref[own ^ j] = ins[j][...]
        o_ref[own ^ j] = ins[QUART + j][...]
        do_ref[own ^ j] = ins[2 * QUART + j][...]
    dk[...] = jnp.zeros_like(dk)
    dv[...] = jnp.zeros_like(dv)
    for i in range(QUART):
        qb = QUART * i + quarter
        q = q_ref[i]
        do = do_ref[i]
        lse = lse_ref[i]
        pairs = do.astype(F32) * o_ref[i].astype(F32)
        delta = jnp.sum(pairs.T, axis=0, keepdims=True)

        def step(kb, dqt, masked=False):
            key = pack[kb, :, VDIM:]
            s = matmul_nt(key, q) * SCALE
            p = jnp.exp(s - lse)
            if masked:
                p = jnp.where(causal_mask(), p, 0.0)
            dp = matmul_nt(pack[kb, :, :VDIM], do)
            ds = (p * (dp - delta) * SCALE).astype(BF16)
            dv[kb] += matmul(p.astype(BF16), do)
            dk[kb] += matmul(ds, q)
            return dqt + matmul_tn(key, ds)

        dqt = step(qb, jnp.zeros((QKP, BLK), F32), True)
        if i == 0:
            dqt = lax.fori_loop(0, quarter, step, dqt)
        else:
            for kb in range(TRUNK // BLK):
                dqt = step(kb, dqt)
            count = list_ancestors(meta, qb, listed)
            dqt = lax.fori_loop(0, count, lambda t, c: step(listed[t], c), dqt)
        dq_ref[i] = dqt.T.astype(BF16)
    for j in range(QUART):
        outs[j][...] = dq_ref[own ^ j]
    for half, ref in ((core, keep_ref), (1 - core, send_ref)):
        part = pl.ds(pl.multiple_of(half * HALF, HALF), HALF)
        ref[:, :, :VDIM] = dv[:, part, :].astype(BF16)
        ref[:, :, VDIM:] = dk[:, part, :].astype(BF16)


def attend_back(meta, q, o, d_o, near, far, lse):
    smem = pl.BlockSpec(memory_space=pltpu.SMEM)
    vmem = pl.BlockSpec(memory_space=pltpu.VMEM)
    pairs = 32 * BLK * BLK
    return pl.pallas_call(
        attend_back_kernel,
        out_shape=[jax.ShapeDtypeStruct((BLK, QKP), BF16)] * QUART
        + [jax.ShapeDtypeStruct((ROWS, HALF, PACK), BF16)] * 2,
        in_specs=[smem] + [vmem] * 15,
        out_specs=[vmem] * 6,
        scratch_shapes=[
            pltpu.VMEM((QUART, BLK, QKP), BF16),
            pltpu.VMEM((QUART, BLK, VDIM), BF16),
            pltpu.VMEM((QUART, BLK, VDIM), BF16),
            pltpu.VMEM((QUART, BLK, QKP), BF16),
            pltpu.VMEM((ROWS, BLK, PACK), BF16),
            pltpu.VMEM((ROWS, BLK, QKP), F32),
            pltpu.VMEM((ROWS, BLK, VDIM), F32),
            pltpu.SMEM((16,), jnp.int32),
        ],
        compiler_params=pltpu.CompilerParams(vmem_limit_bytes=60 * MIB),
        cost_estimate=pl.CostEstimate(
            flops=pairs * 2 * (3 * QK + 2 * VDIM), bytes_accessed=10 * MIB, transcendentals=pairs
        ),
    )(meta, *q, *o, *d_o, near, far, lse)


def project_kernel(own_ref, b0, b1, b2, b3, w_ref, attended_ref, out_ref, blocks):
    for j, ref in enumerate((b0, b1, b2, b3)):
        blocks[own_ref[0] ^ j] = ref[...]
    for h in range(2):
        for m in range(MICRO):
            attended_ref[m * BLK : (m + 1) * BLK, h * VDIM : (h + 1) * VDIM] = blocks[2 * h + m]
    out = matmul_nt(attended_ref[...], w_ref[...]).astype(BF16)
    for c in range(COLS):
        out_ref[c] = out[c * OWN : (c + 1) * OWN]


def project(own, blocks, w_packed):
    def whole(*shape):
        return pl.BlockSpec(shape, lambda i: (0,) * len(shape))

    return pl.pallas_call(
        project_kernel,
        grid=(1,),
        out_shape=(
            jax.ShapeDtypeStruct((TOK, 2 * VDIM), BF16),
            jax.ShapeDtypeStruct((COLS, OWN, D), BF16),
        ),
        in_specs=[pl.BlockSpec(memory_space=pltpu.SMEM)]
        + [whole(BLK, VDIM)] * QUART
        + [pl.BlockSpec((D, 2 * VDIM), lambda i: (0, 2))],
        out_specs=(whole(TOK, 2 * VDIM), whole(COLS, OWN, D)),
        scratch_shapes=[pltpu.VMEM((QUART, BLK, VDIM), BF16)],
        compiler_params=pltpu.CompilerParams(vmem_limit_bytes=60 * MIB),
        cost_estimate=pl.CostEstimate(flops=TOK * D * 512, bytes_accessed=MIB, transcendentals=0),
    )(smem_values(own), *blocks, w_packed)


def project_back_kernel(own_ref, d_ref, w_ref, o0, o1, o2, o3, blocks):
    for c in range(COLS):
        rows = slice((c % QUART) * OWN, (c % QUART + 1) * OWN)
        part = matmul(d_ref[c], w_ref[...]).astype(BF16)
        for h in range(2):
            blocks[2 * h + c // QUART, rows, :] = part[:, h * VDIM : (h + 1) * VDIM]
    for j, ref in enumerate((o0, o1, o2, o3)):
        ref[...] = blocks[own_ref[0] ^ j]


def project_back(own, d_low, w_packed):
    def whole(*shape):
        return pl.BlockSpec(shape, lambda i: (0,) * len(shape))

    return pl.pallas_call(
        project_back_kernel,
        grid=(1,),
        out_shape=[jax.ShapeDtypeStruct((BLK, VDIM), BF16)] * QUART,
        in_specs=[
            pl.BlockSpec(memory_space=pltpu.SMEM),
            whole(COLS, OWN, D),
            pl.BlockSpec((D, 2 * VDIM), lambda i: (0, 2)),
        ],
        out_specs=[whole(BLK, VDIM)] * QUART,
        scratch_shapes=[pltpu.VMEM((QUART, BLK, VDIM), BF16)],
        compiler_params=pltpu.CompilerParams(vmem_limit_bytes=60 * MIB),
        cost_estimate=pl.CostEstimate(flops=TOK * D * 512, bytes_accessed=MIB, transcendentals=0),
    )(smem_values(own), d_low, w_packed)


def front_kernel(col_ref, pieces_ref, gain_ref, wl_ref, x_ref, normed_ref, scale_ref, lat_ref):
    for y in range(4):
        for z in range(2):
            at = (2 * y + (z ^ (col_ref[0] & 1))) * FEAT
            x_ref[:, pl.ds(pl.multiple_of(at, FEAT), FEAT)] = pieces_ref[y, z]
    x = x_ref[...].astype(F32)
    scale = inverse_rms(x)
    scale_ref[...] = scale
    normed = (x * scale * gain_ref[...]).astype(BF16)
    normed_ref[...] = normed
    latent = matmul(normed, wl_ref[...]).T[:LATC].astype(BF16)
    for c in range(COLS):
        lat_ref[c] = latent


def front(col, pieces, gain, w_packed):
    rows = 128
    return pl.pallas_call(
        front_kernel,
        grid=(TOK // rows,),
        out_shape=(
            jax.ShapeDtypeStruct((TOK, D), BF16),
            jax.ShapeDtypeStruct((TOK, D), BF16),
            jax.ShapeDtypeStruct((TOK, 1), F32),
            jax.ShapeDtypeStruct((COLS, LATC, TOK), BF16),
        ),
        in_specs=[
            pl.BlockSpec(memory_space=pltpu.SMEM),
            pl.BlockSpec((4, 2, rows, FEAT), lambda j: (0, 0, j, 0)),
            pl.BlockSpec((1, D), lambda j: (0, 0)),
            pl.BlockSpec((D, 128), lambda j: (0, 6)),
        ],
        out_specs=(
            pl.BlockSpec((rows, D), lambda j: (j, 0)),
            pl.BlockSpec((rows, D), lambda j: (j, 0)),
            pl.BlockSpec((rows, 1), lambda j: (j, 0)),
            pl.BlockSpec((COLS, LATC, rows), lambda j: (0, 0, j)),
        ),
        compiler_params=pltpu.CompilerParams(vmem_limit_bytes=60 * MIB),
        cost_estimate=pl.CostEstimate(flops=TOK * D * 256, bytes_accessed=MIB, transcendentals=0),
    )(smem_values(col), pieces, gain.reshape(1, D), w_packed)


def half_turn():
    source = lax.broadcasted_iota(jnp.int32, (2 * ROPE, 2 * ROPE), 0)
    target = lax.broadcasted_iota(jnp.int32, (2 * ROPE, 2 * ROPE), 1)
    half = ROPE // 2
    first = target % ROPE < half
    value = jnp.where(
        first & (source == target + half),
        -1.0,
        jnp.where((target % ROPE >= half) & (source == target - half), 1.0, 0.0),
    )
    return value.astype(BF16)


def query_kernel(own_ref, normed_ref, w_ref, cos_ref, sin_ref, o0, o1, o2, o3, blocks):
    normed = normed_ref[...]
    w_rope = w_ref[:, 2 * NOPE :]
    turned = matmul(w_rope, half_turn()).astype(BF16)
    rope = matmul(normed, w_rope) * cos_ref[...] + matmul(normed, turned) * sin_ref[...]
    rope = rope.astype(BF16)
    nope = matmul(normed, w_ref[:, : 2 * NOPE]).astype(BF16)
    blank = jnp.zeros((BLK, QKP - QK), BF16)
    for h in range(2):
        for m in range(MICRO):
            rows = slice(m * BLK, (m + 1) * BLK)
            blocks[2 * h + m, :, :NOPE] = nope[rows, h * NOPE : (h + 1) * NOPE]
            blocks[2 * h + m, :, NOPE:QK] = rope[rows, h * ROPE : (h + 1) * ROPE]
            blocks[2 * h + m, :, QK:] = blank
    for j, ref in enumerate((o0, o1, o2, o3)):
        ref[...] = blocks[own_ref[0] ^ j]


def project_query(own, normed, w_packed, cos_wide, sin_wide):
    def whole(shape):
        return pl.BlockSpec(shape, lambda i: (0, 0))

    return pl.pallas_call(
        query_kernel,
        grid=(1,),
        out_shape=[jax.ShapeDtypeStruct((BLK, QKP), BF16)] * QUART,
        in_specs=[
            pl.BlockSpec(memory_space=pltpu.SMEM),
            whole((TOK, D)),
            whole((D, 2 * QK)),
            whole((TOK, 2 * ROPE)),
            whole((TOK, 2 * ROPE)),
        ],
        out_specs=[whole((BLK, QKP))] * QUART,
        scratch_shapes=[pltpu.VMEM((QUART, BLK, QKP), BF16)],
        compiler_params=pltpu.CompilerParams(vmem_limit_bytes=60 * MIB),
        cost_estimate=pl.CostEstimate(flops=TOK * D * 256, bytes_accessed=MIB, transcendentals=0),
    )(smem_values(own), normed, w_packed, cos_wide, sin_wide)


def query_back_kernel(own_ref, b0, b1, b2, b3, cos_ref, sin_ref, out_ref, blocks):
    turn = half_turn()
    for j, ref in enumerate((b0, b1, b2, b3)):
        blocks[own_ref[0] ^ j] = ref[...]
    for m in range(MICRO):
        rows = slice(m * BLK, (m + 1) * BLK)
        for h in range(2):
            out_ref[rows, h * NOPE : (h + 1) * NOPE] = blocks[2 * h + m, :, :NOPE]
        rope = jnp.concatenate([blocks[m, :, NOPE:QK], blocks[2 + m, :, NOPE:QK]], axis=1)
        rope = rope.astype(F32) * cos_ref[rows, :] + matmul_nt(rope, turn) * sin_ref[rows, :]
        out_ref[rows, 2 * NOPE :] = rope.astype(BF16)


def query_back(own, blocks, cos_wide, sin_wide):
    vmem = pl.BlockSpec(memory_space=pltpu.VMEM)
    return pl.pallas_call(
        query_back_kernel,
        out_shape=jax.ShapeDtypeStruct((TOK, 2 * QK), BF16),
        in_specs=[pl.BlockSpec(memory_space=pltpu.SMEM)] + [vmem] * 6,
        out_specs=vmem,
        scratch_shapes=[pltpu.VMEM((QUART, BLK, QKP), BF16)],
        compiler_params=pltpu.CompilerParams(vmem_limit_bytes=60 * MIB),
        cost_estimate=pl.CostEstimate(flops=TOK * D * 16, bytes_accessed=MIB, transcendentals=0),
    )(smem_values(own), *blocks, cos_wide, sin_wide)


def expand_kernel(latent_ref, cos_ref, sin_ref, gain_ref, w_ref, normed_ref, out_ref):
    c = latent_ref[:KVL, :].astype(F32)
    scale = lax.rsqrt(jnp.mean(c * c, axis=0, keepdims=True) + EPS)
    normed = (c * scale * gain_ref[...]).astype(BF16)
    normed_ref[...] = normed
    expanded = matmul_tn(normed, w_ref[...]).astype(BF16)
    half = ROPE // 2
    a = latent_ref[KVL : KVL + half, :].astype(F32)
    b = latent_ref[KVL + half :, :].astype(F32)
    cos, sin = cos_ref[...], sin_ref[...]
    rope = jnp.concatenate(
        [a * cos - b * sin, a * sin + b * cos, jnp.zeros((QKP - QK, TOK), F32)], axis=0
    )
    rope = rope.T.astype(BF16)
    for h in range(2):
        key = h * (NOPE + VDIM)
        value = key + NOPE
        for m in range(MICRO):
            for core in range(2):
                rows = slice(m * BLK + core * HALF, m * BLK + (core + 1) * HALF)
                for chip in range(2):
                    at = 8 * h + 4 * m + 2 * chip + core
                    out_ref[at, :, :VDIM] = expanded[rows, value : value + VDIM]
                    out_ref[at, :, VDIM : VDIM + NOPE] = expanded[rows, key : key + NOPE]
                    out_ref[at, :, VDIM + NOPE :] = rope[rows, :]


def expand(latent_t, cos_t, sin_t, gain, w_expand):
    return pl.pallas_call(
        expand_kernel,
        out_shape=(
            jax.ShapeDtypeStruct((KVL, TOK), BF16),
            jax.ShapeDtypeStruct((ROWS, HALF, PACK), BF16),
        ),
        compiler_params=pltpu.CompilerParams(vmem_limit_bytes=60 * MIB),
        cost_estimate=pl.CostEstimate(flops=TOK * D * 256, bytes_accessed=MIB, transcendentals=0),
    )(latent_t, cos_t, sin_t, gain.reshape(KVL, 1), w_expand)


def latent_back_kernel(
    pack_ref, latent_ref, cos_ref, sin_ref, gain_ref, w_ref, d_exp_ref, d_latent_ref, gg_ref
):
    rope = [None] * (2 * MICRO)
    for h in range(2):
        for m in range(MICRO):
            for core in range(2):
                at = 8 * h + 4 * m + core
                part = pack_ref[at].astype(F32) + pack_ref[at + 2].astype(F32)
                rows = slice(m * BLK + core * HALF, m * BLK + (core + 1) * HALF)
                key = h * (NOPE + VDIM)
                d_exp_ref[rows, key : key + NOPE] = part[:, VDIM : VDIM + NOPE].astype(BF16)
                d_exp_ref[rows, key + NOPE : key + NOPE + VDIM] = part[:, :VDIM].astype(BF16)
                piece = part[:, VDIM + NOPE :]
                at = 2 * m + core
                rope[at] = piece if h == 0 else rope[at] + piece
    rope = jnp.concatenate(rope, axis=0).T
    half = ROPE // 2
    a, b = rope[:half], rope[half:ROPE]
    cos, sin = cos_ref[...], sin_ref[...]
    d_latent_ref[KVL : KVL + half, :] = (a * cos + b * sin).astype(BF16)
    d_latent_ref[KVL + half :, :] = (b * cos - a * sin).astype(BF16)
    d_normed = matmul_nt(w_ref[...], d_exp_ref[...])
    c = latent_ref[:KVL, :].astype(F32)
    scale = lax.rsqrt(jnp.mean(c * c, axis=0, keepdims=True) + EPS)
    gg_ref[...] = jnp.sum(d_normed * c * scale, axis=1, keepdims=True)
    weighted = d_normed * gain_ref[...]
    inner = jnp.mean(weighted * c, axis=0, keepdims=True)
    d_latent_ref[:KVL, :] = (scale * weighted - c * (scale * scale * scale) * inner).astype(BF16)


def latent_back(pack, latent_t, cos_t, sin_t, gain, w_expand):
    return pl.pallas_call(
        latent_back_kernel,
        out_shape=(
            jax.ShapeDtypeStruct((TOK, 2 * (NOPE + VDIM)), BF16),
            jax.ShapeDtypeStruct((LAT, TOK), BF16),
            jax.ShapeDtypeStruct((KVL, 1), F32),
        ),
        compiler_params=pltpu.CompilerParams(vmem_limit_bytes=60 * MIB),
        cost_estimate=pl.CostEstimate(flops=TOK * D * 256, bytes_accessed=MIB, transcendentals=0),
    )(pack, latent_t, cos_t, sin_t, gain.reshape(KVL, 1), w_expand)


def hidden_kernel(
    own_ref, mid_ref, grad_ref, gate_ref, spread_ref, wg_ref, wu_ref, wd_ref, out_ref, turned_ref
):
    mid = mid_ref[...]
    pre = matmul(mid, wg_ref[...])
    up = matmul(mid, wu_ref[...])
    back = matmul(grad_ref[...], wd_ref[...])
    gate = matmul(gate_ref[...], spread_ref[...])
    sig = 0.5 + 0.5 * jnp.tanh(0.5 * pre)
    act = pre * sig
    back = back * gate
    out_ref[0] = (back * up * (sig * (1.0 + pre * (1.0 - sig)))).astype(BF16)
    out_ref[1] = (back * act).astype(BF16)
    out_ref[2] = (act * up * gate).astype(BF16)
    for i in range(3):
        r = jnp.minimum(3 * pl.program_id(0) + i, ROWS - 1)
        turned_ref[lanes(place_of(own_ref[0] ^ r)), :] = mid_ref[:, lanes(r)].T


def hidden(row, mid, grad, gates, spread, weights):
    whole = pl.BlockSpec((TOK, D), lambda j: (0, 0))
    parts = HID // BLK

    def weight(at):
        return pl.BlockSpec((D, BLK), lambda j: (0, at * parts + j))

    return pl.pallas_call(
        hidden_kernel,
        grid=(parts,),
        out_shape=(
            jax.ShapeDtypeStruct((3, TOK, HID), BF16),
            jax.ShapeDtypeStruct((D, TOK), BF16),
        ),
        in_specs=[
            pl.BlockSpec(memory_space=pltpu.SMEM),
            whole,
            whole,
            pl.BlockSpec(gates.shape, lambda j: (0, 0)),
            pl.BlockSpec((spread.shape[0], BLK), lambda j: (0, j)),
            weight(0),
            weight(1),
            weight(2),
        ],
        out_specs=(
            pl.BlockSpec((3, TOK, BLK), lambda j: (0, 0, j)),
            pl.BlockSpec((D, TOK), lambda j: (0, 0)),
        ),
        compiler_params=pltpu.CompilerParams(vmem_limit_bytes=60 * MIB),
        cost_estimate=pl.CostEstimate(
            flops=2 * TOK * D * HID * 3, bytes_accessed=32 * MIB, transcendentals=TOK * HID
        ),
    )(smem_values(row), mid, grad, gates, spread, weights, weights, weights)


def mid_grad_kernel(hid_ref, w_ref, out_ref):
    out = matmul_nt(hid_ref[0], w_ref[:, :HID]) + matmul_nt(hid_ref[1], w_ref[:, HID:])
    out_ref[...] = out.astype(BF16)


def mid_grad(hid, weights):
    return pl.pallas_call(
        mid_grad_kernel,
        grid=(4,),
        out_shape=jax.ShapeDtypeStruct((TOK, D), BF16),
        in_specs=[
            pl.BlockSpec((2, TOK, HID), lambda j: (0, 0, 0)),
            pl.BlockSpec((D // 4, 2 * HID), lambda j: (j, 0)),
        ],
        out_specs=pl.BlockSpec((TOK, D // 4), lambda j: (0, j)),
        compiler_params=pltpu.CompilerParams(vmem_limit_bytes=60 * MIB),
        cost_estimate=pl.CostEstimate(
            flops=2 * TOK * D * HID * 2, bytes_accessed=20 * MIB, transcendentals=0
        ),
    )(hid, weights)


def output_kernel(col_ref, hid_ref, w_ref, residual_ref, out_ref):
    out_ref[0] = matmul_nt(hid_ref[0], w_ref[...]).astype(BF16)
    own = pl.ds(pl.multiple_of(col_ref[0] * OWN, OWN), OWN)
    out_ref[0, own, :] = (
        matmul_nt(hid_ref[0, own, :], w_ref[...]) + residual_ref[...]
    ).astype(BF16)


def output(col, hid, weights, residual):
    return pl.pallas_call(
        output_kernel,
        grid=(COLS,),
        out_shape=jax.ShapeDtypeStruct((COLS, TOK, FEAT), BF16),
        in_specs=[
            pl.BlockSpec(memory_space=pltpu.SMEM),
            pl.BlockSpec((1, TOK, HID), lambda j: (2, 0, 0)),
            pl.BlockSpec((FEAT, HID), lambda j: (j, 2)),
            pl.BlockSpec((OWN, FEAT), lambda j: (0, j)),
        ],
        out_specs=pl.BlockSpec((1, TOK, FEAT), lambda j: (j, 0, 0)),
        compiler_params=pltpu.CompilerParams(vmem_limit_bytes=60 * MIB),
        cost_estimate=pl.CostEstimate(
            flops=TOK * D * HID // 8, bytes_accessed=MIB, transcendentals=0
        ),
    )(col.astype(jnp.int32).reshape(1), hid, weights, residual)


def mid_kernel(parts_ref, inputs_ref, gain_ref, residual_ref, scale_ref, normed_ref):
    total = inputs_ref[...].astype(F32)
    for c in range(COLS):
        total = total + parts_ref[c].astype(F32)
    scale = inverse_rms(total)
    residual_ref[...] = total
    scale_ref[...] = scale
    normed = (total * scale * gain_ref[...]).astype(BF16)
    for c in range(COLS):
        normed_ref[c] = normed


def mid(parts, inputs, gain):
    return pl.pallas_call(
        mid_kernel,
        out_shape=(
            jax.ShapeDtypeStruct((OWN, D), F32),
            jax.ShapeDtypeStruct((OWN, 1), F32),
            jax.ShapeDtypeStruct((COLS, OWN, D), BF16),
        ),
        compiler_params=pltpu.CompilerParams(vmem_limit_bytes=60 * MIB),
        cost_estimate=pl.CostEstimate(
            flops=OWN * D * 16, bytes_accessed=5 * MIB, transcendentals=0
        ),
    )(parts, inputs, gain.reshape(1, D))


def mid_back_kernel(
    parts_ref, residual_ref, scale_ref, grad_ref, gain_ref, out_ref, low_ref, gain_grad_ref
):
    d_mid = parts_ref[0].astype(F32)
    for c in range(1, COLS):
        d_mid = d_mid + parts_ref[c].astype(F32)
    residual, scale = residual_ref[...], scale_ref[...]
    gain_grad_ref[...] = jnp.sum(d_mid * residual * scale, axis=0, keepdims=True)
    out = grad_ref[...].astype(F32) + norm_backward(d_mid, residual, scale, gain_ref[...])
    out_ref[...] = out
    low = out.astype(BF16)
    for c in range(COLS):
        low_ref[c] = low


def mid_back(parts, residual, scale, grad, gain):
    return pl.pallas_call(
        mid_back_kernel,
        out_shape=(
            jax.ShapeDtypeStruct((OWN, D), F32),
            jax.ShapeDtypeStruct((COLS, OWN, D), BF16),
            jax.ShapeDtypeStruct((1, D), F32),
        ),
        compiler_params=pltpu.CompilerParams(vmem_limit_bytes=60 * MIB),
        cost_estimate=pl.CostEstimate(
            flops=OWN * D * 24, bytes_accessed=5 * MIB, transcendentals=0
        ),
    )(parts, residual, scale, grad, gain.reshape(1, D))


def input_back_kernel(
    col_ref, dq_ref, dl_ref, wq_ref, wl_ref, x_ref, scale_ref, gain_ref, own_ref, out_ref, gg_ref
):
    step = pl.program_id(0)
    d_in = matmul_nt(dq_ref[...], wq_ref[...]) + matmul_nt(dl_ref[...], wl_ref[...])
    x, scale = x_ref[...].astype(F32), scale_ref[...]
    gain_grad = jnp.sum(d_in * x * scale, axis=0, keepdims=True)

    @pl.when(step == 0)
    def _():
        gg_ref[...] = gain_grad

    @pl.when(step > 0)
    def _():
        gg_ref[...] += gain_grad

    out = norm_backward(d_in, x, scale, gain_ref[...])
    for half in range(2):
        mine = (col_ref[0] == 2 * step + half).astype(F32)
        rows = slice(half * OWN, (half + 1) * OWN)
        part = (out[rows] + mine * own_ref[...]).astype(BF16)
        for c in range(COLS):
            out_ref[c, rows, :] = part[:, c * FEAT : (c + 1) * FEAT]


def input_back(col, d_query, d_latent, w_packed, inputs, scale, gain, own):
    rows = 2 * OWN
    widths = (d_query.shape[1], d_latent.shape[1])
    return pl.pallas_call(
        input_back_kernel,
        grid=(TOK // rows,),
        out_shape=(
            jax.ShapeDtypeStruct((COLS, TOK, FEAT), BF16),
            jax.ShapeDtypeStruct((1, D), F32),
        ),
        in_specs=[
            pl.BlockSpec(memory_space=pltpu.SMEM),
            pl.BlockSpec((rows, widths[0]), lambda j: (j, 0)),
            pl.BlockSpec((rows, widths[1]), lambda j: (j, 0)),
            pl.BlockSpec((D, widths[0]), lambda j: (0, 0)),
            pl.BlockSpec((D, widths[1]), lambda j: (0, 6)),
            pl.BlockSpec((rows, D), lambda j: (j, 0)),
            pl.BlockSpec((rows, 1), lambda j: (j, 0)),
            pl.BlockSpec((1, D), lambda j: (0, 0)),
            pl.BlockSpec((OWN, D), lambda j: (0, 0)),
        ],
        out_specs=(
            pl.BlockSpec((COLS, rows, FEAT), lambda j: (0, j, 0)),
            pl.BlockSpec((1, D), lambda j: (0, 0)),
        ),
        compiler_params=pltpu.CompilerParams(vmem_limit_bytes=60 * MIB),
        cost_estimate=pl.CostEstimate(
            flops=2 * TOK * D * 640, bytes_accessed=9 * MIB, transcendentals=0
        ),
    )(
        smem_values(col),
        d_query,
        d_latent,
        w_packed,
        w_packed,
        inputs,
        scale,
        gain.reshape(1, D),
        own,
    )


def send_grad_kernel(mid_ref, grad_ref, hid_ref, out_ref):
    @pl.when(pl.program_id(0) < 2)
    def _():
        out_ref[...] = matmul(mid_ref[...], hid_ref[0]).astype(BF16)

    @pl.when(pl.program_id(0) == 2)
    def _():
        out_ref[...] = matmul(grad_ref[...], hid_ref[0]).astype(BF16)


def keep_grad_kernel(mid_ref, grad_ref, hid_ref, got_ref, *out_refs):
    def store(lhs_ref):
        out = matmul(lhs_ref[...], hid_ref[0]) + got_ref[...].astype(F32)
        first = 0
        for ref in out_refs:
            rows = ref.shape[0]
            ref[...] = out[first : first + rows].astype(BF16)
            first += rows

    @pl.when(pl.program_id(0) < 2)
    def _():
        store(mid_ref)

    @pl.when(pl.program_id(0) == 2)
    def _():
        store(grad_ref)


def send_grads(z, mid_t, grad_t, hid):
    rows = D // 4
    whole = pl.BlockSpec((rows, TOK), lambda s: (2 + z, 0))
    return pl.pallas_call(
        send_grad_kernel,
        grid=(3,),
        out_shape=jax.ShapeDtypeStruct((rows, WIDE), BF16),
        in_specs=[whole, whole, pl.BlockSpec((1, TOK, HID), lambda s: (s, 0, 0))],
        out_specs=pl.BlockSpec((rows, HID), lambda s: (0, s)),
        compiler_params=pltpu.CompilerParams(vmem_limit_bytes=60 * MIB),
        cost_estimate=pl.CostEstimate(
            flops=TOK * D * HID // 32, bytes_accessed=MIB, transcendentals=0
        ),
    )(mid_t, grad_t, hid)


def keep_grads(z, mid_t, grad_t, hid, got):
    rows = D // 4
    whole = pl.BlockSpec((rows, TOK), lambda s: (z, 0))
    heights = (LANES, LANES, CUT, CUT, LANES)
    return pl.pallas_call(
        keep_grad_kernel,
        grid=(3,),
        out_shape=[jax.ShapeDtypeStruct((height, WIDE), BF16) for height in heights],
        in_specs=[
            whole,
            whole,
            pl.BlockSpec((1, TOK, HID), lambda s: (s, 0, 0)),
            pl.BlockSpec((rows, HID), lambda s: (0, s)),
        ],
        out_specs=[pl.BlockSpec((h, HID), lambda s: (0, s)) for h in heights],
        compiler_params=pltpu.CompilerParams(vmem_limit_bytes=60 * MIB),
        cost_estimate=pl.CostEstimate(
            flops=TOK * D * HID // 32, bytes_accessed=MIB, transcendentals=0
        ),
    )(mid_t, grad_t, hid, got)


def rotary_tables(parents, row):
    seg = jnp.maximum(row - (TRUNK // BLK - 1), 0).astype(jnp.int32)
    depths = ancestor_depths(parents, seg.reshape(1))
    starts = jnp.where(seg > 0, TRUNK + BLK * depths, BLK * row)
    positions = (starts[:, None] + jnp.arange(BLK, dtype=jnp.int32)[None, :]).reshape(TOK)
    frequency = THETA ** (-jnp.arange(ROPE // 2, dtype=F32) / (ROPE // 2))
    angles = positions.astype(F32)[:, None] * frequency[None, :]
    cos_table, sin_table = jnp.cos(angles), jnp.sin(angles)
    cos_wide, sin_wide = jnp.tile(cos_table, (1, 4)), jnp.tile(sin_table, (1, 4))
    return cos_table.T, sin_table.T, cos_wide, sin_wide


def pack_hidden(shared, routed):
    rows = shared.shape[0]
    return jnp.concatenate(
        [
            shared,
            jnp.swapaxes(routed, 0, 1).reshape(rows, EXPERTS * ROUTED),
            jnp.zeros((rows, HID - SHARED - EXPERTS * ROUTED), routed.dtype),
        ],
        axis=1,
    )


def local(
    tokens,
    out_grad,
    parents,
    routes,
    gates,
    norm_in,
    w_query,
    w_latent,
    norm_latent,
    w_expand,
    w_output,
    norm_mid,
    w_shared_gate,
    w_shared_up,
    w_shared_down,
    w_expert_gate,
    w_expert_up,
    w_expert_down,
):
    row = lax.axis_index("row")
    col = lax.axis_index("col")
    group = row // QUART
    own_start = col * OWN
    gain_in = norm_in.astype(F32)
    gain_latent = norm_latent.astype(F32)
    gain_mid = norm_mid.astype(F32)
    heads = 2

    query_pack = w_query.reshape(D // ROWS, heads, QK)
    attn_pack = jnp.concatenate(
        [
            query_pack[:, :, :NOPE].reshape(D // ROWS, heads * NOPE),
            query_pack[:, :, NOPE:].reshape(D // ROWS, heads * ROPE),
            w_expand.reshape(KVL // ROWS, 4, 128).transpose(1, 0, 2).reshape(D // ROWS, 128),
            w_output.T,
            w_latent,
            jnp.zeros((D // ROWS, 128 - LATC), BF16),
        ],
        axis=1,
    )
    ffn_pack = jnp.concatenate(
        [
            pack_hidden(w_shared_gate, w_expert_gate),
            pack_hidden(w_shared_up, w_expert_up),
            pack_hidden(w_shared_down.T, jnp.swapaxes(w_expert_down, 1, 2)),
        ],
        axis=1,
    )
    attn_pair, input_pair, ffn_pack = together(
        pair_up(attn_pack, "row"), pair_up(tokens.reshape(TOK, FEAT), "col"), ffn_pack
    )
    line_groups = [[2 * y + z for y in range(4)] for z in range(2)]
    input_copies = jnp.broadcast_to(input_pair[None], (4,) + input_pair.shape)
    attn_ring, input_ring, ffn_pack, ffn_other, tables = together(
        ring_up(attn_pair, "row"),
        swap(input_copies, "col", line_groups),
        ffn_pack,
        trade(ffn_pack, "row", 8),
        rotary_tables(parents, row),
    )
    cos_t, sin_t, cos_wide, sin_wide = tables
    ffn_near = near_shards(ffn_pack)
    attn_full = finish_rows(attn_ring, row)
    expand_full = attn_full[:, 384:512].reshape(ROWS, 4, KVL // ROWS, 128)
    expand_full = expand_full.transpose(0, 2, 1, 3).reshape(KVL, heads * (NOPE + VDIM))

    inputs, normed_in, scale_in, latent_parts = front(col, input_ring, gain_in, attn_full)
    query = project_query(group, normed_in, attn_full, cos_wide, sin_wide)
    latent_t, query, normed_in, ffn_near = together(
        swap(latent_parts, "col"), query, normed_in, ffn_near
    )
    latent_t = latent_t.reshape(LAT, TOK)
    latent_normed_t, pack = expand(latent_t, cos_t, sin_t, gain_latent, expand_full)
    pack, query, ffn_near, out_grad, ffn_other = together(
        pack, query, ffn_near, out_grad, ffn_other
    )
    near, query, ffn_cut, grad_copies = together(
        swap(pack, "row"),
        trade_quarter(query),
        cut_near(ffn_near),
        jnp.broadcast_to(out_grad.reshape(1, TOK, FEAT), (COLS, TOK, FEAT)),
    )
    grad_ring = swap(grad_copies, "col")
    ffn_far = far_halves(ffn_cut)
    far = trade(near, "row", 1)

    meta = jnp.concatenate([pick(parents, group % MICRO), smem_values(row % QUART, group)])
    *attended_own, lse = attend(meta, query, near, far)
    attended_own, lse, ffn_far = together(attended_own, lse, ffn_far)
    attended_parts, grad_ring, ffn_far, ffn_other = together(
        trade_quarter(attended_own), grad_ring, ffn_far, ffn_other
    )
    attended, attn_parts = project(group, attended_parts, attn_full)
    grad_full, grad_t = features(row, grad_ring)

    def both_cores(pieces):
        far_pieces = [(trade(v, "row", 1), apart ^ 1, first) for v, apart, first in pieces]
        return list(pieces) + far_pieces

    pieces = both_cores(
        [(ffn_pack, 0, 0), (ffn_near[0], 2, 0), (ffn_near[1], 6, 0)]
        + [(ffn_far[0], 4, 0), (ffn_far[1], 4, CUT)]
    )
    own_inputs = lax.dynamic_slice_in_dim(inputs, own_start, OWN, 0)
    attn_parts, grad_full, grad_t, values = together(
        swap(attn_parts, "col"), grad_full, grad_t, [v for v, _, _ in pieces]
    )
    named = routes.reshape(TOK, TOPK, 1) == jnp.arange(EXPERTS, dtype=jnp.int32)
    gate_of = jnp.sum(jnp.where(named, gates.reshape(TOK, TOPK, 1), 0.0), axis=1)
    gate_of = jnp.concatenate(
        [jnp.ones((TOK, 1), F32), gate_of, jnp.zeros((TOK, 15 - EXPERTS), F32)], axis=1
    )
    gate_high = gate_of.astype(BF16)
    gate_low = (gate_of - gate_high.astype(F32)).astype(BF16)
    gate_parts = jnp.concatenate([gate_high, gate_low], axis=1)
    unit = jnp.arange(HID, dtype=jnp.int32)
    expert = jnp.where(unit < SHARED, 0, 1 + (unit - SHARED) // ROUTED)
    spread = (expert[None, :] == jnp.arange(16, dtype=jnp.int32)[:, None]).astype(BF16)
    spread = jnp.concatenate([spread, spread], axis=0)
    attn_parts, gate_parts, spread = together(attn_parts, gate_parts, spread)
    residual, scale_mid, normed_mid = mid(attn_parts, own_inputs, gain_mid)
    normed_mid, other_near = together(normed_mid, near_shards(ffn_other))
    pieces = [(v, apart, first) for v, (_, apart, first) in zip(values, pieces)]
    ffn_full = put_shards(row, None, pieces)
    pieces = both_cores([(ffn_other, 8, 0), (other_near[0], 10, 0), (other_near[1], 14, 0)])
    ffn_full = put_shards(row, ffn_full, pieces)
    normed_mid, ffn_full, other_far = together(
        swap(normed_mid, "col"), ffn_full, far_halves(cut_near(other_near))
    )
    normed_mid = normed_mid.reshape(TOK, D)
    pieces = both_cores([(other_far[0], 12, 0), (other_far[1], 12, CUT)])
    ffn_full = put_shards(row, ffn_full, pieces)

    hid, normed_t = hidden(row, normed_mid, grad_full, gate_parts, spread, ffn_full)
    send = send_grads(1, normed_t, grad_t, hid)
    hid, send, normed_t = together(hid, send, normed_t)
    mid_parts = mid_grad(hid, ffn_full)
    hid, normed_t, mid_parts = together(hid, normed_t, mid_parts)
    blocks = keep_grads(1, normed_t, grad_t, hid, trade(send, "row", 1))
    send = send_grads(0, normed_t, grad_t, after(hid, blocks))
    mid_parts, hid, block, sides, send, normed_t = together(
        swap(mid_parts.reshape(COLS, OWN, D), "col"),
        hid,
        blocks[0],
        with_opposite(blocks, sum_opposite(blocks)),
        send,
        normed_t,
    )
    own_grad = lax.dynamic_slice_in_dim(grad_full, own_start, OWN, 0)
    d_residual, d_low, mid_gain = mid_back(mid_parts, residual, scale_mid, own_grad, gain_mid)
    d_low, hid, send = together(d_low, hid, send)
    d_low, out_parts, sides, own_blocks = together(
        swap(d_low, "col"),
        output(col, hid, ffn_full, residual),
        sum_neighbours(sides),
        keep_grads(0, normed_t, grad_t, hid, trade(send, "row", 1)),
    )
    other_sum = add_low(block.astype(F32) + sides[0].astype(F32), sides[1])

    d_attended = trade_quarter(project_back(group, d_low, attn_full))
    d_attended, other_sum, out_parts = together(d_attended, other_sum, out_parts)
    *d_query, d_near, d_far = attend_back(
        meta, query, attended_own, d_attended, near, far, lse
    )
    d_query, d_near, d_far, halves, other_low, out_parts, out_left = together(
        d_query,
        d_near,
        d_far,
        sum_opposite(own_blocks),
        trade(other_sum[:CUT], "row", 8),
        out_parts,
        collect_y(out_parts, col // 2, 1),
    )
    d_far = trade(d_far, "row", 1)
    d_query, d_pack = together(trade_quarter(d_query), add_low(d_near, d_far))
    d_query = query_back(group, d_query, cos_wide, sin_wide)
    d_pack, sides, out_right, out_parts, d_query, attn_grads = together(
        swap(d_pack, "row"),
        with_opposite(own_blocks, halves),
        collect_y(out_parts, col // 2, 3),
        out_parts,
        d_query,
        attn_weight_grads(row, normed_in, d_query, d_low.reshape(TOK, D), attended),
    )
    sides = sum_neighbours(sides)

    d_expanded, d_latent, latent_gain = latent_back(
        d_pack, latent_t, cos_t, sin_t, gain_latent, expand_full
    )
    other_high = trade(after(other_sum, d_latent)[CUT:], "row", 8)
    d_latent, attn_grads, out_far, out_own = together(
        swap(d_latent.reshape(COLS, LATC, TOK), "col"),
        add_low(attn_grads[0], trade(attn_grads[1], "row", 1)),
        collect_y(out_parts, col // 2, 2),
        collect_y(out_parts, col // 2, 0),
    )
    out_parts = (out_own, out_left, out_far, out_right)
    d_latent = jnp.sum(d_latent.astype(F32), axis=0).astype(BF16)
    d_latent = jnp.concatenate([d_latent, jnp.zeros((128 - LATC, TOK), BF16)], axis=0).T

    d_tokens, in_gain = input_back(
        col, d_query, d_latent, attn_full, inputs, scale_in, gain_in, d_residual
    )
    d_tokens, in_gain, sides, other_high = together(d_tokens, in_gain, sides, other_high)

    gain = jnp.concatenate([in_gain.reshape(D), latent_gain.reshape(KVL), mid_gain.reshape(D)])
    d_tokens, d_latent = together(d_tokens, d_latent)
    latent_grads = latent_weight_grads(row, normed_in, d_latent, latent_normed_t, d_expanded)
    latent_grads = add_low(latent_grads[0], trade(latent_grads[1], "row", 1))
    ffn_grads = own_blocks[0].astype(F32) + sides[0].astype(F32) + sides[1].astype(F32)
    other_sum = jnp.concatenate([other_low, other_high], axis=0)
    ffn_grads = ffn_grads + other_sum.astype(F32)

    def unpack(at):
        part = ffn_grads[:, at * HID : (at + 1) * HID]
        routed = part[:, SHARED : SHARED + EXPERTS * ROUTED]
        return part[:, :SHARED], routed.reshape(-1, EXPERTS, ROUTED)

    grad_shared_gate, grad_expert_gate = unpack(0)
    grad_shared_up, grad_expert_up = unpack(1)
    grad_shared_down, grad_expert_down = unpack(2)
    ffn_outs = (
        grad_shared_gate,
        grad_shared_up,
        grad_shared_down.T,
        jnp.swapaxes(grad_expert_gate, 0, 1),
        jnp.swapaxes(grad_expert_up, 0, 1),
        grad_expert_down.transpose(1, 2, 0),
    )
    d_tokens, attn_grads, latent_grads, out_parts, gain, ffn_outs = together(
        swap(d_tokens, "col"),
        [reduce_x(attn_grads, j) for j in range(4)],
        latent_grads,
        out_parts,
        gain,
        ffn_outs,
    )
    latent_grads = [reduce_x(latent_grads, j) for j in range(4)]
    attn_grads = reduce_z(attn_grads, latent_grads)
    layer_out = collect_z(out_parts, col % 2).astype(BF16)
    input_grad = jnp.sum(d_tokens.astype(F32), axis=0).astype(BF16)
    gain = share(gain.astype(BF16).reshape(-1, 128), ("row", "col"), ROWS * COLS)
    gain, input_grad, attn_grads, layer_out = together(gain, input_grad, attn_grads, layer_out)
    gain = jnp.sum(gain.astype(F32), axis=0).reshape(-1)
    grad_query = jnp.concatenate(
        [
            attn_grads[:, : heads * NOPE].reshape(-1, heads, NOPE),
            attn_grads[:, heads * NOPE : heads * QK].reshape(-1, heads, ROPE),
        ],
        axis=-1,
    ).reshape(-1, heads * QK)
    grad_output = attn_grads[:, 384:640].T
    grad_expand = attn_grads[:, 640:768].reshape(4, KVL // ROWS, 128)
    grad_expand = grad_expand.transpose(1, 0, 2).reshape(KVL // ROWS, heads * (NOPE + VDIM))
    grad_latent = attn_grads[:, 768 : 768 + LATC]

    return (
        layer_out.reshape(MICRO, BLK, FEAT),
        input_grad.reshape(MICRO, BLK, FEAT),
        gain[:D],
        grad_query,
        grad_latent,
        gain[D : D + KVL],
        grad_expand,
        grad_output,
        gain[D + KVL :],
        *ffn_outs,
    )


def solution(mesh):
    in_specs = (
        P(None, "row", "col"),
        P(None, "row", "col"),
        P(),
        P(None, "row", None),
        P(None, "row", None),
        P(),
        P("row", "col"),
        P("row", "col"),
        P(),
        P("row", "col"),
        P("col", "row"),
        P(),
        P("row", "col"),
        P("row", "col"),
        P("col", "row"),
        P(None, "row", "col"),
        P(None, "row", "col"),
        P(None, "col", "row"),
    )
    out_specs = (
        P(None, "row", "col"),
        P(None, "row", "col"),
        P(),
        P("row", "col"),
        P("row", "col"),
        P(),
        P("row", "col"),
        P("col", "row"),
        P(),
        P("row", "col"),
        P("row", "col"),
        P("col", "row"),
        P(None, "row", "col"),
        P(None, "row", "col"),
        P(None, "col", "row"),
    )
    return jax.shard_map(local, mesh=mesh, in_specs=in_specs, out_specs=out_specs, check_vma=False)
```

```python
import functools

import jax
import jax.numpy as jnp
from jax import lax
from jax.experimental import pallas as pl
from jax.experimental.pallas import tpu as pltpu
from jax.sharding import PartitionSpec as P

D = 2048
NOPE = 128
ROPE = 64
QK = NOPE + ROPE
VDIM = 128
KVL = 512
TOPK = 6
EXPERTS = 8
MICRO = 2
TRUNK = 1024
BLK = 256
SEGS = 13
ROWS = 16
COLS = 8
TOK = MICRO * BLK
OWN = TOK // COLS
FEAT = D // COLS
QUART = 4
SHARED = 352
ROUTED = 176
HID = 1792
LAT = KVL + ROPE
HALF = BLK // 2
QKP = 256
PACK = VDIM + QKP
WIDE = 3 * HID
LANES = D // ROWS
CUT = LANES // 2
LATC = LAT // COLS
SCALE = QK**-0.5
EPS = 1e-06
THETA = 10000.0
NEG = -1e30
MIB = 1024 * 1024
F32 = jnp.float32
BF16 = jnp.bfloat16
NT = (((1,), (1,)), ((), ()))
TN = (((0,), (0,)), ((), ()))


def inverse_rms(values):
    return lax.rsqrt(jnp.mean(values * values, axis=-1, keepdims=True) + EPS)


def norm_backward(grad_out, values, inv_scale, norm_gain):
    weighted = grad_out * norm_gain
    inner = jnp.mean(weighted * values, axis=-1, keepdims=True)
    return inv_scale * weighted - values * (inv_scale * inv_scale * inv_scale) * inner


def matmul(a, b):
    return jnp.dot(a, b, preferred_element_type=F32)


def matmul_nt(a, b):
    return lax.dot_general(a, b, NT, preferred_element_type=F32)


def matmul_tn(a, b):
    return lax.dot_general(a, b, TN, preferred_element_type=F32)


def swap(values, axis, groups=None):
    return lax.all_to_all(values, axis, 0, 0, tiled=True, axis_index_groups=groups)


def share(values, axis, count):
    return swap(jnp.broadcast_to(values[None], (count,) + values.shape), axis)


def trade(values, axis, mask):
    count = ROWS if axis == "row" else COLS
    return lax.ppermute(values, axis, [(i, i ^ mask) for i in range(count)])


def after(values, *others):
    return lax.optimization_barrier((values,) + others)[0]


def together(*values):
    return lax.optimization_barrier(values)


def smem_values(*values):
    return jnp.stack([jnp.asarray(v, jnp.int32) for v in values])


def pick(values, index, axis=0):
    return lax.dynamic_index_in_dim(values, index, axis, keepdims=False)


def pair_up(shard, axis):
    return jnp.stack([shard, trade(shard, axis, 8 if axis == "row" else 1)])


def ring_up(pair, axis):
    return [pair] + [trade(pair, axis, j << 1) for j in (1, 2, 3)]


def sort_rows_kernel(own_ref, near_ref, far_ref, out_ref):
    for core, ref in ((0, near_ref), (1, far_ref)):
        for x in range(4):
            for z in range(2):
                out_ref[own_ref[0] ^ (8 * z + 2 * x + core)] = ref[x, z]


def finish_rows(ring, row):
    near = jnp.stack(ring)
    far = trade(near, "row", 1)
    vmem = pl.BlockSpec(memory_space=pltpu.VMEM)
    out = pl.pallas_call(
        sort_rows_kernel,
        out_shape=jax.ShapeDtypeStruct((ROWS,) + near.shape[2:], near.dtype),
        in_specs=[pl.BlockSpec(memory_space=pltpu.SMEM), vmem, vmem],
        out_specs=vmem,
        compiler_params=pltpu.CompilerParams(vmem_limit_bytes=16 * MIB),
        cost_estimate=pl.CostEstimate(flops=0, bytes_accessed=near.size, transcendentals=0),
    )(smem_values(row), near, far)
    return out.reshape(D, near.shape[3])


def place_of(apart):
    return ((apart & 1) << 3) | ((apart >> 3) << 2) | ((apart >> 1) & 3)


def lanes(at):
    return pl.ds(pl.multiple_of(at * LANES, LANES), LANES)


def features_kernel(own_ref, blocks_ref, out_ref, out_t_ref):
    for c in range(COLS):
        out_ref[:, c * FEAT : (c + 1) * FEAT] = blocks_ref[c]
    for r in range(ROWS):
        block = blocks_ref[r // 2, :, (r % 2) * LANES : (r % 2 + 1) * LANES]
        out_t_ref[lanes(place_of(own_ref[0] ^ r)), :] = block.T


def features(row, blocks):
    vmem = pl.BlockSpec(memory_space=pltpu.VMEM)
    return pl.pallas_call(
        features_kernel,
        out_shape=(
            jax.ShapeDtypeStruct((TOK, D), BF16),
            jax.ShapeDtypeStruct((D, TOK), BF16),
        ),
        in_specs=[pl.BlockSpec(memory_space=pltpu.SMEM), vmem],
        out_specs=(vmem, vmem),
        compiler_params=pltpu.CompilerParams(vmem_limit_bytes=60 * MIB),
        cost_estimate=pl.CostEstimate(flops=0, bytes_accessed=MIB, transcendentals=0),
    )(smem_values(row), blocks)


def near_shards(shard):
    return trade(shard, "row", 2), trade(shard, "row", 6)


def cut_near(near):
    return near[1][:CUT], near[0][CUT:]


def far_halves(parts):
    return trade(parts[0], "row", 2), trade(parts[1], "row", 6)


def put_kernel(places, own_ref, *refs):
    out_ref, sems = refs[-2:]
    copies = []
    for i, (apart, first) in enumerate(places):
        at = (own_ref[0] ^ apart) * LANES + first
        rows = pl.ds(pl.multiple_of(at, CUT), refs[i].shape[0])
        copy = pltpu.make_async_copy(refs[i], out_ref.at[rows], sems.at[i])
        copy.start()
        copies.append(copy)
    for copy in copies:
        copy.wait()


def put_shards(row, whole, pieces):
    values = [piece for piece, _, _ in pieces]
    places = [(apart, first) for _, apart, first in pieces]
    fresh = whole is None
    return pl.pallas_call(
        functools.partial(put_kernel, places),
        out_shape=jax.ShapeDtypeStruct((D, WIDE), BF16),
        in_specs=[pl.BlockSpec(memory_space=pltpu.SMEM)]
        + [pl.BlockSpec(memory_space=pltpu.VMEM)] * len(values)
        + ([] if fresh else [pl.BlockSpec(memory_space=pl.ANY)]),
        out_specs=pl.BlockSpec(memory_space=pl.ANY),
        scratch_shapes=[pltpu.SemaphoreType.DMA((len(values),))],
        input_output_aliases={} if fresh else {1 + len(values): 0},
        compiler_params=pltpu.CompilerParams(vmem_limit_bytes=60 * MIB),
        cost_estimate=pl.CostEstimate(flops=0, bytes_accessed=MIB, transcendentals=0),
    )(smem_values(row), *values, *([] if fresh else [whole]))


def sum_opposite(blocks):
    return trade(blocks[2], "row", 2), trade(blocks[3], "row", 6)


def add_low(a, b):
    return (a.astype(F32) + b.astype(F32)).astype(BF16)


def sides_kernel(b1_ref, b3_ref, h1_ref, h3_ref, left_ref, right_ref):
    left_ref[:CUT] = b1_ref[:CUT]
    left_ref[CUT:] = (b1_ref[CUT:].astype(F32) + h3_ref[...].astype(F32)).astype(BF16)
    right_ref[:CUT] = (b3_ref[:CUT].astype(F32) + h1_ref[...].astype(F32)).astype(BF16)
    right_ref[CUT:] = b3_ref[CUT:]


def with_opposite(blocks, halves):
    return pl.pallas_call(
        sides_kernel,
        out_shape=[jax.ShapeDtypeStruct((LANES, WIDE), BF16)] * 2,
        compiler_params=pltpu.CompilerParams(vmem_limit_bytes=60 * MIB),
        cost_estimate=pl.CostEstimate(flops=0, bytes_accessed=MIB, transcendentals=0),
    )(blocks[1], blocks[4], *halves)


def sum_neighbours(sides):
    return trade(sides[0], "row", 2), trade(sides[1], "row", 6)


def reduce_x(blocks, j):
    blocks = blocks.reshape((4, 2) + blocks.shape[1:])
    return trade(blocks[j], "row", j << 1) if j else blocks[0]


def reduce_z(*packs):
    sums = []
    for parts in packs:
        parts = [part.astype(F32) for part in parts]
        sums.append(parts[0] + parts[1] + (parts[2] + parts[3]))
    blocks = jnp.concatenate(sums, axis=-1).astype(BF16)
    return blocks[0].astype(F32) + trade(blocks[1], "row", 8).astype(F32)


def attn_grads_kernel(own_ref, x_ref, dq_ref, low_ref, att_ref, keep_ref, send_ref, out):
    out[:, :384] = matmul_tn(x_ref[...], dq_ref[...])
    out[:, 384:] = matmul_tn(low_ref[...], att_ref[...])
    core = own_ref[0] & 1
    keep_ref[0] = out[lanes(core), :].astype(BF16)
    send_ref[0] = out[lanes(1 - core), :].astype(BF16)


def latent_grads_kernel(own_ref, x_ref, dl_ref, lat_ref, de_ref, keep_ref, send_ref, out):
    out[:, 128:] = matmul_tn(x_ref[...], dl_ref[...])
    expand_grad = matmul(lat_ref[...], de_ref[...])
    for half in range(2):
        for i in range(4):
            rows = slice(half * LANES + 32 * i, half * LANES + 32 * (i + 1))
            part = expand_grad[32 * half : 32 * (half + 1), 128 * i : 128 * (i + 1)]
            out[rows, :128] = part
    core = own_ref[0] & 1
    keep_ref[0] = out[lanes(core), :].astype(BF16)
    send_ref[0] = out[lanes(1 - core), :].astype(BF16)


def place_pair(i, own):
    apart = i ^ (own[0] >> 1)
    return (apart & 3) * 2 + (apart >> 2), 0, 0


def weight_grad_pairs(kernel, width, row, ins, specs):
    block = pl.BlockSpec((1, LANES, width), place_pair)
    return pl.pallas_call(
        kernel,
        out_shape=[jax.ShapeDtypeStruct((ROWS // 2, LANES, width), BF16)] * 2,
        grid_spec=pltpu.PrefetchScalarGridSpec(
            num_scalar_prefetch=1,
            grid=(ROWS // 2,),
            in_specs=specs,
            out_specs=[block, block],
            scratch_shapes=[pltpu.VMEM((2 * LANES, width), F32)],
        ),
        compiler_params=pltpu.CompilerParams(vmem_limit_bytes=60 * MIB),
        cost_estimate=pl.CostEstimate(flops=TOK * D * 16, bytes_accessed=MIB, transcendentals=0),
    )(smem_values(row), *ins)


def whole_block(values):
    return pl.BlockSpec(values.shape, lambda i, own: (0, 0))


def attn_weight_grads(row, normed, d_query, d_low, attended):
    columns = pl.BlockSpec((TOK, 2 * LANES), lambda i, own: (0, i))
    specs = [columns, whole_block(d_query), columns, whole_block(attended)]
    ins = (normed, d_query, d_low, attended)
    return weight_grad_pairs(attn_grads_kernel, 640, row, ins, specs)


def latent_weight_grads(row, normed, d_latent, latent_t, d_expanded):
    columns = pl.BlockSpec((TOK, 2 * LANES), lambda i, own: (0, i))
    lines = pl.BlockSpec((2 * KVL // ROWS, TOK), lambda i, own: (i, 0))
    specs = [columns, whole_block(d_latent), lines, whole_block(d_expanded)]
    ins = (normed, d_latent, latent_t, d_expanded)
    return weight_grad_pairs(latent_grads_kernel, 256, row, ins, specs)


def collect_y(blocks, y, j):
    blocks = blocks.reshape((4, 2) + blocks.shape[1:])
    return trade(pick(blocks, y ^ j), "col", j << 1) if j else pick(blocks, y)


def collect_z(blocks, z):
    blocks = [block.astype(F32) for block in blocks]
    blocks = (blocks[0] + blocks[1] + (blocks[2] + blocks[3])).astype(BF16)
    got = trade(pick(blocks, 1 - z), "col", 1)
    return pick(blocks, z).astype(F32) + got.astype(F32)


def trade_quarter(blocks):
    return [blocks[0]] + [trade(blocks[j], "row", j << 2) for j in (1, 2, 3)]


def depth_kernel(parents_ref, seg_ref, out_ref):
    seg = seg_ref[0]
    for m in range(MICRO):

        def climb(step, state):
            at, count = state
            return parents_ref[m, at], count + (at > 0).astype(jnp.int32)

        _, count = lax.fori_loop(0, SEGS, climb, (parents_ref[m, seg], jnp.int32(0)))
        out_ref[m] = count


def ancestor_depths(parents, seg):
    smem = pl.BlockSpec(memory_space=pltpu.SMEM)
    return pl.pallas_call(
        depth_kernel,
        out_shape=jax.ShapeDtypeStruct((MICRO,), jnp.int32),
        in_specs=[smem, smem],
        out_specs=smem,
    )(parents, seg)


def list_ancestors(meta, qb, listed):
    def climb(step, state):
        at, count = state
        listed[count] = at + 3
        return meta[at], count + (at > 0).astype(jnp.int32)

    _, count = lax.fori_loop(0, SEGS, climb, (meta[qb - 3], jnp.int32(0)))
    return count


def causal_mask():
    key = lax.broadcasted_iota(jnp.int32, (BLK, BLK), 0)
    query = lax.broadcasted_iota(jnp.int32, (BLK, BLK), 1)
    return key <= query


def join_halves(meta, near_ref, far_ref, pack):
    core = meta[SEGS] % 2
    pack[:, pl.ds(pl.multiple_of(core * HALF, HALF), HALF), :] = near_ref[...]
    pack[:, pl.ds(pl.multiple_of((1 - core) * HALF, HALF), HALF), :] = far_ref[...]


def attend_kernel(meta, q0, q1, q2, q3, near_ref, far_ref, o0, o1, o2, o3, lse_ref, *scratch):
    q_ref, o_ref, pack, listed = scratch
    quarter, own = meta[SEGS], meta[SEGS + 1]
    join_halves(meta, near_ref, far_ref, pack)
    for j, ref in enumerate((q0, q1, q2, q3)):
        q_ref[own ^ j] = ref[...]
    for i in range(QUART):
        qb = QUART * i + quarter
        q = q_ref[i]
        s = matmul_nt(pack[qb, :, VDIM:], q) * SCALE
        s = jnp.where(causal_mask(), s, NEG)
        top = jnp.max(s, axis=0, keepdims=True)
        p = jnp.exp(s - top)
        total = jnp.sum(p, axis=0, keepdims=True)
        out = matmul_tn(pack[qb, :, :VDIM], p.astype(BF16))

        def visit(block, state):
            top, total, out = state
            s = matmul_nt(block[:, VDIM:], q) * SCALE
            new_top = jnp.maximum(top, jnp.max(s, axis=0, keepdims=True))
            shrink = jnp.exp(top - new_top)
            p = jnp.exp(s - new_top)
            total = total * shrink + jnp.sum(p, axis=0, keepdims=True)
            out = out * shrink + matmul_tn(block[:, :VDIM], p.astype(BF16))
            return new_top, total, out

        def step(kb, state):
            return visit(pack[kb], state)

        state = (top, total, out)
        if i == 0:
            state = lax.fori_loop(0, quarter, step, state)
        else:
            state = visit(pack[: TRUNK // BLK].reshape(TRUNK, PACK), state)
            count = list_ancestors(meta, qb, listed)
            state = lax.fori_loop(0, count, lambda t, c: step(listed[t], c), state)
        top, total, out = state
        o_ref[i] = (out * (1.0 / total)).T.astype(BF16)
        lse_ref[i] = top + jnp.log(total)
    for j, ref in enumerate((o0, o1, o2, o3)):
        ref[...] = o_ref[own ^ j]


def attend(meta, q, near, far):
    smem = pl.BlockSpec(memory_space=pltpu.SMEM)
    vmem = pl.BlockSpec(memory_space=pltpu.VMEM)
    pairs = 32 * BLK * BLK
    return pl.pallas_call(
        attend_kernel,
        out_shape=[jax.ShapeDtypeStruct((BLK, VDIM), BF16)] * QUART
        + [jax.ShapeDtypeStruct((QUART, 1, BLK), F32)],
        in_specs=[smem] + [vmem] * 6,
        out_specs=[vmem] * 5,
        scratch_shapes=[
            pltpu.VMEM((QUART, BLK, QKP), BF16),
            pltpu.VMEM((QUART, BLK, VDIM), BF16),
            pltpu.VMEM((ROWS, BLK, PACK), BF16),
            pltpu.SMEM((16,), jnp.int32),
        ],
        compiler_params=pltpu.CompilerParams(vmem_limit_bytes=60 * MIB),
        cost_estimate=pl.CostEstimate(
            flops=pairs * 2 * (QK + VDIM), bytes_accessed=4 * MIB, transcendentals=pairs
        ),
    )(meta, *q, near, far)


def attend_back_kernel(meta, *refs):
    ins, outs, scratch = refs[:15], refs[15:21], refs[21:]
    near_ref, far_ref, lse_ref = ins[12:]
    keep_ref, send_ref = outs[4:]
    q_ref, o_ref, do_ref, dq_ref, pack, dk, dv, listed = scratch
    quarter, own = meta[SEGS], meta[SEGS + 1]
    core = quarter % 2
    join_halves(meta, near_ref, far_ref, pack)
    for j in range(QUART):
        q_ref[own ^ j] = ins[j][...]
        o_ref[own ^ j] = ins[QUART + j][...]
        do_ref[own ^ j] = ins[2 * QUART + j][...]
    dk[...] = jnp.zeros_like(dk)
    dv[...] = jnp.zeros_like(dv)
    for i in range(QUART):
        qb = QUART * i + quarter
        q = q_ref[i]
        do = do_ref[i]
        lse = lse_ref[i]
        pairs = do.astype(F32) * o_ref[i].astype(F32)
        delta = jnp.sum(pairs.T, axis=0, keepdims=True)

        def trunk(dqt):
            block = pack[: TRUNK // BLK].reshape(TRUNK, PACK)
            key = block[:, VDIM:]
            p = jnp.exp(matmul_nt(key, q) * SCALE - lse)
            dp = matmul_nt(block[:, :VDIM], do)
            ds = (p * (dp - delta) * SCALE).astype(BF16)
            shape = (TRUNK // BLK, BLK, -1)
            dv[: TRUNK // BLK] += matmul(p.astype(BF16), do).reshape(shape)
            dk[: TRUNK // BLK] += matmul(ds, q).reshape(shape)
            return dqt + matmul_tn(key, ds)

        def step(kb, dqt, masked=False):
            key = pack[kb, :, VDIM:]
            s = matmul_nt(key, q) * SCALE
            p = jnp.exp(s - lse)
            if masked:
                p = jnp.where(causal_mask(), p, 0.0)
            dp = matmul_nt(pack[kb, :, :VDIM], do)
            ds = (p * (dp - delta) * SCALE).astype(BF16)
            dv[kb] += matmul(p.astype(BF16), do)
            dk[kb] += matmul(ds, q)
            return dqt + matmul_tn(key, ds)

        dqt = step(qb, jnp.zeros((QKP, BLK), F32), True)
        if i == 0:
            dqt = lax.fori_loop(0, quarter, step, dqt)
        else:
            dqt = trunk(dqt)
            count = list_ancestors(meta, qb, listed)
            dqt = lax.fori_loop(0, count, lambda t, c: step(listed[t], c), dqt)
        dq_ref[i] = dqt.T.astype(BF16)
    for j in range(QUART):
        outs[j][...] = dq_ref[own ^ j]
    for half, ref in ((core, keep_ref), (1 - core, send_ref)):
        part = pl.ds(pl.multiple_of(half * HALF, HALF), HALF)
        ref[:, :, :VDIM] = dv[:, part, :].astype(BF16)
        ref[:, :, VDIM:] = dk[:, part, :].astype(BF16)


def attend_back(meta, q, o, d_o, near, far, lse):
    smem = pl.BlockSpec(memory_space=pltpu.SMEM)
    vmem = pl.BlockSpec(memory_space=pltpu.VMEM)
    pairs = 32 * BLK * BLK
    return pl.pallas_call(
        attend_back_kernel,
        out_shape=[jax.ShapeDtypeStruct((BLK, QKP), BF16)] * QUART
        + [jax.ShapeDtypeStruct((ROWS, HALF, PACK), BF16)] * 2,
        in_specs=[smem] + [vmem] * 15,
        out_specs=[vmem] * 6,
        scratch_shapes=[
            pltpu.VMEM((QUART, BLK, QKP), BF16),
            pltpu.VMEM((QUART, BLK, VDIM), BF16),
            pltpu.VMEM((QUART, BLK, VDIM), BF16),
            pltpu.VMEM((QUART, BLK, QKP), BF16),
            pltpu.VMEM((ROWS, BLK, PACK), BF16),
            pltpu.VMEM((ROWS, BLK, QKP), F32),
            pltpu.VMEM((ROWS, BLK, VDIM), F32),
            pltpu.SMEM((16,), jnp.int32),
        ],
        compiler_params=pltpu.CompilerParams(vmem_limit_bytes=60 * MIB),
        cost_estimate=pl.CostEstimate(
            flops=pairs * 2 * (3 * QK + 2 * VDIM), bytes_accessed=10 * MIB, transcendentals=pairs
        ),
    )(meta, *q, *o, *d_o, near, far, lse)


def project_kernel(own_ref, b0, b1, b2, b3, w_ref, attended_ref, out_ref, blocks):
    for j, ref in enumerate((b0, b1, b2, b3)):
        blocks[own_ref[0] ^ j] = ref[...]
    for h in range(2):
        for m in range(MICRO):
            attended_ref[m * BLK : (m + 1) * BLK, h * VDIM : (h + 1) * VDIM] = blocks[2 * h + m]
    out = matmul_nt(attended_ref[...], w_ref[...]).astype(BF16)
    for c in range(COLS):
        out_ref[c] = out[c * OWN : (c + 1) * OWN]


def project(own, blocks, w_packed):
    def whole(*shape):
        return pl.BlockSpec(shape, lambda i: (0,) * len(shape))

    return pl.pallas_call(
        project_kernel,
        grid=(1,),
        out_shape=(
            jax.ShapeDtypeStruct((TOK, 2 * VDIM), BF16),
            jax.ShapeDtypeStruct((COLS, OWN, D), BF16),
        ),
        in_specs=[pl.BlockSpec(memory_space=pltpu.SMEM)]
        + [whole(BLK, VDIM)] * QUART
        + [pl.BlockSpec((D, 2 * VDIM), lambda i: (0, 2))],
        out_specs=(whole(TOK, 2 * VDIM), whole(COLS, OWN, D)),
        scratch_shapes=[pltpu.VMEM((QUART, BLK, VDIM), BF16)],
        compiler_params=pltpu.CompilerParams(vmem_limit_bytes=60 * MIB),
        cost_estimate=pl.CostEstimate(flops=TOK * D * 512, bytes_accessed=MIB, transcendentals=0),
    )(smem_values(own), *blocks, w_packed)


def project_back_kernel(own_ref, d_ref, w_ref, o0, o1, o2, o3, blocks):
    for c in range(COLS):
        rows = slice((c % QUART) * OWN, (c % QUART + 1) * OWN)
        part = matmul(d_ref[c], w_ref[...]).astype(BF16)
        for h in range(2):
            blocks[2 * h + c // QUART, rows, :] = part[:, h * VDIM : (h + 1) * VDIM]
    for j, ref in enumerate((o0, o1, o2, o3)):
        ref[...] = blocks[own_ref[0] ^ j]


def project_back(own, d_low, w_packed):
    def whole(*shape):
        return pl.BlockSpec(shape, lambda i: (0,) * len(shape))

    return pl.pallas_call(
        project_back_kernel,
        grid=(1,),
        out_shape=[jax.ShapeDtypeStruct((BLK, VDIM), BF16)] * QUART,
        in_specs=[
            pl.BlockSpec(memory_space=pltpu.SMEM),
            whole(COLS, OWN, D),
            pl.BlockSpec((D, 2 * VDIM), lambda i: (0, 2)),
        ],
        out_specs=[whole(BLK, VDIM)] * QUART,
        scratch_shapes=[pltpu.VMEM((QUART, BLK, VDIM), BF16)],
        compiler_params=pltpu.CompilerParams(vmem_limit_bytes=60 * MIB),
        cost_estimate=pl.CostEstimate(flops=TOK * D * 512, bytes_accessed=MIB, transcendentals=0),
    )(smem_values(own), d_low, w_packed)


def front_kernel(col_ref, pieces_ref, gain_ref, wl_ref, x_ref, normed_ref, scale_ref, lat_ref):
    for y in range(4):
        for z in range(2):
            at = (2 * y + (z ^ (col_ref[0] & 1))) * FEAT
            x_ref[:, pl.ds(pl.multiple_of(at, FEAT), FEAT)] = pieces_ref[y, z]
    x = x_ref[...].astype(F32)
    scale = inverse_rms(x)
    scale_ref[...] = scale
    normed = (x * scale * gain_ref[...]).astype(BF16)
    normed_ref[...] = normed
    latent = matmul(normed, wl_ref[...]).T[:LATC].astype(BF16)
    for c in range(COLS):
        lat_ref[c] = latent


def front(col, pieces, gain, w_packed):
    rows = 128
    return pl.pallas_call(
        front_kernel,
        grid=(TOK // rows,),
        out_shape=(
            jax.ShapeDtypeStruct((TOK, D), BF16),
            jax.ShapeDtypeStruct((TOK, D), BF16),
            jax.ShapeDtypeStruct((TOK, 1), F32),
            jax.ShapeDtypeStruct((COLS, LATC, TOK), BF16),
        ),
        in_specs=[
            pl.BlockSpec(memory_space=pltpu.SMEM),
            pl.BlockSpec((4, 2, rows, FEAT), lambda j: (0, 0, j, 0)),
            pl.BlockSpec((1, D), lambda j: (0, 0)),
            pl.BlockSpec((D, 128), lambda j: (0, 6)),
        ],
        out_specs=(
            pl.BlockSpec((rows, D), lambda j: (j, 0)),
            pl.BlockSpec((rows, D), lambda j: (j, 0)),
            pl.BlockSpec((rows, 1), lambda j: (j, 0)),
            pl.BlockSpec((COLS, LATC, rows), lambda j: (0, 0, j)),
        ),
        compiler_params=pltpu.CompilerParams(vmem_limit_bytes=60 * MIB),
        cost_estimate=pl.CostEstimate(flops=TOK * D * 256, bytes_accessed=MIB, transcendentals=0),
    )(smem_values(col), pieces, gain.reshape(1, D), w_packed)


def half_turn():
    source = lax.broadcasted_iota(jnp.int32, (2 * ROPE, 2 * ROPE), 0)
    target = lax.broadcasted_iota(jnp.int32, (2 * ROPE, 2 * ROPE), 1)
    half = ROPE // 2
    first = target % ROPE < half
    value = jnp.where(
        first & (source == target + half),
        -1.0,
        jnp.where((target % ROPE >= half) & (source == target - half), 1.0, 0.0),
    )
    return value.astype(BF16)


def query_kernel(own_ref, normed_ref, w_ref, cos_ref, sin_ref, o0, o1, o2, o3, blocks):
    normed = normed_ref[...]
    w_rope = w_ref[:, 2 * NOPE :]
    turned = matmul(w_rope, half_turn()).astype(BF16)
    rope = matmul(normed, w_rope) * cos_ref[...] + matmul(normed, turned) * sin_ref[...]
    rope = rope.astype(BF16)
    nope = matmul(normed, w_ref[:, : 2 * NOPE]).astype(BF16)
    blank = jnp.zeros((BLK, QKP - QK), BF16)
    for h in range(2):
        for m in range(MICRO):
            rows = slice(m * BLK, (m + 1) * BLK)
            blocks[2 * h + m, :, :NOPE] = nope[rows, h * NOPE : (h + 1) * NOPE]
            blocks[2 * h + m, :, NOPE:QK] = rope[rows, h * ROPE : (h + 1) * ROPE]
            blocks[2 * h + m, :, QK:] = blank
    for j, ref in enumerate((o0, o1, o2, o3)):
        ref[...] = blocks[own_ref[0] ^ j]


def project_query(own, normed, w_packed, cos_wide, sin_wide):
    def whole(shape):
        return pl.BlockSpec(shape, lambda i: (0, 0))

    return pl.pallas_call(
        query_kernel,
        grid=(1,),
        out_shape=[jax.ShapeDtypeStruct((BLK, QKP), BF16)] * QUART,
        in_specs=[
            pl.BlockSpec(memory_space=pltpu.SMEM),
            whole((TOK, D)),
            whole((D, 2 * QK)),
            whole((TOK, 2 * ROPE)),
            whole((TOK, 2 * ROPE)),
        ],
        out_specs=[whole((BLK, QKP))] * QUART,
        scratch_shapes=[pltpu.VMEM((QUART, BLK, QKP), BF16)],
        compiler_params=pltpu.CompilerParams(vmem_limit_bytes=60 * MIB),
        cost_estimate=pl.CostEstimate(flops=TOK * D * 256, bytes_accessed=MIB, transcendentals=0),
    )(smem_values(own), normed, w_packed, cos_wide, sin_wide)


def query_back_kernel(own_ref, b0, b1, b2, b3, cos_ref, sin_ref, out_ref, blocks):
    turn = half_turn()
    for j, ref in enumerate((b0, b1, b2, b3)):
        blocks[own_ref[0] ^ j] = ref[...]
    for m in range(MICRO):
        rows = slice(m * BLK, (m + 1) * BLK)
        for h in range(2):
            out_ref[rows, h * NOPE : (h + 1) * NOPE] = blocks[2 * h + m, :, :NOPE]
        rope = jnp.concatenate([blocks[m, :, NOPE:QK], blocks[2 + m, :, NOPE:QK]], axis=1)
        rope = rope.astype(F32) * cos_ref[rows, :] + matmul_nt(rope, turn) * sin_ref[rows, :]
        out_ref[rows, 2 * NOPE :] = rope.astype(BF16)


def query_back(own, blocks, cos_wide, sin_wide):
    vmem = pl.BlockSpec(memory_space=pltpu.VMEM)
    return pl.pallas_call(
        query_back_kernel,
        out_shape=jax.ShapeDtypeStruct((TOK, 2 * QK), BF16),
        in_specs=[pl.BlockSpec(memory_space=pltpu.SMEM)] + [vmem] * 6,
        out_specs=vmem,
        scratch_shapes=[pltpu.VMEM((QUART, BLK, QKP), BF16)],
        compiler_params=pltpu.CompilerParams(vmem_limit_bytes=60 * MIB),
        cost_estimate=pl.CostEstimate(flops=TOK * D * 16, bytes_accessed=MIB, transcendentals=0),
    )(smem_values(own), *blocks, cos_wide, sin_wide)


def expand_kernel(latent_ref, cos_ref, sin_ref, gain_ref, w_ref, normed_ref, out_ref):
    c = latent_ref[:KVL, :].astype(F32)
    scale = lax.rsqrt(jnp.mean(c * c, axis=0, keepdims=True) + EPS)
    normed = (c * scale * gain_ref[...]).astype(BF16)
    normed_ref[...] = normed
    expanded = matmul_tn(normed, w_ref[...]).astype(BF16)
    half = ROPE // 2
    a = latent_ref[KVL : KVL + half, :].astype(F32)
    b = latent_ref[KVL + half :, :].astype(F32)
    cos, sin = cos_ref[...], sin_ref[...]
    rope = jnp.concatenate(
        [a * cos - b * sin, a * sin + b * cos, jnp.zeros((QKP - QK, TOK), F32)], axis=0
    )
    rope = rope.T.astype(BF16)
    for h in range(2):
        key = h * (NOPE + VDIM)
        value = key + NOPE
        for m in range(MICRO):
            for core in range(2):
                rows = slice(m * BLK + core * HALF, m * BLK + (core + 1) * HALF)
                for chip in range(2):
                    at = 8 * h + 4 * m + 2 * chip + core
                    out_ref[at, :, :VDIM] = expanded[rows, value : value + VDIM]
                    out_ref[at, :, VDIM : VDIM + NOPE] = expanded[rows, key : key + NOPE]
                    out_ref[at, :, VDIM + NOPE :] = rope[rows, :]


def expand(latent_t, cos_t, sin_t, gain, w_expand):
    return pl.pallas_call(
        expand_kernel,
        out_shape=(
            jax.ShapeDtypeStruct((KVL, TOK), BF16),
            jax.ShapeDtypeStruct((ROWS, HALF, PACK), BF16),
        ),
        compiler_params=pltpu.CompilerParams(vmem_limit_bytes=24 * MIB),
        cost_estimate=pl.CostEstimate(flops=TOK * D * 256, bytes_accessed=MIB, transcendentals=0),
    )(latent_t, cos_t, sin_t, gain.reshape(KVL, 1), w_expand)


def latent_back_kernel(
    pack_ref, latent_ref, cos_ref, sin_ref, gain_ref, w_ref, d_exp_ref, d_latent_ref, gg_ref
):
    rope = [None] * (2 * MICRO)
    for h in range(2):
        for m in range(MICRO):
            for core in range(2):
                at = 8 * h + 4 * m + core
                part = pack_ref[at].astype(F32) + pack_ref[at + 2].astype(F32)
                rows = slice(m * BLK + core * HALF, m * BLK + (core + 1) * HALF)
                key = h * (NOPE + VDIM)
                d_exp_ref[rows, key : key + NOPE] = part[:, VDIM : VDIM + NOPE].astype(BF16)
                d_exp_ref[rows, key + NOPE : key + NOPE + VDIM] = part[:, :VDIM].astype(BF16)
                piece = part[:, VDIM + NOPE :]
                at = 2 * m + core
                rope[at] = piece if h == 0 else rope[at] + piece
    rope = jnp.concatenate(rope, axis=0).T
    half = ROPE // 2
    a, b = rope[:half], rope[half:ROPE]
    cos, sin = cos_ref[...], sin_ref[...]
    d_latent_ref[KVL : KVL + half, :] = (a * cos + b * sin).astype(BF16)
    d_latent_ref[KVL + half :, :] = (b * cos - a * sin).astype(BF16)
    d_normed = matmul_nt(w_ref[...], d_exp_ref[...])
    c = latent_ref[:KVL, :].astype(F32)
    scale = lax.rsqrt(jnp.mean(c * c, axis=0, keepdims=True) + EPS)
    gg_ref[...] = jnp.sum(d_normed * c * scale, axis=1, keepdims=True)
    weighted = d_normed * gain_ref[...]
    inner = jnp.mean(weighted * c, axis=0, keepdims=True)
    d_latent_ref[:KVL, :] = (scale * weighted - c * (scale * scale * scale) * inner).astype(BF16)


def latent_back(pack, latent_t, cos_t, sin_t, gain, w_expand):
    return pl.pallas_call(
        latent_back_kernel,
        out_shape=(
            jax.ShapeDtypeStruct((TOK, 2 * (NOPE + VDIM)), BF16),
            jax.ShapeDtypeStruct((LAT, TOK), BF16),
            jax.ShapeDtypeStruct((KVL, 1), F32),
        ),
        compiler_params=pltpu.CompilerParams(vmem_limit_bytes=60 * MIB),
        cost_estimate=pl.CostEstimate(flops=TOK * D * 256, bytes_accessed=MIB, transcendentals=0),
    )(pack, latent_t, cos_t, sin_t, gain.reshape(KVL, 1), w_expand)


def hidden_kernel(
    own_ref, mid_ref, grad_ref, gate_ref, spread_ref, wg_ref, wu_ref, wd_ref, out_ref, turned_ref
):
    mid = mid_ref[...]
    pre = matmul(mid, wg_ref[...])
    up = matmul(mid, wu_ref[...])
    back = matmul(grad_ref[...], wd_ref[...])
    gate = matmul(gate_ref[...], spread_ref[...])
    sig = 0.5 + 0.5 * jnp.tanh(0.5 * pre)
    act = pre * sig
    back = back * gate
    out_ref[0] = (back * up * (sig * (1.0 + pre * (1.0 - sig)))).astype(BF16)
    out_ref[1] = (back * act).astype(BF16)
    out_ref[2] = (act * up * gate).astype(BF16)
    for i in range(3):
        r = jnp.minimum(3 * pl.program_id(0) + i, ROWS - 1)
        turned_ref[lanes(place_of(own_ref[0] ^ r)), :] = mid_ref[:, lanes(r)].T


def hidden(row, mid, grad, gates, spread, weights):
    whole = pl.BlockSpec((TOK, D), lambda j: (0, 0))
    parts = HID // BLK

    def weight(at):
        return pl.BlockSpec((D, BLK), lambda j: (0, at * parts + j))

    return pl.pallas_call(
        hidden_kernel,
        grid=(parts,),
        out_shape=(
            jax.ShapeDtypeStruct((3, TOK, HID), BF16),
            jax.ShapeDtypeStruct((D, TOK), BF16),
        ),
        in_specs=[
            pl.BlockSpec(memory_space=pltpu.SMEM),
            whole,
            whole,
            pl.BlockSpec(gates.shape, lambda j: (0, 0)),
            pl.BlockSpec((spread.shape[0], BLK), lambda j: (0, j)),
            weight(0),
            weight(1),
            weight(2),
        ],
        out_specs=(
            pl.BlockSpec((3, TOK, BLK), lambda j: (0, 0, j)),
            pl.BlockSpec((D, TOK), lambda j: (0, 0)),
        ),
        compiler_params=pltpu.CompilerParams(vmem_limit_bytes=60 * MIB),
        cost_estimate=pl.CostEstimate(
            flops=2 * TOK * D * HID * 3, bytes_accessed=32 * MIB, transcendentals=TOK * HID
        ),
    )(smem_values(row), mid, grad, gates, spread, weights, weights, weights)


def mid_grad_kernel(hid_ref, w_ref, out_ref):
    out = matmul_nt(hid_ref[0], w_ref[:, :HID]) + matmul_nt(hid_ref[1], w_ref[:, HID:])
    out_ref[...] = out.astype(BF16)


def mid_grad(hid, weights):
    return pl.pallas_call(
        mid_grad_kernel,
        grid=(4,),
        out_shape=jax.ShapeDtypeStruct((TOK, D), BF16),
        in_specs=[
            pl.BlockSpec((2, TOK, HID), lambda j: (0, 0, 0)),
            pl.BlockSpec((D // 4, 2 * HID), lambda j: (j, 0)),
        ],
        out_specs=pl.BlockSpec((TOK, D // 4), lambda j: (0, j)),
        compiler_params=pltpu.CompilerParams(vmem_limit_bytes=60 * MIB),
        cost_estimate=pl.CostEstimate(
            flops=2 * TOK * D * HID * 2, bytes_accessed=20 * MIB, transcendentals=0
        ),
    )(hid, weights)


def output_kernel(col_ref, hid_ref, w_ref, residual_ref, out_ref):
    out_ref[0] = matmul_nt(hid_ref[0], w_ref[...]).astype(BF16)
    own = pl.ds(pl.multiple_of(col_ref[0] * OWN, OWN), OWN)
    out_ref[0, own, :] = (
        matmul_nt(hid_ref[0, own, :], w_ref[...]) + residual_ref[...]
    ).astype(BF16)


def output(col, hid, weights, residual):
    return pl.pallas_call(
        output_kernel,
        grid=(COLS,),
        out_shape=jax.ShapeDtypeStruct((COLS, TOK, FEAT), BF16),
        in_specs=[
            pl.BlockSpec(memory_space=pltpu.SMEM),
            pl.BlockSpec((1, TOK, HID), lambda j: (2, 0, 0)),
            pl.BlockSpec((FEAT, HID), lambda j: (j, 2)),
            pl.BlockSpec((OWN, FEAT), lambda j: (0, j)),
        ],
        out_specs=pl.BlockSpec((1, TOK, FEAT), lambda j: (j, 0, 0)),
        compiler_params=pltpu.CompilerParams(vmem_limit_bytes=60 * MIB),
        cost_estimate=pl.CostEstimate(
            flops=TOK * D * HID // 8, bytes_accessed=MIB, transcendentals=0
        ),
    )(col.astype(jnp.int32).reshape(1), hid, weights, residual)


def mid_kernel(parts_ref, inputs_ref, gain_ref, residual_ref, scale_ref, normed_ref):
    total = inputs_ref[...].astype(F32)
    for c in range(COLS):
        total = total + parts_ref[c].astype(F32)
    scale = inverse_rms(total)
    residual_ref[...] = total
    scale_ref[...] = scale
    normed = (total * scale * gain_ref[...]).astype(BF16)
    for c in range(COLS):
        normed_ref[c] = normed


def mid(parts, inputs, gain):
    return pl.pallas_call(
        mid_kernel,
        out_shape=(
            jax.ShapeDtypeStruct((OWN, D), F32),
            jax.ShapeDtypeStruct((OWN, 1), F32),
            jax.ShapeDtypeStruct((COLS, OWN, D), BF16),
        ),
        compiler_params=pltpu.CompilerParams(vmem_limit_bytes=20 * MIB),
        cost_estimate=pl.CostEstimate(
            flops=OWN * D * 16, bytes_accessed=5 * MIB, transcendentals=0
        ),
    )(parts, inputs, gain.reshape(1, D))


def mid_back_kernel(
    parts_ref, residual_ref, scale_ref, grad_ref, gain_ref, out_ref, low_ref, gain_grad_ref
):
    d_mid = parts_ref[0].astype(F32)
    for c in range(1, COLS):
        d_mid = d_mid + parts_ref[c].astype(F32)
    residual, scale = residual_ref[...], scale_ref[...]
    gain_grad_ref[...] = jnp.sum(d_mid * residual * scale, axis=0, keepdims=True)
    out = grad_ref[...].astype(F32) + norm_backward(d_mid, residual, scale, gain_ref[...])
    out_ref[...] = out
    low = out.astype(BF16)
    for c in range(COLS):
        low_ref[c] = low


def mid_back(parts, residual, scale, grad, gain):
    return pl.pallas_call(
        mid_back_kernel,
        out_shape=(
            jax.ShapeDtypeStruct((OWN, D), F32),
            jax.ShapeDtypeStruct((COLS, OWN, D), BF16),
            jax.ShapeDtypeStruct((1, D), F32),
        ),
        compiler_params=pltpu.CompilerParams(vmem_limit_bytes=20 * MIB),
        cost_estimate=pl.CostEstimate(
            flops=OWN * D * 24, bytes_accessed=5 * MIB, transcendentals=0
        ),
    )(parts, residual, scale, grad, gain.reshape(1, D))


def input_back_kernel(
    col_ref, dq_ref, dl_ref, wq_ref, wl_ref, x_ref, scale_ref, gain_ref, own_ref, out_ref, gg_ref
):
    step = pl.program_id(0)
    d_in = matmul_nt(dq_ref[...], wq_ref[...]) + matmul_nt(dl_ref[...], wl_ref[...])
    x, scale = x_ref[...].astype(F32), scale_ref[...]
    gain_grad = jnp.sum(d_in * x * scale, axis=0, keepdims=True)

    @pl.when(step == 0)
    def _():
        gg_ref[...] = gain_grad

    @pl.when(step > 0)
    def _():
        gg_ref[...] += gain_grad

    out = norm_backward(d_in, x, scale, gain_ref[...])
    for half in range(2):
        mine = (col_ref[0] == 2 * step + half).astype(F32)
        rows = slice(half * OWN, (half + 1) * OWN)
        part = (out[rows] + mine * own_ref[...]).astype(BF16)
        for c in range(COLS):
            out_ref[c, rows, :] = part[:, c * FEAT : (c + 1) * FEAT]


def input_back(col, d_query, d_latent, w_packed, inputs, scale, gain, own):
    rows = 2 * OWN
    widths = (d_query.shape[1], d_latent.shape[1])
    return pl.pallas_call(
        input_back_kernel,
        grid=(TOK // rows,),
        out_shape=(
            jax.ShapeDtypeStruct((COLS, TOK, FEAT), BF16),
            jax.ShapeDtypeStruct((1, D), F32),
        ),
        in_specs=[
            pl.BlockSpec(memory_space=pltpu.SMEM),
            pl.BlockSpec((rows, widths[0]), lambda j: (j, 0)),
            pl.BlockSpec((rows, widths[1]), lambda j: (j, 0)),
            pl.BlockSpec((D, widths[0]), lambda j: (0, 0)),
            pl.BlockSpec((D, widths[1]), lambda j: (0, 6)),
            pl.BlockSpec((rows, D), lambda j: (j, 0)),
            pl.BlockSpec((rows, 1), lambda j: (j, 0)),
            pl.BlockSpec((1, D), lambda j: (0, 0)),
            pl.BlockSpec((OWN, D), lambda j: (0, 0)),
        ],
        out_specs=(
            pl.BlockSpec((COLS, rows, FEAT), lambda j: (0, j, 0)),
            pl.BlockSpec((1, D), lambda j: (0, 0)),
        ),
        compiler_params=pltpu.CompilerParams(vmem_limit_bytes=60 * MIB),
        cost_estimate=pl.CostEstimate(
            flops=2 * TOK * D * 640, bytes_accessed=9 * MIB, transcendentals=0
        ),
    )(
        smem_values(col),
        d_query,
        d_latent,
        w_packed,
        w_packed,
        inputs,
        scale,
        gain.reshape(1, D),
        own,
    )


def send_grad_kernel(mid_ref, grad_ref, hid_ref, out_ref):
    @pl.when(pl.program_id(0) < 2)
    def _():
        out_ref[...] = matmul(mid_ref[...], hid_ref[0]).astype(BF16)

    @pl.when(pl.program_id(0) == 2)
    def _():
        out_ref[...] = matmul(grad_ref[...], hid_ref[0]).astype(BF16)


def keep_grad_kernel(mid_ref, grad_ref, hid_ref, got_ref, *out_refs):
    def store(lhs_ref):
        out = matmul(lhs_ref[...], hid_ref[0]) + got_ref[...].astype(F32)
        first = 0
        for ref in out_refs:
            rows = ref.shape[0]
            ref[...] = out[first : first + rows].astype(BF16)
            first += rows

    @pl.when(pl.program_id(0) < 2)
    def _():
        store(mid_ref)

    @pl.when(pl.program_id(0) == 2)
    def _():
        store(grad_ref)


def send_grads(z, mid_t, grad_t, hid):
    rows = D // 4
    whole = pl.BlockSpec((rows, TOK), lambda s: (2 + z, 0))
    return pl.pallas_call(
        send_grad_kernel,
        grid=(3,),
        out_shape=jax.ShapeDtypeStruct((rows, WIDE), BF16),
        in_specs=[whole, whole, pl.BlockSpec((1, TOK, HID), lambda s: (s, 0, 0))],
        out_specs=pl.BlockSpec((rows, HID), lambda s: (0, s)),
        compiler_params=pltpu.CompilerParams(vmem_limit_bytes=60 * MIB),
        cost_estimate=pl.CostEstimate(
            flops=TOK * D * HID // 32, bytes_accessed=MIB, transcendentals=0
        ),
    )(mid_t, grad_t, hid)


def keep_grads(z, mid_t, grad_t, hid, got):
    rows = D // 4
    whole = pl.BlockSpec((rows, TOK), lambda s: (z, 0))
    heights = (LANES, LANES, CUT, CUT, LANES)
    return pl.pallas_call(
        keep_grad_kernel,
        grid=(3,),
        out_shape=[jax.ShapeDtypeStruct((height, WIDE), BF16) for height in heights],
        in_specs=[
            whole,
            whole,
            pl.BlockSpec((1, TOK, HID), lambda s: (s, 0, 0)),
            pl.BlockSpec((rows, HID), lambda s: (0, s)),
        ],
        out_specs=[pl.BlockSpec((h, HID), lambda s: (0, s)) for h in heights],
        compiler_params=pltpu.CompilerParams(vmem_limit_bytes=60 * MIB),
        cost_estimate=pl.CostEstimate(
            flops=TOK * D * HID // 32, bytes_accessed=MIB, transcendentals=0
        ),
    )(mid_t, grad_t, hid, got)


def rotary_tables(parents, row):
    seg = jnp.maximum(row - (TRUNK // BLK - 1), 0).astype(jnp.int32)
    depths = ancestor_depths(parents, seg.reshape(1))
    starts = jnp.where(seg > 0, TRUNK + BLK * depths, BLK * row)
    positions = (starts[:, None] + jnp.arange(BLK, dtype=jnp.int32)[None, :]).reshape(TOK)
    frequency = THETA ** (-jnp.arange(ROPE // 2, dtype=F32) / (ROPE // 2))
    angles = positions.astype(F32)[:, None] * frequency[None, :]
    cos_table, sin_table = jnp.cos(angles), jnp.sin(angles)
    cos_wide, sin_wide = jnp.tile(cos_table, (1, 4)), jnp.tile(sin_table, (1, 4))
    return cos_table.T, sin_table.T, cos_wide, sin_wide


def pack_hidden(shared, routed):
    rows = shared.shape[0]
    return jnp.concatenate(
        [
            shared,
            jnp.swapaxes(routed, 0, 1).reshape(rows, EXPERTS * ROUTED),
            jnp.zeros((rows, HID - SHARED - EXPERTS * ROUTED), routed.dtype),
        ],
        axis=1,
    )


def local(
    tokens,
    out_grad,
    parents,
    routes,
    gates,
    norm_in,
    w_query,
    w_latent,
    norm_latent,
    w_expand,
    w_output,
    norm_mid,
    w_shared_gate,
    w_shared_up,
    w_shared_down,
    w_expert_gate,
    w_expert_up,
    w_expert_down,
):
    row = lax.axis_index("row")
    col = lax.axis_index("col")
    group = row // QUART
    own_start = col * OWN
    gain_in = norm_in.astype(F32)
    gain_latent = norm_latent.astype(F32)
    gain_mid = norm_mid.astype(F32)
    heads = 2

    query_pack = w_query.reshape(D // ROWS, heads, QK)
    attn_pack = jnp.concatenate(
        [
            query_pack[:, :, :NOPE].reshape(D // ROWS, heads * NOPE),
            query_pack[:, :, NOPE:].reshape(D // ROWS, heads * ROPE),
            w_expand.reshape(KVL // ROWS, 4, 128).transpose(1, 0, 2).reshape(D // ROWS, 128),
            w_output.T,
            w_latent,
            jnp.zeros((D // ROWS, 128 - LATC), BF16),
        ],
        axis=1,
    )
    ffn_pack = jnp.concatenate(
        [
            pack_hidden(w_shared_gate, w_expert_gate),
            pack_hidden(w_shared_up, w_expert_up),
            pack_hidden(w_shared_down.T, jnp.swapaxes(w_expert_down, 1, 2)),
        ],
        axis=1,
    )
    attn_pair, input_pair, ffn_pack = together(
        pair_up(attn_pack, "row"), pair_up(tokens.reshape(TOK, FEAT), "col"), ffn_pack
    )
    line_groups = [[2 * y + z for y in range(4)] for z in range(2)]
    input_copies = jnp.broadcast_to(input_pair[None], (4,) + input_pair.shape)
    attn_ring, input_ring, ffn_pack, ffn_other, tables = together(
        ring_up(attn_pair, "row"),
        swap(input_copies, "col", line_groups),
        ffn_pack,
        trade(ffn_pack, "row", 8),
        rotary_tables(parents, row),
    )
    cos_t, sin_t, cos_wide, sin_wide = tables
    ffn_near = near_shards(ffn_pack)
    attn_full = finish_rows(attn_ring, row)
    expand_full = attn_full[:, 384:512].reshape(ROWS, 4, KVL // ROWS, 128)
    expand_full = expand_full.transpose(0, 2, 1, 3).reshape(KVL, heads * (NOPE + VDIM))

    inputs, normed_in, scale_in, latent_parts = front(col, input_ring, gain_in, attn_full)
    query = project_query(group, normed_in, attn_full, cos_wide, sin_wide)
    latent_t, query, normed_in, ffn_near = together(
        swap(latent_parts, "col"), query, normed_in, ffn_near
    )
    latent_t = latent_t.reshape(LAT, TOK)
    latent_normed_t, pack = expand(latent_t, cos_t, sin_t, gain_latent, expand_full)
    pack, query, ffn_near, out_grad, ffn_other = together(
        pack, query, ffn_near, out_grad, ffn_other
    )
    near, query, ffn_cut, grad_copies = together(
        swap(pack, "row"),
        trade_quarter(query),
        cut_near(ffn_near),
        jnp.broadcast_to(out_grad.reshape(1, TOK, FEAT), (COLS, TOK, FEAT)),
    )
    grad_ring = swap(grad_copies, "col")
    ffn_far = far_halves(ffn_cut)
    far = trade(near, "row", 1)

    meta = jnp.concatenate([pick(parents, group % MICRO), smem_values(row % QUART, group)])
    *attended_own, lse = attend(meta, query, near, far)
    attended_own, lse, ffn_far = together(attended_own, lse, ffn_far)
    attended_parts, grad_ring, ffn_far, ffn_other = together(
        trade_quarter(attended_own), grad_ring, ffn_far, ffn_other
    )
    attended, attn_parts = project(group, attended_parts, attn_full)
    grad_full, grad_t = features(row, grad_ring)

    def both_cores(pieces):
        far_pieces = [(trade(v, "row", 1), apart ^ 1, first) for v, apart, first in pieces]
        return list(pieces) + far_pieces

    pieces = both_cores(
        [(ffn_pack, 0, 0), (ffn_near[0], 2, 0), (ffn_near[1], 6, 0)]
        + [(ffn_far[0], 4, 0), (ffn_far[1], 4, CUT)]
    )
    own_inputs = lax.dynamic_slice_in_dim(inputs, own_start, OWN, 0)
    ffn_full = put_shards(row, None, pieces)
    attn_parts, grad_full, grad_t, ffn_full = together(
        swap(attn_parts, "col"), grad_full, grad_t, ffn_full
    )
    named = routes.reshape(TOK, TOPK, 1) == jnp.arange(EXPERTS, dtype=jnp.int32)
    gate_of = jnp.sum(jnp.where(named, gates.reshape(TOK, TOPK, 1), 0.0), axis=1)
    gate_of = jnp.concatenate(
        [jnp.ones((TOK, 1), F32), gate_of, jnp.zeros((TOK, 15 - EXPERTS), F32)], axis=1
    )
    gate_high = gate_of.astype(BF16)
    gate_low = (gate_of - gate_high.astype(F32)).astype(BF16)
    gate_parts = jnp.concatenate([gate_high, gate_low], axis=1)
    unit = jnp.arange(HID, dtype=jnp.int32)
    expert = jnp.where(unit < SHARED, 0, 1 + (unit - SHARED) // ROUTED)
    spread = (expert[None, :] == jnp.arange(16, dtype=jnp.int32)[:, None]).astype(BF16)
    spread = jnp.concatenate([spread, spread], axis=0)
    attn_parts, gate_parts, spread = together(attn_parts, gate_parts, spread)
    residual, scale_mid, normed_mid = mid(attn_parts, own_inputs, gain_mid)
    normed_mid, other_near = together(normed_mid, near_shards(ffn_other))
    pieces = both_cores([(ffn_other, 8, 0), (other_near[0], 10, 0), (other_near[1], 14, 0)])
    ffn_full = put_shards(row, ffn_full, pieces)
    normed_mid, ffn_full, other_far = together(
        swap(normed_mid, "col"), ffn_full, far_halves(cut_near(other_near))
    )
    normed_mid = normed_mid.reshape(TOK, D)
    pieces = both_cores([(other_far[0], 12, 0), (other_far[1], 12, CUT)])
    ffn_full = put_shards(row, ffn_full, pieces)

    hid, normed_t = hidden(row, normed_mid, grad_full, gate_parts, spread, ffn_full)
    mid_parts = mid_grad(hid, ffn_full)
    hid, normed_t, mid_parts = together(hid, normed_t, mid_parts)
    send = send_grads(1, normed_t, grad_t, hid)
    blocks = keep_grads(1, normed_t, grad_t, hid, trade(send, "row", 1))
    send = send_grads(0, normed_t, grad_t, after(hid, blocks))
    halves = sum_opposite(blocks)
    mid_parts, hid, blocks, send, normed_t = together(
        swap(mid_parts.reshape(COLS, OWN, D), "col"), hid, blocks, send, normed_t
    )
    own_grad = lax.dynamic_slice_in_dim(grad_full, own_start, OWN, 0)
    d_residual, d_low, mid_gain = mid_back(mid_parts, residual, scale_mid, own_grad, gain_mid)
    d_low, hid, send, halves, blocks = together(d_low, hid, send, halves, blocks)
    block, sides = blocks[0], with_opposite(blocks, halves)
    d_low, out_parts, sides, own_blocks = together(
        swap(d_low, "col"),
        output(col, hid, ffn_full, residual),
        sum_neighbours(sides),
        keep_grads(0, normed_t, grad_t, hid, trade(send, "row", 1)),
    )
    other_sum = add_low(block.astype(F32) + sides[0].astype(F32), sides[1])

    d_attended = trade_quarter(project_back(group, d_low, attn_full))
    d_attended, other_sum, out_parts = together(d_attended, other_sum, out_parts)
    *d_query, d_near, d_far = attend_back(
        meta, query, attended_own, d_attended, near, far, lse
    )
    d_query, d_near, d_far, halves, other_low, out_parts, out_left = together(
        d_query,
        d_near,
        d_far,
        sum_opposite(own_blocks),
        trade(other_sum[:CUT], "row", 8),
        out_parts,
        collect_y(out_parts, col // 2, 1),
    )
    d_far = trade(d_far, "row", 1)
    d_query, d_pack = together(trade_quarter(d_query), add_low(d_near, d_far))
    d_query = query_back(group, d_query, cos_wide, sin_wide)
    d_pack, sides, out_right, out_parts, d_query, attn_grads = together(
        swap(d_pack, "row"),
        with_opposite(own_blocks, halves),
        collect_y(out_parts, col // 2, 3),
        out_parts,
        d_query,
        attn_weight_grads(row, normed_in, d_query, d_low.reshape(TOK, D), attended),
    )
    sides = sum_neighbours(sides)

    d_expanded, d_latent, latent_gain = latent_back(
        d_pack, latent_t, cos_t, sin_t, gain_latent, expand_full
    )
    other_high = trade(after(other_sum, d_latent)[CUT:], "row", 8)
    d_latent, attn_grads, out_far, out_own = together(
        swap(d_latent.reshape(COLS, LATC, TOK), "col"),
        add_low(attn_grads[0], trade(attn_grads[1], "row", 1)),
        collect_y(out_parts, col // 2, 2),
        collect_y(out_parts, col // 2, 0),
    )
    out_parts = (out_own, out_left, out_far, out_right)
    d_latent = jnp.sum(d_latent.astype(F32), axis=0).astype(BF16)
    d_latent = jnp.concatenate([d_latent, jnp.zeros((128 - LATC, TOK), BF16)], axis=0).T

    d_tokens, in_gain = input_back(
        col, d_query, d_latent, attn_full, inputs, scale_in, gain_in, d_residual
    )
    d_tokens, in_gain, sides, other_high = together(d_tokens, in_gain, sides, other_high)

    gain = jnp.concatenate([in_gain.reshape(D), latent_gain.reshape(KVL), mid_gain.reshape(D)])
    d_tokens, d_latent = together(d_tokens, d_latent)
    latent_grads = latent_weight_grads(row, normed_in, d_latent, latent_normed_t, d_expanded)
    latent_grads = add_low(latent_grads[0], trade(latent_grads[1], "row", 1))
    ffn_grads = own_blocks[0].astype(F32) + sides[0].astype(F32) + sides[1].astype(F32)
    other_sum = jnp.concatenate([other_low, other_high], axis=0)
    ffn_grads = ffn_grads + other_sum.astype(F32)

    def unpack(at):
        part = ffn_grads[:, at * HID : (at + 1) * HID]
        routed = part[:, SHARED : SHARED + EXPERTS * ROUTED]
        return part[:, :SHARED], routed.reshape(-1, EXPERTS, ROUTED)

    grad_shared_gate, grad_expert_gate = unpack(0)
    grad_shared_up, grad_expert_up = unpack(1)
    grad_shared_down, grad_expert_down = unpack(2)
    ffn_outs = (
        grad_shared_gate,
        grad_shared_up,
        grad_shared_down.T,
        jnp.swapaxes(grad_expert_gate, 0, 1),
        jnp.swapaxes(grad_expert_up, 0, 1),
        grad_expert_down.transpose(1, 2, 0),
    )
    d_tokens, attn_grads, latent_grads, out_parts, gain, ffn_outs = together(
        swap(d_tokens, "col"),
        [reduce_x(attn_grads, j) for j in range(4)],
        latent_grads,
        out_parts,
        gain,
        ffn_outs,
    )
    latent_grads = [reduce_x(latent_grads, j) for j in range(4)]
    attn_grads = reduce_z(attn_grads, latent_grads)
    layer_out = collect_z(out_parts, col % 2).astype(BF16)
    input_grad = jnp.sum(d_tokens.astype(F32), axis=0).astype(BF16)
    gain = share(gain.astype(BF16).reshape(-1, 128), ("row", "col"), ROWS * COLS)
    gain, input_grad, attn_grads, layer_out = together(gain, input_grad, attn_grads, layer_out)
    gain = jnp.sum(gain.astype(F32), axis=0).reshape(-1)
    grad_query = jnp.concatenate(
        [
            attn_grads[:, : heads * NOPE].reshape(-1, heads, NOPE),
            attn_grads[:, heads * NOPE : heads * QK].reshape(-1, heads, ROPE),
        ],
        axis=-1,
    ).reshape(-1, heads * QK)
    grad_output = attn_grads[:, 384:640].T
    grad_expand = attn_grads[:, 640:768].reshape(4, KVL // ROWS, 128)
    grad_expand = grad_expand.transpose(1, 0, 2).reshape(KVL // ROWS, heads * (NOPE + VDIM))
    grad_latent = attn_grads[:, 768 : 768 + LATC]

    return (
        layer_out.reshape(MICRO, BLK, FEAT),
        input_grad.reshape(MICRO, BLK, FEAT),
        gain[:D],
        grad_query,
        grad_latent,
        gain[D : D + KVL],
        grad_expand,
        grad_output,
        gain[D + KVL :],
        *ffn_outs,
    )


def solution(mesh):
    in_specs = (
        P(None, "row", "col"),
        P(None, "row", "col"),
        P(),
        P(None, "row", None),
        P(None, "row", None),
        P(),
        P("row", "col"),
        P("row", "col"),
        P(),
        P("row", "col"),
        P("col", "row"),
        P(),
        P("row", "col"),
        P("row", "col"),
        P("col", "row"),
        P(None, "row", "col"),
        P(None, "row", "col"),
        P(None, "col", "row"),
    )
    out_specs = (
        P(None, "row", "col"),
        P(None, "row", "col"),
        P(),
        P("row", "col"),
        P("row", "col"),
        P(),
        P("row", "col"),
        P("col", "row"),
        P(),
        P("row", "col"),
        P("row", "col"),
        P("col", "row"),
        P(None, "row", "col"),
        P(None, "row", "col"),
        P(None, "col", "row"),
    )
    return jax.shard_map(local, mesh=mesh, in_specs=in_specs, out_specs=out_specs, check_vma=False)
```

```python
import functools

import jax
import jax.numpy as jnp
from jax import lax
from jax.experimental import pallas as pl
from jax.experimental.pallas import tpu as pltpu
from jax.sharding import PartitionSpec as P

D = 2048
NOPE = 128
ROPE = 64
QK = NOPE + ROPE
VDIM = 128
KVL = 512
TOPK = 6
EXPERTS = 8
MICRO = 2
TRUNK = 1024
BLK = 256
SEGS = 13
ROWS = 16
COLS = 8
TOK = MICRO * BLK
OWN = TOK // COLS
FEAT = D // COLS
QUART = 4
SHARED = 352
ROUTED = 176
HID = 1792
LAT = KVL + ROPE
HALF = BLK // 2
QKP = 256
PACK = VDIM + QKP
WIDE = 3 * HID
LANES = D // ROWS
CUT = LANES // 2
LATC = LAT // COLS
SCALE = QK**-0.5
EPS = 1e-06
THETA = 10000.0
NEG = -1e30
MIB = 1024 * 1024
F32 = jnp.float32
BF16 = jnp.bfloat16
NT = (((1,), (1,)), ((), ()))
TN = (((0,), (0,)), ((), ()))


def inverse_rms(values):
    return lax.rsqrt(jnp.mean(values * values, axis=-1, keepdims=True) + EPS)


def norm_backward(grad_out, values, inv_scale, norm_gain):
    weighted = grad_out * norm_gain
    inner = jnp.mean(weighted * values, axis=-1, keepdims=True)
    return inv_scale * weighted - values * (inv_scale * inv_scale * inv_scale) * inner


def matmul(a, b):
    return jnp.dot(a, b, preferred_element_type=F32)


def matmul_nt(a, b):
    return lax.dot_general(a, b, NT, preferred_element_type=F32)


def matmul_tn(a, b):
    return lax.dot_general(a, b, TN, preferred_element_type=F32)


def swap(values, axis, groups=None):
    return lax.all_to_all(values, axis, 0, 0, tiled=True, axis_index_groups=groups)


def share(values, axis, count):
    return swap(jnp.broadcast_to(values[None], (count,) + values.shape), axis)


def trade(values, axis, mask):
    count = ROWS if axis == "row" else COLS
    return lax.ppermute(values, axis, [(i, i ^ mask) for i in range(count)])


def after(values, *others):
    return lax.optimization_barrier((values,) + others)[0]


def together(*values):
    return lax.optimization_barrier(values)


def smem_values(*values):
    return jnp.stack([jnp.asarray(v, jnp.int32) for v in values])


def pick(values, index, axis=0):
    return lax.dynamic_index_in_dim(values, index, axis, keepdims=False)


def pair_up(shard, axis):
    return jnp.stack([shard, trade(shard, axis, 8 if axis == "row" else 1)])


def ring_up(pair, axis):
    return [pair] + [trade(pair, axis, j << 1) for j in (1, 2, 3)]


def sort_rows_kernel(own_ref, near_ref, far_ref, out_ref):
    for core, ref in ((0, near_ref), (1, far_ref)):
        for x in range(4):
            for z in range(2):
                out_ref[own_ref[0] ^ (8 * z + 2 * x + core)] = ref[x, z]


def finish_rows(ring, row):
    near = jnp.stack(ring)
    far = trade(near, "row", 1)
    vmem = pl.BlockSpec(memory_space=pltpu.VMEM)
    out = pl.pallas_call(
        sort_rows_kernel,
        out_shape=jax.ShapeDtypeStruct((ROWS,) + near.shape[2:], near.dtype),
        in_specs=[pl.BlockSpec(memory_space=pltpu.SMEM), vmem, vmem],
        out_specs=vmem,
        compiler_params=pltpu.CompilerParams(vmem_limit_bytes=16 * MIB),
        cost_estimate=pl.CostEstimate(flops=0, bytes_accessed=near.size, transcendentals=0),
    )(smem_values(row), near, far)
    return out.reshape(D, near.shape[3])


def place_of(apart):
    return ((apart & 1) << 3) | ((apart >> 3) << 2) | ((apart >> 1) & 3)


def lanes(at):
    return pl.ds(pl.multiple_of(at * LANES, LANES), LANES)


def features_kernel(own_ref, blocks_ref, out_ref, out_t_ref):
    for c in range(COLS):
        out_ref[:, c * FEAT : (c + 1) * FEAT] = blocks_ref[c]
    for r in range(ROWS):
        block = blocks_ref[r // 2, :, (r % 2) * LANES : (r % 2 + 1) * LANES]
        out_t_ref[lanes(place_of(own_ref[0] ^ r)), :] = block.T


def features(row, blocks):
    vmem = pl.BlockSpec(memory_space=pltpu.VMEM)
    return pl.pallas_call(
        features_kernel,
        out_shape=(
            jax.ShapeDtypeStruct((TOK, D), BF16),
            jax.ShapeDtypeStruct((D, TOK), BF16),
        ),
        in_specs=[pl.BlockSpec(memory_space=pltpu.SMEM), vmem],
        out_specs=(vmem, vmem),
        compiler_params=pltpu.CompilerParams(vmem_limit_bytes=60 * MIB),
        cost_estimate=pl.CostEstimate(flops=0, bytes_accessed=MIB, transcendentals=0),
    )(smem_values(row), blocks)


def near_shards(shard):
    return trade(shard, "row", 2), trade(shard, "row", 6)


def cut_near(near):
    return near[1][:CUT], near[0][CUT:]


def far_halves(parts):
    return trade(parts[0], "row", 2), trade(parts[1], "row", 6)


def put_kernel(places, own_ref, *refs):
    out_ref, sems = refs[-2:]
    copies = []
    for i, (apart, first) in enumerate(places):
        at = (own_ref[0] ^ apart) * LANES + first
        rows = pl.ds(pl.multiple_of(at, CUT), refs[i].shape[0])
        copy = pltpu.make_async_copy(refs[i], out_ref.at[rows], sems.at[i])
        copy.start()
        copies.append(copy)
    for copy in copies:
        copy.wait()


def put_shards(row, whole, pieces):
    values = [piece for piece, _, _ in pieces]
    places = [(apart, first) for _, apart, first in pieces]
    fresh = whole is None
    return pl.pallas_call(
        functools.partial(put_kernel, places),
        out_shape=jax.ShapeDtypeStruct((D, WIDE), BF16),
        in_specs=[pl.BlockSpec(memory_space=pltpu.SMEM)]
        + [pl.BlockSpec(memory_space=pltpu.VMEM)] * len(values)
        + ([] if fresh else [pl.BlockSpec(memory_space=pl.ANY)]),
        out_specs=pl.BlockSpec(memory_space=pl.ANY),
        scratch_shapes=[pltpu.SemaphoreType.DMA((len(values),))],
        input_output_aliases={} if fresh else {1 + len(values): 0},
        compiler_params=pltpu.CompilerParams(vmem_limit_bytes=60 * MIB),
        cost_estimate=pl.CostEstimate(flops=0, bytes_accessed=MIB, transcendentals=0),
    )(smem_values(row), *values, *([] if fresh else [whole]))


def sum_opposite(blocks):
    return trade(blocks[2], "row", 2), trade(blocks[3], "row", 6)


def add_low(a, b):
    return (a.astype(F32) + b.astype(F32)).astype(BF16)


def sides_kernel(b1_ref, b3_ref, h1_ref, h3_ref, left_ref, right_ref):
    left_ref[:CUT] = b1_ref[:CUT]
    left_ref[CUT:] = (b1_ref[CUT:].astype(F32) + h3_ref[...].astype(F32)).astype(BF16)
    right_ref[:CUT] = (b3_ref[:CUT].astype(F32) + h1_ref[...].astype(F32)).astype(BF16)
    right_ref[CUT:] = b3_ref[CUT:]


def with_opposite(blocks, halves):
    return pl.pallas_call(
        sides_kernel,
        out_shape=[jax.ShapeDtypeStruct((LANES, WIDE), BF16)] * 2,
        compiler_params=pltpu.CompilerParams(vmem_limit_bytes=60 * MIB),
        cost_estimate=pl.CostEstimate(flops=0, bytes_accessed=MIB, transcendentals=0),
    )(blocks[1], blocks[4], *halves)


def sum_neighbours(sides):
    return trade(sides[0], "row", 2), trade(sides[1], "row", 6)


def reduce_x(blocks, j):
    blocks = blocks.reshape((4, 2) + blocks.shape[1:])
    return trade(blocks[j], "row", j << 1) if j else blocks[0]


def reduce_z(*packs):
    sums = []
    for parts in packs:
        parts = [part.astype(F32) for part in parts]
        sums.append(parts[0] + parts[1] + (parts[2] + parts[3]))
    blocks = jnp.concatenate(sums, axis=-1).astype(BF16)
    return blocks[0].astype(F32) + trade(blocks[1], "row", 8).astype(F32)


def attn_grads_kernel(own_ref, x_ref, dq_ref, low_ref, att_ref, keep_ref, send_ref, out):
    out[:, :384] = matmul_tn(x_ref[...], dq_ref[...])
    out[:, 384:] = matmul_tn(low_ref[...], att_ref[...])
    core = own_ref[0] & 1
    keep_ref[0] = out[lanes(core), :].astype(BF16)
    send_ref[0] = out[lanes(1 - core), :].astype(BF16)


def latent_grads_kernel(own_ref, x_ref, dl_ref, lat_ref, de_ref, keep_ref, send_ref, out):
    out[:, 128:] = matmul_tn(x_ref[...], dl_ref[...])
    expand_grad = matmul(lat_ref[...], de_ref[...])
    for half in range(2):
        for i in range(4):
            rows = slice(half * LANES + 32 * i, half * LANES + 32 * (i + 1))
            part = expand_grad[32 * half : 32 * (half + 1), 128 * i : 128 * (i + 1)]
            out[rows, :128] = part
    core = own_ref[0] & 1
    keep_ref[0] = out[lanes(core), :].astype(BF16)
    send_ref[0] = out[lanes(1 - core), :].astype(BF16)


def place_pair(i, own):
    apart = i ^ (own[0] >> 1)
    return (apart & 3) * 2 + (apart >> 2), 0, 0


def weight_grad_pairs(kernel, width, row, ins, specs):
    block = pl.BlockSpec((1, LANES, width), place_pair)
    return pl.pallas_call(
        kernel,
        out_shape=[jax.ShapeDtypeStruct((ROWS // 2, LANES, width), BF16)] * 2,
        grid_spec=pltpu.PrefetchScalarGridSpec(
            num_scalar_prefetch=1,
            grid=(ROWS // 2,),
            in_specs=specs,
            out_specs=[block, block],
            scratch_shapes=[pltpu.VMEM((2 * LANES, width), F32)],
        ),
        compiler_params=pltpu.CompilerParams(vmem_limit_bytes=60 * MIB),
        cost_estimate=pl.CostEstimate(flops=TOK * D * 16, bytes_accessed=MIB, transcendentals=0),
    )(smem_values(row), *ins)


def whole_block(values):
    return pl.BlockSpec(values.shape, lambda i, own: (0, 0))


def attn_weight_grads(row, normed, d_query, d_low, attended):
    columns = pl.BlockSpec((TOK, 2 * LANES), lambda i, own: (0, i))
    specs = [columns, whole_block(d_query), columns, whole_block(attended)]
    ins = (normed, d_query, d_low, attended)
    return weight_grad_pairs(attn_grads_kernel, 640, row, ins, specs)


def latent_weight_grads(row, normed, d_latent, latent_t, d_expanded):
    columns = pl.BlockSpec((TOK, 2 * LANES), lambda i, own: (0, i))
    lines = pl.BlockSpec((2 * KVL // ROWS, TOK), lambda i, own: (i, 0))
    specs = [columns, whole_block(d_latent), lines, whole_block(d_expanded)]
    ins = (normed, d_latent, latent_t, d_expanded)
    return weight_grad_pairs(latent_grads_kernel, 256, row, ins, specs)


def collect_y(blocks, y, j):
    blocks = blocks.reshape((4, 2) + blocks.shape[1:])
    return trade(pick(blocks, y ^ j), "col", j << 1) if j else pick(blocks, y)


def collect_z(blocks, z):
    blocks = [block.astype(F32) for block in blocks]
    blocks = (blocks[0] + blocks[1] + (blocks[2] + blocks[3])).astype(BF16)
    got = trade(pick(blocks, 1 - z), "col", 1)
    return pick(blocks, z).astype(F32) + got.astype(F32)


def trade_quarter(blocks):
    return [blocks[0]] + [trade(blocks[j], "row", j << 2) for j in (1, 2, 3)]


def depth_kernel(parents_ref, seg_ref, out_ref):
    seg = seg_ref[0]
    for m in range(MICRO):

        def climb(step, state):
            at, count = state
            return parents_ref[m, at], count + (at > 0).astype(jnp.int32)

        _, count = lax.fori_loop(0, SEGS, climb, (parents_ref[m, seg], jnp.int32(0)))
        out_ref[m] = count


def ancestor_depths(parents, seg):
    smem = pl.BlockSpec(memory_space=pltpu.SMEM)
    return pl.pallas_call(
        depth_kernel,
        out_shape=jax.ShapeDtypeStruct((MICRO,), jnp.int32),
        in_specs=[smem, smem],
        out_specs=smem,
    )(parents, seg)


def list_ancestors(meta, qb, listed):
    def climb(step, state):
        at, count = state
        listed[count] = at + 3
        return meta[at], count + (at > 0).astype(jnp.int32)

    _, count = lax.fori_loop(0, SEGS, climb, (meta[qb - 3], jnp.int32(0)))
    return count


def causal_mask():
    key = lax.broadcasted_iota(jnp.int32, (BLK, BLK), 0)
    query = lax.broadcasted_iota(jnp.int32, (BLK, BLK), 1)
    return key <= query


def join_halves(meta, near_ref, far_ref, pack):
    core = meta[SEGS] % 2
    pack[:, pl.ds(pl.multiple_of(core * HALF, HALF), HALF), :] = near_ref[...]
    pack[:, pl.ds(pl.multiple_of((1 - core) * HALF, HALF), HALF), :] = far_ref[...]


def attend_kernel(meta, q0, q1, q2, q3, near_ref, far_ref, o0, o1, o2, o3, lse_ref, *scratch):
    q_ref, o_ref, pack, listed = scratch
    quarter, own = meta[SEGS], meta[SEGS + 1]
    join_halves(meta, near_ref, far_ref, pack)
    for j, ref in enumerate((q0, q1, q2, q3)):
        q_ref[own ^ j] = ref[...]
    for i in range(QUART):
        qb = QUART * i + quarter
        q = q_ref[i]
        s = matmul_nt(pack[qb, :, VDIM:], q) * SCALE
        s = jnp.where(causal_mask(), s, NEG)
        top = jnp.max(s, axis=0, keepdims=True)
        p = jnp.exp(s - top)
        total = jnp.sum(p, axis=0, keepdims=True)
        out = matmul_tn(pack[qb, :, :VDIM], p.astype(BF16))

        def visit(block, state):
            top, total, out = state
            s = matmul_nt(block[:, VDIM:], q) * SCALE
            new_top = jnp.maximum(top, jnp.max(s, axis=0, keepdims=True))
            shrink = jnp.exp(top - new_top)
            p = jnp.exp(s - new_top)
            total = total * shrink + jnp.sum(p, axis=0, keepdims=True)
            out = out * shrink + matmul_tn(block[:, :VDIM], p.astype(BF16))
            return new_top, total, out

        def step(kb, state):
            return visit(pack[kb], state)

        state = (top, total, out)
        if i == 0:
            state = lax.fori_loop(0, quarter, step, state)
        else:
            state = visit(pack[: TRUNK // BLK].reshape(TRUNK, PACK), state)
            count = list_ancestors(meta, qb, listed)
            state = lax.fori_loop(0, count, lambda t, c: step(listed[t], c), state)
        top, total, out = state
        o_ref[i] = (out * (1.0 / total)).T.astype(BF16)
        lse_ref[i] = top + jnp.log(total)
    for j, ref in enumerate((o0, o1, o2, o3)):
        ref[...] = o_ref[own ^ j]


def attend(meta, q, near, far):
    smem = pl.BlockSpec(memory_space=pltpu.SMEM)
    vmem = pl.BlockSpec(memory_space=pltpu.VMEM)
    pairs = 32 * BLK * BLK
    return pl.pallas_call(
        attend_kernel,
        out_shape=[jax.ShapeDtypeStruct((BLK, VDIM), BF16)] * QUART
        + [jax.ShapeDtypeStruct((QUART, 1, BLK), F32)],
        in_specs=[smem] + [vmem] * 6,
        out_specs=[vmem] * 5,
        scratch_shapes=[
            pltpu.VMEM((QUART, BLK, QKP), BF16),
            pltpu.VMEM((QUART, BLK, VDIM), BF16),
            pltpu.VMEM((ROWS, BLK, PACK), BF16),
            pltpu.SMEM((16,), jnp.int32),
        ],
        compiler_params=pltpu.CompilerParams(vmem_limit_bytes=60 * MIB),
        cost_estimate=pl.CostEstimate(
            flops=pairs * 2 * (QK + VDIM), bytes_accessed=4 * MIB, transcendentals=pairs
        ),
    )(meta, *q, near, far)


def attend_back_kernel(meta, *refs):
    ins, outs, scratch = refs[:15], refs[15:21], refs[21:]
    near_ref, far_ref, lse_ref = ins[12:]
    keep_ref, send_ref = outs[4:]
    q_ref, o_ref, do_ref, dq_ref, pack, dk, dv, listed = scratch
    quarter, own = meta[SEGS], meta[SEGS + 1]
    core = quarter % 2
    join_halves(meta, near_ref, far_ref, pack)
    for j in range(QUART):
        q_ref[own ^ j] = ins[j][...]
        o_ref[own ^ j] = ins[QUART + j][...]
        do_ref[own ^ j] = ins[2 * QUART + j][...]
    dk[...] = jnp.zeros_like(dk)
    dv[...] = jnp.zeros_like(dv)
    for i in range(QUART):
        qb = QUART * i + quarter
        q = q_ref[i]
        do = do_ref[i]
        lse = lse_ref[i]
        pairs = do.astype(F32) * o_ref[i].astype(F32)
        delta = jnp.sum(pairs.T, axis=0, keepdims=True)

        def trunk(dqt):
            block = pack[: TRUNK // BLK].reshape(TRUNK, PACK)
            key = block[:, VDIM:]
            p = jnp.exp(matmul_nt(key, q) * SCALE - lse)
            dp = matmul_nt(block[:, :VDIM], do)
            ds = (p * (dp - delta) * SCALE).astype(BF16)
            shape = (TRUNK // BLK, BLK, -1)
            dv[: TRUNK // BLK] += matmul(p.astype(BF16), do).reshape(shape)
            dk[: TRUNK // BLK] += matmul(ds, q).reshape(shape)
            return dqt + matmul_tn(key, ds)

        def step(kb, dqt, masked=False):
            key = pack[kb, :, VDIM:]
            s = matmul_nt(key, q) * SCALE
            p = jnp.exp(s - lse)
            if masked:
                p = jnp.where(causal_mask(), p, 0.0)
            dp = matmul_nt(pack[kb, :, :VDIM], do)
            ds = (p * (dp - delta) * SCALE).astype(BF16)
            dv[kb] += matmul(p.astype(BF16), do)
            dk[kb] += matmul(ds, q)
            return dqt + matmul_tn(key, ds)

        dqt = step(qb, jnp.zeros((QKP, BLK), F32), True)
        if i == 0:
            dqt = lax.fori_loop(0, quarter, step, dqt)
        else:
            dqt = trunk(dqt)
            count = list_ancestors(meta, qb, listed)
            dqt = lax.fori_loop(0, count, lambda t, c: step(listed[t], c), dqt)
        dq_ref[i] = dqt.T.astype(BF16)
    for j in range(QUART):
        outs[j][...] = dq_ref[own ^ j]
    for half, ref in ((core, keep_ref), (1 - core, send_ref)):
        part = pl.ds(pl.multiple_of(half * HALF, HALF), HALF)
        ref[:, :, :VDIM] = dv[:, part, :].astype(BF16)
        ref[:, :, VDIM:] = dk[:, part, :].astype(BF16)


def attend_back(meta, q, o, d_o, near, far, lse):
    smem = pl.BlockSpec(memory_space=pltpu.SMEM)
    vmem = pl.BlockSpec(memory_space=pltpu.VMEM)
    pairs = 32 * BLK * BLK
    return pl.pallas_call(
        attend_back_kernel,
        out_shape=[jax.ShapeDtypeStruct((BLK, QKP), BF16)] * QUART
        + [jax.ShapeDtypeStruct((ROWS, HALF, PACK), BF16)] * 2,
        in_specs=[smem] + [vmem] * 15,
        out_specs=[vmem] * 6,
        scratch_shapes=[
            pltpu.VMEM((QUART, BLK, QKP), BF16),
            pltpu.VMEM((QUART, BLK, VDIM), BF16),
            pltpu.VMEM((QUART, BLK, VDIM), BF16),
            pltpu.VMEM((QUART, BLK, QKP), BF16),
            pltpu.VMEM((ROWS, BLK, PACK), BF16),
            pltpu.VMEM((ROWS, BLK, QKP), F32),
            pltpu.VMEM((ROWS, BLK, VDIM), F32),
            pltpu.SMEM((16,), jnp.int32),
        ],
        compiler_params=pltpu.CompilerParams(vmem_limit_bytes=60 * MIB),
        cost_estimate=pl.CostEstimate(
            flops=pairs * 2 * (3 * QK + 2 * VDIM), bytes_accessed=10 * MIB, transcendentals=pairs
        ),
    )(meta, *q, *o, *d_o, near, far, lse)


def project_kernel(own_ref, b0, b1, b2, b3, w_ref, attended_ref, out_ref, blocks):
    for j, ref in enumerate((b0, b1, b2, b3)):
        blocks[own_ref[0] ^ j] = ref[...]
    for h in range(2):
        for m in range(MICRO):
            attended_ref[m * BLK : (m + 1) * BLK, h * VDIM : (h + 1) * VDIM] = blocks[2 * h + m]
    out = matmul_nt(attended_ref[...], w_ref[...]).astype(BF16)
    for c in range(COLS):
        out_ref[c] = out[c * OWN : (c + 1) * OWN]


def project(own, blocks, w_packed):
    def whole(*shape):
        return pl.BlockSpec(shape, lambda i: (0,) * len(shape))

    return pl.pallas_call(
        project_kernel,
        grid=(1,),
        out_shape=(
            jax.ShapeDtypeStruct((TOK, 2 * VDIM), BF16),
            jax.ShapeDtypeStruct((COLS, OWN, D), BF16),
        ),
        in_specs=[pl.BlockSpec(memory_space=pltpu.SMEM)]
        + [whole(BLK, VDIM)] * QUART
        + [pl.BlockSpec((D, 2 * VDIM), lambda i: (0, 2))],
        out_specs=(whole(TOK, 2 * VDIM), whole(COLS, OWN, D)),
        scratch_shapes=[pltpu.VMEM((QUART, BLK, VDIM), BF16)],
        compiler_params=pltpu.CompilerParams(vmem_limit_bytes=60 * MIB),
        cost_estimate=pl.CostEstimate(flops=TOK * D * 512, bytes_accessed=MIB, transcendentals=0),
    )(smem_values(own), *blocks, w_packed)


def project_back_kernel(own_ref, d_ref, w_ref, o0, o1, o2, o3, blocks):
    for c in range(COLS):
        rows = slice((c % QUART) * OWN, (c % QUART + 1) * OWN)
        part = matmul(d_ref[c], w_ref[...]).astype(BF16)
        for h in range(2):
            blocks[2 * h + c // QUART, rows, :] = part[:, h * VDIM : (h + 1) * VDIM]
    for j, ref in enumerate((o0, o1, o2, o3)):
        ref[...] = blocks[own_ref[0] ^ j]


def project_back(own, d_low, w_packed):
    def whole(*shape):
        return pl.BlockSpec(shape, lambda i: (0,) * len(shape))

    return pl.pallas_call(
        project_back_kernel,
        grid=(1,),
        out_shape=[jax.ShapeDtypeStruct((BLK, VDIM), BF16)] * QUART,
        in_specs=[
            pl.BlockSpec(memory_space=pltpu.SMEM),
            whole(COLS, OWN, D),
            pl.BlockSpec((D, 2 * VDIM), lambda i: (0, 2)),
        ],
        out_specs=[whole(BLK, VDIM)] * QUART,
        scratch_shapes=[pltpu.VMEM((QUART, BLK, VDIM), BF16)],
        compiler_params=pltpu.CompilerParams(vmem_limit_bytes=60 * MIB),
        cost_estimate=pl.CostEstimate(flops=TOK * D * 512, bytes_accessed=MIB, transcendentals=0),
    )(smem_values(own), d_low, w_packed)


def front_kernel(col_ref, pieces_ref, gain_ref, wl_ref, x_ref, normed_ref, scale_ref, lat_ref):
    for y in range(4):
        for z in range(2):
            at = (2 * y + (z ^ (col_ref[0] & 1))) * FEAT
            x_ref[:, pl.ds(pl.multiple_of(at, FEAT), FEAT)] = pieces_ref[y, z]
    x = x_ref[...].astype(F32)
    scale = inverse_rms(x)
    scale_ref[...] = scale
    normed = (x * scale * gain_ref[...]).astype(BF16)
    normed_ref[...] = normed
    latent = matmul(normed, wl_ref[...]).T[:LATC].astype(BF16)
    for c in range(COLS):
        lat_ref[c] = latent


def front(col, pieces, gain, w_packed):
    rows = 128
    return pl.pallas_call(
        front_kernel,
        grid=(TOK // rows,),
        out_shape=(
            jax.ShapeDtypeStruct((TOK, D), BF16),
            jax.ShapeDtypeStruct((TOK, D), BF16),
            jax.ShapeDtypeStruct((TOK, 1), F32),
            jax.ShapeDtypeStruct((COLS, LATC, TOK), BF16),
        ),
        in_specs=[
            pl.BlockSpec(memory_space=pltpu.SMEM),
            pl.BlockSpec((4, 2, rows, FEAT), lambda j: (0, 0, j, 0)),
            pl.BlockSpec((1, D), lambda j: (0, 0)),
            pl.BlockSpec((D, 128), lambda j: (0, 6)),
        ],
        out_specs=(
            pl.BlockSpec((rows, D), lambda j: (j, 0)),
            pl.BlockSpec((rows, D), lambda j: (j, 0)),
            pl.BlockSpec((rows, 1), lambda j: (j, 0)),
            pl.BlockSpec((COLS, LATC, rows), lambda j: (0, 0, j)),
        ),
        compiler_params=pltpu.CompilerParams(vmem_limit_bytes=60 * MIB),
        cost_estimate=pl.CostEstimate(flops=TOK * D * 256, bytes_accessed=MIB, transcendentals=0),
    )(smem_values(col), pieces, gain.reshape(1, D), w_packed)


def half_turn():
    source = lax.broadcasted_iota(jnp.int32, (2 * ROPE, 2 * ROPE), 0)
    target = lax.broadcasted_iota(jnp.int32, (2 * ROPE, 2 * ROPE), 1)
    half = ROPE // 2
    first = target % ROPE < half
    value = jnp.where(
        first & (source == target + half),
        -1.0,
        jnp.where((target % ROPE >= half) & (source == target - half), 1.0, 0.0),
    )
    return value.astype(BF16)


def query_kernel(own_ref, normed_ref, w_ref, cos_ref, sin_ref, o0, o1, o2, o3, blocks):
    normed = normed_ref[...]
    w_rope = w_ref[:, 2 * NOPE :]
    turned = matmul(w_rope, half_turn()).astype(BF16)
    rope = matmul(normed, w_rope) * cos_ref[...] + matmul(normed, turned) * sin_ref[...]
    rope = rope.astype(BF16)
    nope = matmul(normed, w_ref[:, : 2 * NOPE]).astype(BF16)
    blank = jnp.zeros((BLK, QKP - QK), BF16)
    for h in range(2):
        for m in range(MICRO):
            rows = slice(m * BLK, (m + 1) * BLK)
            blocks[2 * h + m, :, :NOPE] = nope[rows, h * NOPE : (h + 1) * NOPE]
            blocks[2 * h + m, :, NOPE:QK] = rope[rows, h * ROPE : (h + 1) * ROPE]
            blocks[2 * h + m, :, QK:] = blank
    for j, ref in enumerate((o0, o1, o2, o3)):
        ref[...] = blocks[own_ref[0] ^ j]


def project_query(own, normed, w_packed, cos_wide, sin_wide):
    def whole(shape):
        return pl.BlockSpec(shape, lambda i: (0, 0))

    return pl.pallas_call(
        query_kernel,
        grid=(1,),
        out_shape=[jax.ShapeDtypeStruct((BLK, QKP), BF16)] * QUART,
        in_specs=[
            pl.BlockSpec(memory_space=pltpu.SMEM),
            whole((TOK, D)),
            whole((D, 2 * QK)),
            whole((TOK, 2 * ROPE)),
            whole((TOK, 2 * ROPE)),
        ],
        out_specs=[whole((BLK, QKP))] * QUART,
        scratch_shapes=[pltpu.VMEM((QUART, BLK, QKP), BF16)],
        compiler_params=pltpu.CompilerParams(vmem_limit_bytes=60 * MIB),
        cost_estimate=pl.CostEstimate(flops=TOK * D * 256, bytes_accessed=MIB, transcendentals=0),
    )(smem_values(own), normed, w_packed, cos_wide, sin_wide)


def query_back_kernel(own_ref, b0, b1, b2, b3, cos_ref, sin_ref, out_ref, blocks):
    turn = half_turn()
    for j, ref in enumerate((b0, b1, b2, b3)):
        blocks[own_ref[0] ^ j] = ref[...]
    for m in range(MICRO):
        rows = slice(m * BLK, (m + 1) * BLK)
        for h in range(2):
            out_ref[rows, h * NOPE : (h + 1) * NOPE] = blocks[2 * h + m, :, :NOPE]
        rope = jnp.concatenate([blocks[m, :, NOPE:QK], blocks[2 + m, :, NOPE:QK]], axis=1)
        rope = rope.astype(F32) * cos_ref[rows, :] + matmul_nt(rope, turn) * sin_ref[rows, :]
        out_ref[rows, 2 * NOPE :] = rope.astype(BF16)


def query_back(own, blocks, cos_wide, sin_wide):
    vmem = pl.BlockSpec(memory_space=pltpu.VMEM)
    return pl.pallas_call(
        query_back_kernel,
        out_shape=jax.ShapeDtypeStruct((TOK, 2 * QK), BF16),
        in_specs=[pl.BlockSpec(memory_space=pltpu.SMEM)] + [vmem] * 6,
        out_specs=vmem,
        scratch_shapes=[pltpu.VMEM((QUART, BLK, QKP), BF16)],
        compiler_params=pltpu.CompilerParams(vmem_limit_bytes=60 * MIB),
        cost_estimate=pl.CostEstimate(flops=TOK * D * 16, bytes_accessed=MIB, transcendentals=0),
    )(smem_values(own), *blocks, cos_wide, sin_wide)


def expand_kernel(latent_ref, cos_ref, sin_ref, gain_ref, w_ref, normed_ref, out_ref):
    c = latent_ref[:KVL, :].astype(F32)
    scale = lax.rsqrt(jnp.mean(c * c, axis=0, keepdims=True) + EPS)
    normed = (c * scale * gain_ref[...]).astype(BF16)
    normed_ref[...] = normed
    expanded = matmul_tn(normed, w_ref[...]).astype(BF16)
    half = ROPE // 2
    a = latent_ref[KVL : KVL + half, :].astype(F32)
    b = latent_ref[KVL + half :, :].astype(F32)
    cos, sin = cos_ref[...], sin_ref[...]
    rope = jnp.concatenate(
        [a * cos - b * sin, a * sin + b * cos, jnp.zeros((QKP - QK, TOK), F32)], axis=0
    )
    rope = rope.T.astype(BF16)
    for h in range(2):
        key = h * (NOPE + VDIM)
        value = key + NOPE
        for m in range(MICRO):
            for core in range(2):
                rows = slice(m * BLK + core * HALF, m * BLK + (core + 1) * HALF)
                for chip in range(2):
                    at = 8 * h + 4 * m + 2 * chip + core
                    out_ref[at, :, :VDIM] = expanded[rows, value : value + VDIM]
                    out_ref[at, :, VDIM : VDIM + NOPE] = expanded[rows, key : key + NOPE]
                    out_ref[at, :, VDIM + NOPE :] = rope[rows, :]


def expand(latent_t, cos_t, sin_t, gain, w_expand):
    return pl.pallas_call(
        expand_kernel,
        out_shape=(
            jax.ShapeDtypeStruct((KVL, TOK), BF16),
            jax.ShapeDtypeStruct((ROWS, HALF, PACK), BF16),
        ),
        compiler_params=pltpu.CompilerParams(vmem_limit_bytes=24 * MIB),
        cost_estimate=pl.CostEstimate(flops=TOK * D * 256, bytes_accessed=MIB, transcendentals=0),
    )(latent_t, cos_t, sin_t, gain.reshape(KVL, 1), w_expand)


def latent_back_kernel(
    pack_ref, latent_ref, cos_ref, sin_ref, gain_ref, w_ref, d_exp_ref, d_latent_ref, gg_ref
):
    rope = [None] * (2 * MICRO)
    for h in range(2):
        for m in range(MICRO):
            for core in range(2):
                at = 8 * h + 4 * m + core
                part = pack_ref[at].astype(F32) + pack_ref[at + 2].astype(F32)
                rows = slice(m * BLK + core * HALF, m * BLK + (core + 1) * HALF)
                key = h * (NOPE + VDIM)
                d_exp_ref[rows, key : key + NOPE] = part[:, VDIM : VDIM + NOPE].astype(BF16)
                d_exp_ref[rows, key + NOPE : key + NOPE + VDIM] = part[:, :VDIM].astype(BF16)
                piece = part[:, VDIM + NOPE :]
                at = 2 * m + core
                rope[at] = piece if h == 0 else rope[at] + piece
    rope = jnp.concatenate(rope, axis=0).T
    half = ROPE // 2
    a, b = rope[:half], rope[half:ROPE]
    cos, sin = cos_ref[...], sin_ref[...]
    d_latent_ref[KVL : KVL + half, :] = (a * cos + b * sin).astype(BF16)
    d_latent_ref[KVL + half :, :] = (b * cos - a * sin).astype(BF16)
    d_normed = matmul_nt(w_ref[...], d_exp_ref[...])
    c = latent_ref[:KVL, :].astype(F32)
    scale = lax.rsqrt(jnp.mean(c * c, axis=0, keepdims=True) + EPS)
    gg_ref[...] = jnp.sum(d_normed * c * scale, axis=1, keepdims=True)
    weighted = d_normed * gain_ref[...]
    inner = jnp.mean(weighted * c, axis=0, keepdims=True)
    d_latent_ref[:KVL, :] = (scale * weighted - c * (scale * scale * scale) * inner).astype(BF16)


def latent_back(pack, latent_t, cos_t, sin_t, gain, w_expand):
    return pl.pallas_call(
        latent_back_kernel,
        out_shape=(
            jax.ShapeDtypeStruct((TOK, 2 * (NOPE + VDIM)), BF16),
            jax.ShapeDtypeStruct((LAT, TOK), BF16),
            jax.ShapeDtypeStruct((KVL, 1), F32),
        ),
        compiler_params=pltpu.CompilerParams(vmem_limit_bytes=60 * MIB),
        cost_estimate=pl.CostEstimate(flops=TOK * D * 256, bytes_accessed=MIB, transcendentals=0),
    )(pack, latent_t, cos_t, sin_t, gain.reshape(KVL, 1), w_expand)


def hidden_kernel(
    own_ref, mid_ref, grad_ref, gate_ref, spread_ref, wg_ref, wu_ref, wd_ref, out_ref, turned_ref
):
    mid = mid_ref[...]
    pre = matmul(mid, wg_ref[...])
    up = matmul(mid, wu_ref[...])
    back = matmul(grad_ref[...], wd_ref[...])
    gate = matmul(gate_ref[...], spread_ref[...])
    sig = 0.5 + 0.5 * jnp.tanh(0.5 * pre)
    act = pre * sig
    back = back * gate
    out_ref[0] = (back * up * (sig * (1.0 + pre * (1.0 - sig)))).astype(BF16)
    out_ref[1] = (back * act).astype(BF16)
    out_ref[2] = (act * up * gate).astype(BF16)
    for i in range(3):
        r = jnp.minimum(3 * pl.program_id(0) + i, ROWS - 1)
        turned_ref[lanes(place_of(own_ref[0] ^ r)), :] = mid_ref[:, lanes(r)].T


def hidden(row, mid, grad, gates, spread, weights):
    whole = pl.BlockSpec((TOK, D), lambda j: (0, 0))
    parts = HID // BLK

    def weight(at):
        return pl.BlockSpec((D, BLK), lambda j: (0, at * parts + j))

    return pl.pallas_call(
        hidden_kernel,
        grid=(parts,),
        out_shape=(
            jax.ShapeDtypeStruct((3, TOK, HID), BF16),
            jax.ShapeDtypeStruct((D, TOK), BF16),
        ),
        in_specs=[
            pl.BlockSpec(memory_space=pltpu.SMEM),
            whole,
            whole,
            pl.BlockSpec(gates.shape, lambda j: (0, 0)),
            pl.BlockSpec((spread.shape[0], BLK), lambda j: (0, j)),
            weight(0),
            weight(1),
            weight(2),
        ],
        out_specs=(
            pl.BlockSpec((3, TOK, BLK), lambda j: (0, 0, j)),
            pl.BlockSpec((D, TOK), lambda j: (0, 0)),
        ),
        compiler_params=pltpu.CompilerParams(vmem_limit_bytes=60 * MIB),
        cost_estimate=pl.CostEstimate(
            flops=2 * TOK * D * HID * 3, bytes_accessed=32 * MIB, transcendentals=TOK * HID
        ),
    )(smem_values(row), mid, grad, gates, spread, weights, weights, weights)


def mid_grad_kernel(hid_ref, w_ref, out_ref):
    out = matmul_nt(hid_ref[0], w_ref[:, :HID]) + matmul_nt(hid_ref[1], w_ref[:, HID:])
    out_ref[...] = out.astype(BF16)


def mid_grad(hid, weights):
    return pl.pallas_call(
        mid_grad_kernel,
        grid=(4,),
        out_shape=jax.ShapeDtypeStruct((TOK, D), BF16),
        in_specs=[
            pl.BlockSpec((2, TOK, HID), lambda j: (0, 0, 0)),
            pl.BlockSpec((D // 4, 2 * HID), lambda j: (j, 0)),
        ],
        out_specs=pl.BlockSpec((TOK, D // 4), lambda j: (0, j)),
        compiler_params=pltpu.CompilerParams(vmem_limit_bytes=60 * MIB),
        cost_estimate=pl.CostEstimate(
            flops=2 * TOK * D * HID * 2, bytes_accessed=20 * MIB, transcendentals=0
        ),
    )(hid, weights)


def output_kernel(col_ref, hid_ref, w_ref, residual_ref, out_ref):
    out_ref[0] = matmul_nt(hid_ref[0], w_ref[...]).astype(BF16)
    own = pl.ds(pl.multiple_of(col_ref[0] * OWN, OWN), OWN)
    out_ref[0, own, :] = (
        matmul_nt(hid_ref[0, own, :], w_ref[...]) + residual_ref[...]
    ).astype(BF16)


def output(col, hid, weights, residual):
    return pl.pallas_call(
        output_kernel,
        grid=(COLS,),
        out_shape=jax.ShapeDtypeStruct((COLS, TOK, FEAT), BF16),
        in_specs=[
            pl.BlockSpec(memory_space=pltpu.SMEM),
            pl.BlockSpec((1, TOK, HID), lambda j: (2, 0, 0)),
            pl.BlockSpec((FEAT, HID), lambda j: (j, 2)),
            pl.BlockSpec((OWN, FEAT), lambda j: (0, j)),
        ],
        out_specs=pl.BlockSpec((1, TOK, FEAT), lambda j: (j, 0, 0)),
        compiler_params=pltpu.CompilerParams(vmem_limit_bytes=60 * MIB),
        cost_estimate=pl.CostEstimate(
            flops=TOK * D * HID // 8, bytes_accessed=MIB, transcendentals=0
        ),
    )(col.astype(jnp.int32).reshape(1), hid, weights, residual)


def mid_kernel(parts_ref, inputs_ref, gain_ref, residual_ref, scale_ref, normed_ref):
    total = inputs_ref[...].astype(F32)
    for c in range(COLS):
        total = total + parts_ref[c].astype(F32)
    scale = inverse_rms(total)
    residual_ref[...] = total
    scale_ref[...] = scale
    normed = (total * scale * gain_ref[...]).astype(BF16)
    for c in range(COLS):
        normed_ref[c] = normed


def mid(parts, inputs, gain):
    return pl.pallas_call(
        mid_kernel,
        out_shape=(
            jax.ShapeDtypeStruct((OWN, D), F32),
            jax.ShapeDtypeStruct((OWN, 1), F32),
            jax.ShapeDtypeStruct((COLS, OWN, D), BF16),
        ),
        compiler_params=pltpu.CompilerParams(vmem_limit_bytes=20 * MIB),
        cost_estimate=pl.CostEstimate(
            flops=OWN * D * 16, bytes_accessed=5 * MIB, transcendentals=0
        ),
    )(parts, inputs, gain.reshape(1, D))


def mid_back_kernel(
    parts_ref, residual_ref, scale_ref, grad_ref, gain_ref, out_ref, low_ref, gain_grad_ref
):
    d_mid = parts_ref[0].astype(F32)
    for c in range(1, COLS):
        d_mid = d_mid + parts_ref[c].astype(F32)
    residual, scale = residual_ref[...], scale_ref[...]
    gain_grad_ref[...] = jnp.sum(d_mid * residual * scale, axis=0, keepdims=True)
    out = grad_ref[...].astype(F32) + norm_backward(d_mid, residual, scale, gain_ref[...])
    out_ref[...] = out
    low = out.astype(BF16)
    for c in range(COLS):
        low_ref[c] = low


def mid_back(parts, residual, scale, grad, gain):
    return pl.pallas_call(
        mid_back_kernel,
        out_shape=(
            jax.ShapeDtypeStruct((OWN, D), F32),
            jax.ShapeDtypeStruct((COLS, OWN, D), BF16),
            jax.ShapeDtypeStruct((1, D), F32),
        ),
        compiler_params=pltpu.CompilerParams(vmem_limit_bytes=20 * MIB),
        cost_estimate=pl.CostEstimate(
            flops=OWN * D * 24, bytes_accessed=5 * MIB, transcendentals=0
        ),
    )(parts, residual, scale, grad, gain.reshape(1, D))


def input_back_kernel(
    col_ref, dq_ref, dl_ref, wq_ref, wl_ref, x_ref, scale_ref, gain_ref, own_ref, out_ref, gg_ref
):
    step = pl.program_id(0)
    d_in = matmul_nt(dq_ref[...], wq_ref[...]) + matmul_nt(dl_ref[...], wl_ref[...])
    x, scale = x_ref[...].astype(F32), scale_ref[...]
    gain_grad = jnp.sum(d_in * x * scale, axis=0, keepdims=True)

    @pl.when(step == 0)
    def _():
        gg_ref[...] = gain_grad

    @pl.when(step > 0)
    def _():
        gg_ref[...] += gain_grad

    out = norm_backward(d_in, x, scale, gain_ref[...])
    for half in range(2):
        mine = (col_ref[0] == 2 * step + half).astype(F32)
        rows = slice(half * OWN, (half + 1) * OWN)
        part = (out[rows] + mine * own_ref[...]).astype(BF16)
        for c in range(COLS):
            out_ref[c, rows, :] = part[:, c * FEAT : (c + 1) * FEAT]


def input_back(col, d_query, d_latent, w_packed, inputs, scale, gain, own):
    rows = 2 * OWN
    widths = (d_query.shape[1], d_latent.shape[1])
    return pl.pallas_call(
        input_back_kernel,
        grid=(TOK // rows,),
        out_shape=(
            jax.ShapeDtypeStruct((COLS, TOK, FEAT), BF16),
            jax.ShapeDtypeStruct((1, D), F32),
        ),
        in_specs=[
            pl.BlockSpec(memory_space=pltpu.SMEM),
            pl.BlockSpec((rows, widths[0]), lambda j: (j, 0)),
            pl.BlockSpec((rows, widths[1]), lambda j: (j, 0)),
            pl.BlockSpec((D, widths[0]), lambda j: (0, 0)),
            pl.BlockSpec((D, widths[1]), lambda j: (0, 6)),
            pl.BlockSpec((rows, D), lambda j: (j, 0)),
            pl.BlockSpec((rows, 1), lambda j: (j, 0)),
            pl.BlockSpec((1, D), lambda j: (0, 0)),
            pl.BlockSpec((OWN, D), lambda j: (0, 0)),
        ],
        out_specs=(
            pl.BlockSpec((COLS, rows, FEAT), lambda j: (0, j, 0)),
            pl.BlockSpec((1, D), lambda j: (0, 0)),
        ),
        compiler_params=pltpu.CompilerParams(vmem_limit_bytes=60 * MIB),
        cost_estimate=pl.CostEstimate(
            flops=2 * TOK * D * 640, bytes_accessed=9 * MIB, transcendentals=0
        ),
    )(
        smem_values(col),
        d_query,
        d_latent,
        w_packed,
        w_packed,
        inputs,
        scale,
        gain.reshape(1, D),
        own,
    )


def send_grad_kernel(mid_ref, grad_ref, hid_ref, out_ref):
    @pl.when(pl.program_id(0) < 2)
    def _():
        out_ref[...] = matmul(mid_ref[...], hid_ref[0]).astype(BF16)

    @pl.when(pl.program_id(0) == 2)
    def _():
        out_ref[...] = matmul(grad_ref[...], hid_ref[0]).astype(BF16)


def keep_grad_kernel(mid_ref, grad_ref, hid_ref, got_ref, *out_refs):
    def store(lhs_ref):
        out = matmul(lhs_ref[...], hid_ref[0]) + got_ref[...].astype(F32)
        first = 0
        for ref in out_refs:
            rows = ref.shape[0]
            ref[...] = out[first : first + rows].astype(BF16)
            first += rows

    @pl.when(pl.program_id(0) < 2)
    def _():
        store(mid_ref)

    @pl.when(pl.program_id(0) == 2)
    def _():
        store(grad_ref)


def send_grads(z, mid_t, grad_t, hid):
    rows = D // 4
    whole = pl.BlockSpec((rows, TOK), lambda s: (2 + z, 0))
    return pl.pallas_call(
        send_grad_kernel,
        grid=(3,),
        out_shape=jax.ShapeDtypeStruct((rows, WIDE), BF16),
        in_specs=[whole, whole, pl.BlockSpec((1, TOK, HID), lambda s: (s, 0, 0))],
        out_specs=pl.BlockSpec((rows, HID), lambda s: (0, s)),
        compiler_params=pltpu.CompilerParams(vmem_limit_bytes=60 * MIB),
        cost_estimate=pl.CostEstimate(
            flops=TOK * D * HID // 32, bytes_accessed=MIB, transcendentals=0
        ),
    )(mid_t, grad_t, hid)


def keep_grads(z, mid_t, grad_t, hid, got):
    rows = D // 4
    whole = pl.BlockSpec((rows, TOK), lambda s: (z, 0))
    heights = (LANES, LANES, CUT, CUT, LANES)
    return pl.pallas_call(
        keep_grad_kernel,
        grid=(3,),
        out_shape=[jax.ShapeDtypeStruct((height, WIDE), BF16) for height in heights],
        in_specs=[
            whole,
            whole,
            pl.BlockSpec((1, TOK, HID), lambda s: (s, 0, 0)),
            pl.BlockSpec((rows, HID), lambda s: (0, s)),
        ],
        out_specs=[pl.BlockSpec((h, HID), lambda s: (0, s)) for h in heights],
        compiler_params=pltpu.CompilerParams(vmem_limit_bytes=60 * MIB),
        cost_estimate=pl.CostEstimate(
            flops=TOK * D * HID // 32, bytes_accessed=MIB, transcendentals=0
        ),
    )(mid_t, grad_t, hid, got)


def rotary_tables(parents, row):
    seg = jnp.maximum(row - (TRUNK // BLK - 1), 0).astype(jnp.int32)
    depths = ancestor_depths(parents, seg.reshape(1))
    starts = jnp.where(seg > 0, TRUNK + BLK * depths, BLK * row)
    positions = (starts[:, None] + jnp.arange(BLK, dtype=jnp.int32)[None, :]).reshape(TOK)
    frequency = THETA ** (-jnp.arange(ROPE // 2, dtype=F32) / (ROPE // 2))
    angles = positions.astype(F32)[:, None] * frequency[None, :]
    cos_table, sin_table = jnp.cos(angles), jnp.sin(angles)
    cos_wide, sin_wide = jnp.tile(cos_table, (1, 4)), jnp.tile(sin_table, (1, 4))
    return cos_table.T, sin_table.T, cos_wide, sin_wide


def pack_hidden(shared, routed):
    rows = shared.shape[0]
    return jnp.concatenate(
        [
            shared,
            jnp.swapaxes(routed, 0, 1).reshape(rows, EXPERTS * ROUTED),
            jnp.zeros((rows, HID - SHARED - EXPERTS * ROUTED), routed.dtype),
        ],
        axis=1,
    )


def local(
    tokens,
    out_grad,
    parents,
    routes,
    gates,
    norm_in,
    w_query,
    w_latent,
    norm_latent,
    w_expand,
    w_output,
    norm_mid,
    w_shared_gate,
    w_shared_up,
    w_shared_down,
    w_expert_gate,
    w_expert_up,
    w_expert_down,
):
    row = lax.axis_index("row")
    col = lax.axis_index("col")
    group = row // QUART
    own_start = col * OWN
    gain_in = norm_in.astype(F32)
    gain_latent = norm_latent.astype(F32)
    gain_mid = norm_mid.astype(F32)
    heads = 2

    query_pack = w_query.reshape(D // ROWS, heads, QK)
    attn_pack = jnp.concatenate(
        [
            query_pack[:, :, :NOPE].reshape(D // ROWS, heads * NOPE),
            query_pack[:, :, NOPE:].reshape(D // ROWS, heads * ROPE),
            w_expand.reshape(KVL // ROWS, 4, 128).transpose(1, 0, 2).reshape(D // ROWS, 128),
            w_output.T,
            w_latent,
            jnp.zeros((D // ROWS, 128 - LATC), BF16),
        ],
        axis=1,
    )
    ffn_pack = jnp.concatenate(
        [
            pack_hidden(w_shared_gate, w_expert_gate),
            pack_hidden(w_shared_up, w_expert_up),
            pack_hidden(w_shared_down.T, jnp.swapaxes(w_expert_down, 1, 2)),
        ],
        axis=1,
    )
    attn_pair, input_pair, ffn_pack = together(
        pair_up(attn_pack, "row"), pair_up(tokens.reshape(TOK, FEAT), "col"), ffn_pack
    )
    line_groups = [[2 * y + z for y in range(4)] for z in range(2)]
    input_copies = jnp.broadcast_to(input_pair[None], (4,) + input_pair.shape)
    attn_ring, input_ring, ffn_pack, ffn_other, tables = together(
        ring_up(attn_pair, "row"),
        swap(input_copies, "col", line_groups),
        ffn_pack,
        trade(ffn_pack, "row", 8),
        rotary_tables(parents, row),
    )
    cos_t, sin_t, cos_wide, sin_wide = tables
    ffn_near = near_shards(ffn_pack)
    attn_full = finish_rows(attn_ring, row)
    expand_full = attn_full[:, 384:512].reshape(ROWS, 4, KVL // ROWS, 128)
    expand_full = expand_full.transpose(0, 2, 1, 3).reshape(KVL, heads * (NOPE + VDIM))

    inputs, normed_in, scale_in, latent_parts = front(col, input_ring, gain_in, attn_full)
    query = project_query(group, normed_in, attn_full, cos_wide, sin_wide)
    latent_t, query, normed_in, ffn_near, grad_copies = together(
        swap(latent_parts, "col"),
        query,
        normed_in,
        ffn_near,
        jnp.broadcast_to(out_grad.reshape(1, TOK, FEAT), (COLS, TOK, FEAT)),
    )
    latent_t = latent_t.reshape(LAT, TOK)
    latent_normed_t, pack = expand(latent_t, cos_t, sin_t, gain_latent, expand_full)
    pack, query, ffn_near, ffn_other = together(pack, query, ffn_near, ffn_other)
    near, query, ffn_cut, grad_copies = together(
        swap(pack, "row"), trade_quarter(query), cut_near(ffn_near), grad_copies
    )
    grad_ring = swap(grad_copies, "col")
    ffn_far = far_halves(ffn_cut)
    far = trade(near, "row", 1)

    meta = jnp.concatenate([pick(parents, group % MICRO), smem_values(row % QUART, group)])
    *attended_own, lse = attend(meta, query, near, far)
    attended_own, lse, ffn_far = together(attended_own, lse, ffn_far)
    attended_parts, grad_ring, ffn_far, ffn_other = together(
        trade_quarter(attended_own), grad_ring, ffn_far, ffn_other
    )
    attended, attn_parts = project(group, attended_parts, attn_full)
    grad_full, grad_t = features(row, grad_ring)

    def both_cores(pieces):
        far_pieces = [(trade(v, "row", 1), apart ^ 1, first) for v, apart, first in pieces]
        return list(pieces) + far_pieces

    pieces = both_cores(
        [(ffn_pack, 0, 0), (ffn_near[0], 2, 0), (ffn_near[1], 6, 0)]
        + [(ffn_far[0], 4, 0), (ffn_far[1], 4, CUT)]
    )
    own_inputs = lax.dynamic_slice_in_dim(inputs, own_start, OWN, 0)
    ffn_full = put_shards(row, None, pieces)
    attn_parts, grad_full, grad_t, ffn_full = together(
        swap(attn_parts, "col"), grad_full, grad_t, ffn_full
    )
    named = routes.reshape(TOK, TOPK, 1) == jnp.arange(EXPERTS, dtype=jnp.int32)
    gate_of = jnp.sum(jnp.where(named, gates.reshape(TOK, TOPK, 1), 0.0), axis=1)
    gate_of = jnp.concatenate(
        [jnp.ones((TOK, 1), F32), gate_of, jnp.zeros((TOK, 15 - EXPERTS), F32)], axis=1
    )
    gate_high = gate_of.astype(BF16)
    gate_low = (gate_of - gate_high.astype(F32)).astype(BF16)
    gate_parts = jnp.concatenate([gate_high, gate_low], axis=1)
    unit = jnp.arange(HID, dtype=jnp.int32)
    expert = jnp.where(unit < SHARED, 0, 1 + (unit - SHARED) // ROUTED)
    spread = (expert[None, :] == jnp.arange(16, dtype=jnp.int32)[:, None]).astype(BF16)
    spread = jnp.concatenate([spread, spread], axis=0)
    attn_parts, gate_parts, spread = together(attn_parts, gate_parts, spread)
    residual, scale_mid, normed_mid = mid(attn_parts, own_inputs, gain_mid)
    normed_mid, other_near = together(normed_mid, near_shards(ffn_other))
    pieces = both_cores([(ffn_other, 8, 0), (other_near[0], 10, 0), (other_near[1], 14, 0)])
    ffn_full = put_shards(row, ffn_full, pieces)
    normed_mid, ffn_full, other_far = together(
        swap(normed_mid, "col"), ffn_full, far_halves(cut_near(other_near))
    )
    normed_mid = normed_mid.reshape(TOK, D)
    pieces = both_cores([(other_far[0], 12, 0), (other_far[1], 12, CUT)])
    ffn_full = put_shards(row, ffn_full, pieces)

    hid, normed_t = hidden(row, normed_mid, grad_full, gate_parts, spread, ffn_full)
    mid_parts = mid_grad(hid, ffn_full)
    hid, normed_t, mid_parts = together(hid, normed_t, mid_parts)
    send = send_grads(1, normed_t, grad_t, hid)
    blocks = keep_grads(1, normed_t, grad_t, hid, trade(send, "row", 1))
    send = send_grads(0, normed_t, grad_t, after(hid, blocks))
    halves = sum_opposite(blocks)
    mid_parts, hid, blocks, send, normed_t = together(
        swap(mid_parts.reshape(COLS, OWN, D), "col"), hid, blocks, send, normed_t
    )
    own_grad = lax.dynamic_slice_in_dim(grad_full, own_start, OWN, 0)
    d_residual, d_low, mid_gain = mid_back(mid_parts, residual, scale_mid, own_grad, gain_mid)
    d_low, hid, send, halves, blocks = together(d_low, hid, send, halves, blocks)
    block, sides = blocks[0], with_opposite(blocks, halves)
    d_low, out_parts, sides, own_blocks = together(
        swap(d_low, "col"),
        output(col, hid, ffn_full, residual),
        sum_neighbours(sides),
        keep_grads(0, normed_t, grad_t, hid, trade(send, "row", 1)),
    )
    other_sum = add_low(block.astype(F32) + sides[0].astype(F32), sides[1])

    d_attended = trade_quarter(project_back(group, d_low, attn_full))
    d_attended, other_sum, out_parts = together(d_attended, other_sum, out_parts)
    *d_query, d_near, d_far = attend_back(
        meta, query, attended_own, d_attended, near, far, lse
    )
    d_query, d_near, d_far, halves, other_low, out_parts, out_left = together(
        d_query,
        d_near,
        d_far,
        sum_opposite(own_blocks),
        trade(other_sum[:CUT], "row", 8),
        out_parts,
        collect_y(out_parts, col // 2, 1),
    )
    d_far = trade(d_far, "row", 1)
    d_query, d_pack = together(trade_quarter(d_query), add_low(d_near, d_far))
    d_query = query_back(group, d_query, cos_wide, sin_wide)
    d_pack, sides, out_right, out_parts, d_query, attn_grads = together(
        swap(d_pack, "row"),
        with_opposite(own_blocks, halves),
        collect_y(out_parts, col // 2, 3),
        out_parts,
        d_query,
        attn_weight_grads(row, normed_in, d_query, d_low.reshape(TOK, D), attended),
    )
    sides = sum_neighbours(sides)

    d_expanded, d_latent, latent_gain = latent_back(
        d_pack, latent_t, cos_t, sin_t, gain_latent, expand_full
    )
    other_high = trade(after(other_sum, d_latent)[CUT:], "row", 8)
    d_latent, attn_grads, out_far, out_own = together(
        swap(d_latent.reshape(COLS, LATC, TOK), "col"),
        add_low(attn_grads[0], trade(attn_grads[1], "row", 1)),
        collect_y(out_parts, col // 2, 2),
        collect_y(out_parts, col // 2, 0),
    )
    out_parts = (out_own, out_left, out_far, out_right)
    d_latent = jnp.sum(d_latent.astype(F32), axis=0).astype(BF16)
    d_latent = jnp.concatenate([d_latent, jnp.zeros((128 - LATC, TOK), BF16)], axis=0).T

    d_tokens, in_gain = input_back(
        col, d_query, d_latent, attn_full, inputs, scale_in, gain_in, d_residual
    )
    d_tokens, in_gain, sides, other_high = together(d_tokens, in_gain, sides, other_high)

    gain = jnp.concatenate([in_gain.reshape(D), latent_gain.reshape(KVL), mid_gain.reshape(D)])
    d_tokens, d_latent = together(d_tokens, d_latent)
    latent_grads = latent_weight_grads(row, normed_in, d_latent, latent_normed_t, d_expanded)
    latent_grads = add_low(latent_grads[0], trade(latent_grads[1], "row", 1))
    ffn_grads = own_blocks[0].astype(F32) + sides[0].astype(F32) + sides[1].astype(F32)
    other_sum = jnp.concatenate([other_low, other_high], axis=0)
    ffn_grads = ffn_grads + other_sum.astype(F32)

    def unpack(at):
        part = ffn_grads[:, at * HID : (at + 1) * HID]
        routed = part[:, SHARED : SHARED + EXPERTS * ROUTED]
        return part[:, :SHARED], routed.reshape(-1, EXPERTS, ROUTED)

    grad_shared_gate, grad_expert_gate = unpack(0)
    grad_shared_up, grad_expert_up = unpack(1)
    grad_shared_down, grad_expert_down = unpack(2)
    ffn_outs = (
        grad_shared_gate,
        grad_shared_up,
        grad_shared_down.T,
        jnp.swapaxes(grad_expert_gate, 0, 1),
        jnp.swapaxes(grad_expert_up, 0, 1),
        grad_expert_down.transpose(1, 2, 0),
    )
    d_tokens, attn_grads, latent_grads, out_parts, gain, ffn_outs = together(
        swap(d_tokens, "col"),
        [reduce_x(attn_grads, j) for j in range(4)],
        latent_grads,
        out_parts,
        gain,
        ffn_outs,
    )
    latent_grads = [reduce_x(latent_grads, j) for j in range(4)]
    attn_grads = reduce_z(attn_grads, latent_grads)
    layer_out = collect_z(out_parts, col % 2).astype(BF16)
    input_grad = jnp.sum(d_tokens.astype(F32), axis=0).astype(BF16)
    gain = share(gain.astype(BF16).reshape(-1, 128), ("row", "col"), ROWS * COLS)
    gain, input_grad, attn_grads, layer_out = together(gain, input_grad, attn_grads, layer_out)
    gain = jnp.sum(gain.astype(F32), axis=0).reshape(-1)
    grad_query = jnp.concatenate(
        [
            attn_grads[:, : heads * NOPE].reshape(-1, heads, NOPE),
            attn_grads[:, heads * NOPE : heads * QK].reshape(-1, heads, ROPE),
        ],
        axis=-1,
    ).reshape(-1, heads * QK)
    grad_output = attn_grads[:, 384:640].T
    grad_expand = attn_grads[:, 640:768].reshape(4, KVL // ROWS, 128)
    grad_expand = grad_expand.transpose(1, 0, 2).reshape(KVL // ROWS, heads * (NOPE + VDIM))
    grad_latent = attn_grads[:, 768 : 768 + LATC]

    return (
        layer_out.reshape(MICRO, BLK, FEAT),
        input_grad.reshape(MICRO, BLK, FEAT),
        gain[:D],
        grad_query,
        grad_latent,
        gain[D : D + KVL],
        grad_expand,
        grad_output,
        gain[D + KVL :],
        *ffn_outs,
    )


def solution(mesh):
    in_specs = (
        P(None, "row", "col"),
        P(None, "row", "col"),
        P(),
        P(None, "row", None),
        P(None, "row", None),
        P(),
        P("row", "col"),
        P("row", "col"),
        P(),
        P("row", "col"),
        P("col", "row"),
        P(),
        P("row", "col"),
        P("row", "col"),
        P("col", "row"),
        P(None, "row", "col"),
        P(None, "row", "col"),
        P(None, "col", "row"),
    )
    out_specs = (
        P(None, "row", "col"),
        P(None, "row", "col"),
        P(),
        P("row", "col"),
        P("row", "col"),
        P(),
        P("row", "col"),
        P("col", "row"),
        P(),
        P("row", "col"),
        P("row", "col"),
        P("col", "row"),
        P(None, "row", "col"),
        P(None, "row", "col"),
        P(None, "col", "row"),
    )
    return jax.shard_map(local, mesh=mesh, in_specs=in_specs, out_specs=out_specs, check_vma=False)
```
